128 devices in a mesh: wide: 16 (over z, y), narrow: 8 (over x, core).
Axes of the slice: x: 4, y: 4, z: 4, core: 2. Of those that a mesh axis runs over, the one named last changes fastest.
Arguments:
- grid_feat: bfloat16 [1048576, 227], P(('wide', 'narrow')), may hold values from -6 to 6
- grid_send: int32 [128, 128], P(('wide', 'narrow')), may hold values from 0 to 127, each once within a row
- w_embed: bfloat16 [227, 512], replicated, may hold values from -0.375 to 0.375
- g2m_src: int32 [2048, 8], P(('wide', 'narrow')), may hold values from 0 to 127
- g2m_coef: bfloat16 [2048, 8, 64, 64], P(('wide', 'narrow')), may hold values from -0.25 to 0.25
- mesh_src: int32 [2048, 6], P(('wide', 'narrow')), may hold values from 0 to 31
- mesh_coef: bfloat16 [2048, 6, 64, 64], P(('wide', 'narrow')), may hold values from -0.3125 to 0.3125
- halo_send: int32 [128, 4], P(('wide', 'narrow')), may hold values from 0 to 15
- message_weight: bfloat16 [2, 512, 512], replicated, may hold values from -0.25 to 0.25
- update_weight: bfloat16 [2, 512, 512], replicated, may hold values from -0.25 to 0.25
- cotangent: bfloat16 [131072, 512], P(('wide', 'narrow')), may hold values from -6 to 6
Outputs:
- mesh_out: bfloat16 [131072, 512], P(('wide', 'narrow'))
- d_embed: float32 [227, 512], replicated
- message_weight_gradient: float32 [2, 512, 512], replicated
- update_weight_gradient: float32 [2, 512, 512], replicated
The draws below stay inside these ranges and needn't reach their ends.
Inputs may be any that keep to these rules, and one draw needn't show every extreme that they name: `grid_send`: each row names every local grid block once. `g2m_src`: an index into the device's received grid blocks. `mesh_src`: an index into the device's own blocks followed by its four halo groups. `halo_send`: a local mesh block of the device.
All inputs are finite; a program needn't handle non-finite values.
Results may differ from the reference program's by a relative error of at most 0.017.
Values may be sent and summed in bfloat16 or wider, within the bound.
No kernel may reach another device: no remote copies, remote signals or barrier semaphores. Data moves between devices by JAX's collectives and lax.ppermute only.
A program may use at most 192 MiB of HBM per device.

```python
import jax
import jax.numpy as jnp
from jax import lax

CHAN = 227
LATENT_WIDTH = 512
BLOCK = 64
GB_DEV = 128
MB_DEV = 16
KG = 8
KM = 6
HB = 4
PROCESSOR_LAYERS = 2
NGRID = 1048576
NMB = 2048
NMESH = 131072
N_WIDE = 16
N_NARROW = 8
DEVICES = 128


def place_ends(entries, stream_key, low, largest):
    place = [jax.random.randint(jax.random.fold_in(stream_key, axis), (), 0, length) for axis, length in enumerate(entries.shape)]
    widest = entries.shape.index(max(entries.shape))
    neighbour = place[:widest] + [(place[widest] + 1) % entries.shape[widest]] + place[widest + 1:]
    return entries.at[tuple(place)].set(low).at[tuple(neighbour)].set(largest)


def block_scale(stream_key, extent, shards, smallest, high):
    def one(axis_at, shards_of):
        heights = jax.random.uniform(jax.random.fold_in(jax.random.fold_in(stream_key, 6), axis_at), (shards_of,), jnp.float32, smallest / len(shards), high / len(shards))
        return jnp.repeat(jnp.exp(heights), extent[axis_at] // shards_of).reshape((-1,) + (1,) * (len(extent) - axis_at - 1))

    loudness = one(*shards[0])
    for cut in shards[1:]:
        loudness = loudness * one(*cut)
    return loudness


def noise(rng, shape, spread, limit, split=(), held_as=jnp.bfloat16):
    factor_of = block_scale(rng, shape, split, -0.22, 0.18) if split else 1.0
    drawn = jax.random.normal(rng, shape, jnp.float32) * spread * factor_of
    return jnp.minimum(jnp.maximum(drawn, -limit), limit).astype(held_as)


def setup_inputs(seed: int = 0) -> dict:
    seeds = jax.random.split(jax.random.key(seed), 12)
    grid_feat = noise(seeds[0], (NGRID, CHAN), 1.0, 6.0, ((0, 128),))
    grid_send = jax.vmap(lambda own: jax.random.permutation(own, GB_DEV))(jax.random.split(seeds[1], DEVICES)).reshape((DEVICES, GB_DEV)).astype(jnp.int32)
    w_embed = noise(seeds[2], (CHAN, LATENT_WIDTH), CHAN ** -0.5, 0.375)
    g2m_src = place_ends(jax.random.randint(seeds[3], (NMB, KG), 0, GB_DEV), jax.random.fold_in(seeds[3], 1), 0, GB_DEV - 1).astype(jnp.int32)
    g2m_coef = noise(seeds[4], (NMB, KG, BLOCK, BLOCK), (KG * BLOCK) ** -0.5, 0.25, ((0, 128),))
    mesh_src = place_ends(jax.random.randint(seeds[5], (NMB, KM), 0, MB_DEV + 4 * HB), jax.random.fold_in(seeds[5], 1), 0, (MB_DEV + 4 * HB) - 1).astype(jnp.int32)
    mesh_coef = noise(seeds[6], (NMB, KM, BLOCK, BLOCK), (KM * BLOCK) ** -0.5, 0.3125, ((0, 128),))
    halo_send = place_ends(jax.random.randint(seeds[7], (DEVICES, HB), 0, MB_DEV), jax.random.fold_in(seeds[7], 1), 0, MB_DEV - 1).astype(jnp.int32)
    message_weight = noise(seeds[8], (PROCESSOR_LAYERS, LATENT_WIDTH, LATENT_WIDTH), LATENT_WIDTH ** -0.5, 0.25)
    update_weight = noise(seeds[9], (PROCESSOR_LAYERS, LATENT_WIDTH, LATENT_WIDTH), LATENT_WIDTH ** -0.5, 0.25)
    cotangent = noise(seeds[10], (NMESH, LATENT_WIDTH), 1.0, 6.0, ((0, 128),))
    return {"grid_feat": grid_feat, "grid_send": grid_send, "w_embed": w_embed, "g2m_src": g2m_src, "g2m_coef": g2m_coef, "mesh_src": mesh_src, "mesh_coef": mesh_coef, "halo_send": halo_send, "message_weight": message_weight, "update_weight": update_weight, "cotangent": cotangent}


def silu_grad(values):
    sigmoid_v = jax.nn.sigmoid(values)
    return sigmoid_v * (1.0 + values * (1.0 - sigmoid_v))

def transposed(left, right):
    return lax.dot_general(left, right, (((0,), (0,)), ((), ())), preferred_element_type=jnp.float32)

def mix_blocks(coeffs, source, indices):
    accum_sum = jnp.zeros((coeffs.shape[0], source.shape[1], source.shape[2]), jnp.float32)
    for slot in range(coeffs.shape[1]):
        picked = source[indices[:, slot]]
        accum_sum = accum_sum + jnp.einsum('bij,bjl->bil', coeffs[:, slot], picked, preferred_element_type=jnp.float32)
    return accum_sum

def mix_back(coeffs, gradient, indices, block_count):
    lowered = gradient.astype(jnp.bfloat16)
    portions = jnp.einsum('bkji,bjl->bkil', coeffs, lowered, preferred_element_type=jnp.float32)
    flat_parts = portions.reshape(-1, gradient.shape[1], gradient.shape[2])
    return jax.ops.segment_sum(flat_parts, indices.reshape(-1), num_segments=block_count)

def reference(grid_feat, grid_send, w_embed, g2m_src, g2m_coef, mesh_src, mesh_coef, halo_send, message_weight, update_weight, cotangent):
    n_devices = N_WIDE * N_NARROW
    per_peer = GB_DEV // n_devices
    all_blocks = MB_DEV + 4 * HB
    features = grid_feat.reshape(n_devices, GB_DEV, BLOCK, CHAN)
    slots_of = grid_send.reshape(n_devices, n_devices, per_peer)
    gcoeffs = g2m_coef.reshape(n_devices, MB_DEV, KG, BLOCK, BLOCK)
    gindices = g2m_src.reshape(n_devices, MB_DEV, KG)
    mcoeffs = mesh_coef.reshape(n_devices, MB_DEV, KM, BLOCK, BLOCK)
    mindices = mesh_src.reshape(n_devices, MB_DEV, KM)
    senders = jnp.arange(n_devices, dtype=jnp.int32)

    def arrived(device):
        picked = slots_of[:, device, :]
        return features[senders[:, None], picked].reshape(GB_DEV * BLOCK, CHAN)

    def neighbours(device):
        wide_pos = device // N_NARROW
        narrow_pos = device % N_NARROW
        return jnp.stack([(wide_pos - 1) % N_WIDE * N_NARROW + narrow_pos, (wide_pos + 1) % N_WIDE * N_NARROW + narrow_pos, wide_pos * N_NARROW + (narrow_pos - 1) % N_NARROW, wide_pos * N_NARROW + (narrow_pos + 1) % N_NARROW]).astype(jnp.int32)

    def encode(device):
        in_rows = arrived(device)
        pre_enc = jnp.dot(in_rows, w_embed, preferred_element_type=jnp.float32)
        received = jax.nn.silu(pre_enc).astype(jnp.bfloat16)
        source = received.reshape(GB_DEV, BLOCK, LATENT_WIDTH)
        return mix_blocks(gcoeffs[device], source, gindices[device]).astype(jnp.bfloat16)

    def messages(mesh_state, layer_number):
        pre_act = jnp.dot(mesh_state.reshape(-1, LATENT_WIDTH), message_weight[layer_number], preferred_element_type=jnp.float32)
        sent = jax.nn.silu(pre_act).astype(jnp.bfloat16)
        return sent.reshape(n_devices, MB_DEV, BLOCK, LATENT_WIDTH)

    def aggregate_of(sent, device):
        beside_all = neighbours(device)
        portions = [sent[device]] + [sent[beside_all[slot]][halo_send[beside_all[slot]]] for slot in range(4)]
        extended = jnp.concatenate(portions, 0)
        return mix_blocks(mcoeffs[device], extended, mindices[device]).astype(jnp.bfloat16)
    states = [lax.map(encode, senders)]
    for layer_number in range(PROCESSOR_LAYERS):
        mesh_state = states[-1]
        sent = messages(mesh_state, layer_number)

        def advance(device):
            aggregate = aggregate_of(sent, device).reshape(-1, LATENT_WIDTH)
            update = jnp.dot(aggregate, update_weight[layer_number], preferred_element_type=jnp.float32)
            fresh = mesh_state[device].reshape(-1, LATENT_WIDTH).astype(jnp.float32) + update
            return fresh.astype(jnp.bfloat16).reshape(MB_DEV, BLOCK, LATENT_WIDTH)
        states.append(lax.map(advance, senders))
    gradient = cotangent.reshape(n_devices, MB_DEV, BLOCK, LATENT_WIDTH).astype(jnp.float32)
    message_weight_gradient = [None] * PROCESSOR_LAYERS
    update_weight_gradient = [None] * PROCESSOR_LAYERS
    block_ids = jnp.arange(MB_DEV, dtype=jnp.int32)
    for layer_number in reversed(range(PROCESSOR_LAYERS)):
        mesh_state = states[layer_number]
        sent = messages(mesh_state, layer_number)

        def first(running, device):
            aggregate = aggregate_of(sent, device).reshape(-1, LATENT_WIDTH)
            grad_low = gradient[device].reshape(-1, LATENT_WIDTH).astype(jnp.bfloat16)
            running = running + transposed(aggregate, grad_low)
            grad_agg = jnp.dot(grad_low, update_weight[layer_number].T, preferred_element_type=jnp.float32)
            grad_ext = mix_back(mcoeffs[device], grad_agg.reshape(MB_DEV, BLOCK, LATENT_WIDTH), mindices[device], all_blocks)
            return (running, (grad_ext[:MB_DEV], grad_ext[MB_DEV:].reshape(4, HB, BLOCK, LATENT_WIDTH)))
        d_up, (grad_own, grad_halo) = lax.scan(first, jnp.zeros((LATENT_WIDTH, LATENT_WIDTH), jnp.float32), senders)

        def second(running, device):
            beside_all = neighbours(device)
            returned = grad_halo[beside_all[1], 0] + grad_halo[beside_all[0], 1] + (grad_halo[beside_all[3], 2] + grad_halo[beside_all[2], 3])
            one_hot = (halo_send[device][:, None] == block_ids[None, :]).astype(jnp.float32)
            grad_msg = grad_own[device] + jnp.einsum('hm,hil->mil', one_hot, returned, precision=lax.Precision.HIGHEST)
            own_rows = mesh_state[device].reshape(-1, LATENT_WIDTH)
            pre_act = jnp.dot(own_rows, message_weight[layer_number], preferred_element_type=jnp.float32)
            grad_pre = (grad_msg.reshape(-1, LATENT_WIDTH) * silu_grad(pre_act)).astype(jnp.bfloat16)
            running = running + transposed(own_rows, grad_pre)
            carried = jnp.dot(grad_pre, message_weight[layer_number].T, preferred_element_type=jnp.float32)
            return (running, gradient[device] + carried.reshape(MB_DEV, BLOCK, LATENT_WIDTH))
        d_ms, gradient = lax.scan(second, jnp.zeros((LATENT_WIDTH, LATENT_WIDTH), jnp.float32), senders)
        message_weight_gradient[layer_number] = d_ms
        update_weight_gradient[layer_number] = d_up

    def encode_back(running, device):
        in_rows = arrived(device)
        pre_enc = jnp.dot(in_rows, w_embed, preferred_element_type=jnp.float32)
        grad_table = lax.optimization_barrier(mix_back(gcoeffs[device], gradient[device], gindices[device], GB_DEV).astype(jnp.bfloat16))
        grad_grid = (grad_table.reshape(-1, LATENT_WIDTH).astype(jnp.float32) * silu_grad(pre_enc)).astype(jnp.bfloat16)
        return (running + transposed(in_rows, grad_grid), None)
    d_embed, unused = lax.scan(encode_back, jnp.zeros((CHAN, LATENT_WIDTH), jnp.float32), senders)
    mesh_out = states[-1].reshape(-1, LATENT_WIDTH)
    return (mesh_out, d_embed, jnp.stack(message_weight_gradient), jnp.stack(update_weight_gradient))
```

```python
import functools

import jax
import jax.numpy as jnp
from jax import lax
from jax.experimental import pallas as pl
from jax.experimental.pallas import tpu as pltpu
from jax.sharding import PartitionSpec as P

CHAN = 227
WIDTH = 512
BLOCK = 64
GRID_BLOCKS = 128
MESH_BLOCKS = 16
SHOWN = 4
G_SLOTS = 8
M_SLOTS = 6
EXTENDED = MESH_BLOCKS + 4 * SHOWN
MESH_ROWS = MESH_BLOCKS * BLOCK
GRID_ROWS = GRID_BLOCKS * BLOCK
SPLIT = 112
PACKED = CHAN - SPLIT
TAIL = 256
AXES = ("wide", "narrow")
BF16 = jnp.bfloat16
F32 = jnp.float32
MIB = 1 << 20

VM = pl.BlockSpec(memory_space=pltpu.VMEM)
SM = pl.BlockSpec(memory_space=pltpu.SMEM)
HBM = pl.BlockSpec(memory_space=pl.ANY)


def kernel_call(body, outs, ins, scratch=(), flops=0, moved=0, limit=56):
    return pl.pallas_call(
        body,
        out_shape=[jax.ShapeDtypeStruct(shape, dtype) for shape, dtype in outs],
        in_specs=ins,
        out_specs=[VM] * len(outs),
        scratch_shapes=list(scratch),
        compiler_params=pltpu.CompilerParams(vmem_limit_bytes=limit * MIB),
        cost_estimate=pl.CostEstimate(flops=flops, bytes_accessed=moved, transcendentals=0),
    )


def times(left, right, left_dim=1, right_dim=0):
    return lax.dot_general(
        left, right, (((left_dim,), (right_dim,)), ((), ())), preferred_element_type=F32
    )


def sigmoid(values):
    return 0.5 * jnp.tanh(0.5 * values) + 0.5


def silu_grad(values):
    s = sigmoid(values)
    return s * (1.0 + values * (1.0 - s))


def swap_halves(tile):
    return jnp.concatenate([tile[:, BLOCK:], tile[:, :BLOCK]], axis=1)


def low_lanes(rows):
    return lax.broadcasted_iota(jnp.int32, (rows, 2 * BLOCK), 1) < BLOCK


def rows_of(block):
    return pl.ds(pl.multiple_of(block * BLOCK, BLOCK), BLOCK)


def chunk(step, size):
    return pl.ds(pl.multiple_of(step * size, size), size)


def pack_body(send, features, out, target):
    def invert(j, carry):
        target[send[0, j]] = j
        return carry

    lax.fori_loop(0, GRID_BLOCKS, invert, 0)
    low = low_lanes(PACKED)

    def pair(i, carry):
        lanes = chunk(i, 2 * BLOCK)
        first = features[0:PACKED, lanes]
        second = features[SPLIT:CHAN, lanes]
        out[target[2 * i]] = jnp.where(low, first, swap_halves(second))
        out[target[2 * i + 1]] = jnp.where(low, swap_halves(first), second)
        return carry

    lax.fori_loop(0, GRID_BLOCKS // 2, pair, 0, unroll=2)


def scatter_back(coeffs_t, gradient, source, table, slots, zero_blocks):
    def clear(i, carry):
        table[i] = jnp.zeros((BLOCK, WIDTH), F32)
        return carry

    lax.fori_loop(0, zero_blocks, clear, 0)

    def one(b, carry):
        parts = times(coeffs_t[b], gradient[rows_of(b), :])
        for k in range(slots):
            at = source[b, k]
            table[at] = table[at] + parts[k * BLOCK : (k + 1) * BLOCK]
        return carry

    lax.fori_loop(0, MESH_BLOCKS, one, 0)


def gather_mix(coeffs, pick, slots, b):
    picked = jnp.concatenate([pick(b, k) for k in range(slots)], axis=0)
    return times(coeffs[b], picked)


def add_returned(own, returned, shown, take):
    for h in range(SHOWN):
        at = shown[0, h]
        extra = (returned[0][h].astype(F32) + returned[1][h].astype(F32)) + (
            returned[2][h].astype(F32) + returned[3][h].astype(F32)
        )
        take[rows_of(at), :] = take[rows_of(at), :] + extra


def write_halo(table, own, halos):
    for i in range(MESH_BLOCKS):
        own[i * BLOCK : (i + 1) * BLOCK, :] = table[i]
    for e in range(4):
        for h in range(SHOWN):
            halos[e][h] = table[MESH_BLOCKS + e * SHOWN + h].astype(BF16)


def early_back_body(source, cot, up, coeffs_t, own, h0, h1, h2, h3, table, lowered):
    def step(c, carry):
        rows = chunk(c, 256)
        lowered[rows, :] = times(cot[rows, :], up[...], 1, 1).astype(BF16)
        return carry

    lax.fori_loop(0, MESH_ROWS // 256, step, 0)
    scatter_back(coeffs_t, lowered, source, table, M_SLOTS, EXTENDED)
    write_halo(table, own, (h0, h1, h2, h3))


def encode_body(source, shown, packed, weight, coeffs, message, points, mesh, sent, mine, embedded):
    low = low_lanes(PACKED)

    def embed(c, carry):
        for p in range(4):
            a = packed[c * 8 + 2 * p]
            b = packed[c * 8 + 2 * p + 1]
            lanes = pl.ds(pl.multiple_of(c * 512 + p * 128, 128), 128)
            points[0:SPLIT, lanes] = jnp.where(low, a, swap_halves(b))[0:SPLIT]
            points[SPLIT:CHAN, lanes] = jnp.where(low, swap_halves(a), b)
        rows = chunk(c, 512)
        pre = times(points[:, rows], weight[...], 0, 0)
        embedded[rows, :] = (pre * sigmoid(pre)).astype(BF16)
        return carry

    lax.fori_loop(0, GRID_ROWS // 512, embed, 0)

    def mix(b, carry):
        pick = lambda b, k: embedded[rows_of(source[b, k]), :]
        mesh[rows_of(b), :] = gather_mix(coeffs, pick, G_SLOTS, b).astype(BF16)
        return carry

    lax.fori_loop(0, MESH_BLOCKS, mix, 0)

    def talk(c, carry):
        rows = chunk(c, 256)
        pre = times(mesh[rows, :], message[...])
        sent[rows, :] = (pre * sigmoid(pre)).astype(BF16)
        return carry

    lax.fori_loop(0, MESH_ROWS // 256, talk, 0)
    for h in range(SHOWN):
        mine[h] = sent[rows_of(shown[0, h]), :]


def slopes_body(points, weight, mesh, message, slope, slope_m):
    pre = times(points[...], weight[...], 0, 0)
    slope[...] = silu_grad(pre).astype(BF16)

    @pl.when(pl.program_id(0) < 4)
    def _():
        slope_m[...] = silu_grad(times(mesh[...], message[...]))


def extend(extended, sent, halos):
    extended[0:MESH_ROWS, :] = sent[...]
    for e in range(4):
        for h in range(SHOWN):
            at = MESH_ROWS + (e * SHOWN + h) * BLOCK
            extended[at : at + BLOCK, :] = halos[e][h]


def middle_body(
    source, shown, sent, n0, n1, n2, n3, coeffs, coeffs_t, mesh, up, message, own, r0, r1, r2, r3,
    cot, aggregate, mesh_1, sent_1, mine, grad_pre, grad_1, own_0, h0, h1, h2, h3,
    extended, table, lowered, grad_msg,
):
    extend(extended, sent, (n0, n1, n2, n3))
    grad_msg[...] = own[...]
    add_returned(own, (r0, r1, r2, r3), shown, grad_msg)

    def mix(b, carry):
        pick = lambda b, k: extended[rows_of(source[b, k]), :]
        aggregate[rows_of(b), :] = gather_mix(coeffs, pick, M_SLOTS, b).astype(BF16)
        return carry

    lax.fori_loop(0, MESH_BLOCKS, mix, 0)

    def step(c, carry):
        rows = chunk(c, 256)
        state = (mesh[rows, :].astype(F32) + times(aggregate[rows, :], up[...])).astype(BF16)
        mesh_1[rows, :] = state
        pre = times(state, message[...])
        s = sigmoid(pre)
        sent_1[rows, :] = (pre * s).astype(BF16)
        gp = (grad_msg[rows, :] * (s * (1.0 + pre * (1.0 - s)))).astype(BF16)
        grad_pre[rows, :] = gp
        g = cot[rows, :].astype(F32) + times(gp, message[...], 1, 1)
        grad_1[rows, :] = g
        lowered[rows, :] = times(g.astype(BF16), up[...], 1, 1).astype(BF16)
        return carry

    lax.fori_loop(0, MESH_ROWS // 256, step, 0)
    for h in range(SHOWN):
        mine[h] = sent_1[rows_of(shown[0, h]), :]
    scatter_back(coeffs_t, lowered, source, table, M_SLOTS, EXTENDED)
    write_halo(table, own_0, (h0, h1, h2, h3))


def two_grads_body(aggregate, grad_1, mesh_1, grad_pre, up_grad, ms_grad):
    up_grad[...] = times(aggregate[...], grad_1[...].astype(BF16), 0, 0).astype(BF16)
    ms_grad[...] = times(mesh_1[...], grad_pre[...], 0, 0).astype(BF16)


def last_body(
    source, sent, n0, n1, n2, n3, coeffs, mesh, up, cot, mesh_out, up_grad, extended, aggregate
):
    extend(extended, sent, (n0, n1, n2, n3))

    def mix(b, carry):
        pick = lambda b, k: extended[rows_of(source[b, k]), :]
        aggregate[rows_of(b), :] = gather_mix(coeffs, pick, M_SLOTS, b).astype(BF16)
        return carry

    lax.fori_loop(0, MESH_BLOCKS, mix, 0)

    def step(c, carry):
        rows = chunk(c, 256)
        update = times(aggregate[rows, :], up[...])
        mesh_out[rows, :] = (mesh[rows, :].astype(F32) + update).astype(BF16)
        return carry

    lax.fori_loop(0, MESH_ROWS // 256, step, 0)
    up_grad[...] = times(aggregate[...], cot[...], 0, 0).astype(BF16)


def final_body(
    source, shown, own, r0, r1, r2, r3, slope_m, grad_1, message, mesh, coeffs_t, slope_hbm,
    points_hbm, grads, slope, points, table, grad_pre, lowered, grad_msg, total, sems,
):
    load_slope = pltpu.make_async_copy(slope_hbm, slope, sems.at[0])
    load_points = pltpu.make_async_copy(points_hbm, points, sems.at[1])
    load_slope.start()
    load_points.start()
    grad_msg[...] = own[...]
    add_returned(own, (r0, r1, r2, r3), shown, grad_msg)

    def step(c, carry):
        rows = chunk(c, 256)
        gp = (grad_msg[rows, :] * slope_m[rows, :]).astype(BF16)
        grad_pre[rows, :] = gp
        lowered[rows, :] = (grad_1[rows, :] + times(gp, message[...], 1, 1)).astype(BF16)
        return carry

    lax.fori_loop(0, MESH_ROWS // 256, step, 0)
    scatter_back(coeffs_t, lowered, source, table, G_SLOTS, GRID_BLOCKS)
    grads[0:WIDTH, :] = times(mesh[...], grad_pre[...], 0, 0).astype(BF16)
    load_slope.wait()
    load_points.wait()
    total[...] = jnp.zeros_like(total)

    def grid_step(c, carry):
        rows = chunk(c, 512)
        grad = table[pl.ds(pl.multiple_of(c * 8, 8), 8)].reshape(512, WIDTH).astype(BF16)
        grad = (grad.astype(F32) * slope[rows, :].astype(F32)).astype(BF16)
        total[0:CHAN, :] = total[0:CHAN, :] + times(points[:, rows], grad)
        return carry

    lax.fori_loop(0, GRID_ROWS // 512, grid_step, 0)
    grads[WIDTH : WIDTH + TAIL, :] = total[...].astype(BF16)


def shift(value, axis, steps):
    count = lax.axis_size(axis)
    return lax.ppermute(value, axis, [(i, (i + steps) % count) for i in range(count)])


def show(mine):
    return (shift(mine, "wide", 1), shift(mine, "wide", -1), shift(mine, "narrow", 1), shift(mine, "narrow", -1))


def give_back(h0, h1, h2, h3):
    return (shift(h0, "wide", -1), shift(h1, "wide", 1), shift(h2, "narrow", -1), shift(h3, "narrow", 1))


def exchange(parts, axis):
    return lax.all_to_all(parts, axis, split_axis=0, concat_axis=0, tiled=True)


def add_up(parts):
    return jnp.sum(parts.astype(F32), axis=0).astype(BF16)


def scatter_sum(rows, axis):
    count = lax.axis_size(axis)
    return add_up(exchange(rows.reshape(count, rows.shape[0] // count, rows.shape[1]), axis))


def gather_all(rows, axis):
    count = lax.axis_size(axis)
    return exchange(jnp.broadcast_to(rows[None], (count,) + rows.shape), axis)


def sum_narrow_first(rows):
    part = scatter_sum(scatter_sum(rows, "narrow"), "wide")
    part = gather_all(part, "wide").reshape(-1, rows.shape[1])
    return gather_all(part, "narrow").reshape(rows.shape)


def sum_wide_first(rows):
    part = add_up(gather_all(scatter_sum(rows, "wide"), "narrow"))
    return gather_all(part, "wide").reshape(rows.shape)


def on_device(
    grid_feat, grid_send, w_embed, g2m_src, g2m_coef, mesh_src, mesh_coef, halo_send,
    message_weight, update_weight, cotangent,
):
    rows_bf16 = ((MESH_ROWS, WIDTH), BF16)
    rows_f32 = ((MESH_ROWS, WIDTH), F32)
    halo = ((SHOWN, BLOCK, WIDTH), BF16)
    square = ((WIDTH, WIDTH), BF16)
    points_shape = ((CHAN, GRID_ROWS), BF16)
    mesh_scratch = pltpu.VMEM((MESH_ROWS, WIDTH), BF16)
    mesh_scratch32 = pltpu.VMEM((MESH_ROWS, WIDTH), F32)
    extended_scratch = pltpu.VMEM((EXTENDED * BLOCK, WIDTH), BF16)
    table_scratch = pltpu.VMEM((EXTENDED, BLOCK, WIDTH), F32)
    w_m = (message_weight[0], message_weight[1])
    w_u = (update_weight[0], update_weight[1])

    packed = kernel_call(
        pack_body, [((GRID_BLOCKS, PACKED, 2 * BLOCK), BF16)], [SM, VM],
        [pltpu.SMEM((GRID_BLOCKS,), jnp.int32)], moved=8 * MIB,
    )(grid_send, grid_feat.T)[0]
    received = lax.all_to_all(packed, AXES, split_axis=0, concat_axis=0, tiled=True)

    g_mix = g2m_coef.transpose(0, 2, 1, 3).reshape(MESH_BLOCKS, BLOCK, G_SLOTS * BLOCK)
    g_back = g2m_coef.transpose(0, 1, 3, 2).reshape(MESH_BLOCKS, G_SLOTS * BLOCK, BLOCK)
    m_mix = mesh_coef.transpose(0, 2, 1, 3).reshape(MESH_BLOCKS, BLOCK, M_SLOTS * BLOCK)
    m_back = mesh_coef.transpose(0, 1, 3, 2).reshape(MESH_BLOCKS, M_SLOTS * BLOCK, BLOCK)

    own_1, *halos = kernel_call(
        early_back_body, [rows_f32] + [halo] * 4, [SM] + [VM] * 3, [table_scratch, mesh_scratch],
        flops=2 * 10**9, moved=8 * MIB,
    )(mesh_src, cotangent, w_u[1], m_back)
    returned_1 = give_back(*halos)

    received, g_mix, g_back, m_mix, m_back = lax.optimization_barrier(
        (received, g_mix, g_back, m_mix, m_back)
    )
    points, mesh_0, sent_0, mine_0 = kernel_call(
        encode_body, [points_shape, rows_bf16, rows_bf16, halo], [SM, SM] + [VM] * 4,
        [pltpu.VMEM((GRID_ROWS, WIDTH), BF16)], flops=4 * 10**9, moved=16 * MIB,
    )(g2m_src, halo_send, received, w_embed, g_mix, w_m[0])
    shown_0 = show(mine_0)

    slope, slope_m = pl.pallas_call(
        slopes_body,
        grid=(16,),
        out_shape=[
            jax.ShapeDtypeStruct((GRID_ROWS, WIDTH), BF16),
            jax.ShapeDtypeStruct((MESH_ROWS, WIDTH), F32),
        ],
        in_specs=[
            pl.BlockSpec((CHAN, 512), lambda i: (0, i)),
            pl.BlockSpec((CHAN, WIDTH), lambda i: (0, 0)),
            pl.BlockSpec((256, WIDTH), lambda i: (jnp.minimum(i, 3), 0)),
            pl.BlockSpec((WIDTH, WIDTH), lambda i: (0, 0)),
        ],
        out_specs=[
            pl.BlockSpec((512, WIDTH), lambda i: (i, 0)),
            pl.BlockSpec((256, WIDTH), lambda i: (jnp.minimum(i, 3), 0)),
        ],
        compiler_params=pltpu.CompilerParams(vmem_limit_bytes=56 * MIB),
        cost_estimate=pl.CostEstimate(flops=3 * 10**9, bytes_accessed=16 * MIB, transcendentals=0),
    )(points, w_embed, mesh_0, w_m[0])
    sent_0, slope, slope_m = lax.optimization_barrier((sent_0, slope, slope_m))

    aggregate_0, mesh_1, sent_1, mine_1, grad_pre_1, grad_1, own_0, *halos = kernel_call(
        middle_body,
        [rows_bf16, rows_bf16, rows_bf16, halo, rows_bf16, rows_f32, rows_f32] + [halo] * 4,
        [SM, SM] + [VM] * 16,
        [extended_scratch, table_scratch, mesh_scratch, mesh_scratch32],
        flops=5 * 10**9, moved=20 * MIB,
    )(
        mesh_src, halo_send, sent_0, *shown_0, m_mix, m_back, mesh_0, w_u[0], w_m[1], own_1,
        *returned_1, cotangent,
    )
    returned_0 = give_back(*halos)
    shown_1 = show(mine_1)

    up_0, ms_1 = kernel_call(
        two_grads_body, [square, square], [VM] * 4, flops=10**9, moved=5 * MIB
    )(aggregate_0, grad_1, mesh_1, grad_pre_1)

    mesh_out, up_1 = kernel_call(
        last_body, [rows_bf16, square], [SM] + [VM] * 9, [extended_scratch, mesh_scratch],
        flops=2 * 10**9, moved=8 * MIB,
    )(mesh_src, sent_1, *shown_1, m_mix, mesh_1, w_u[1], cotangent)
    own_0, up_0, ms_1, up_1 = lax.optimization_barrier((own_0, up_0, ms_1, up_1))
    early = jnp.concatenate([up_0, ms_1, up_1], axis=0)
    late = kernel_call(
        final_body, [((WIDTH + TAIL, WIDTH), BF16)], [SM, SM] + [VM] * 10 + [HBM, HBM],
        [
            pltpu.VMEM((GRID_ROWS, WIDTH), BF16),
            pltpu.VMEM((CHAN, GRID_ROWS), BF16),
            pltpu.VMEM((GRID_BLOCKS, BLOCK, WIDTH), F32),
            mesh_scratch, mesh_scratch, mesh_scratch32,
            pltpu.VMEM((TAIL, WIDTH), F32),
            pltpu.SemaphoreType.DMA((2,)),
        ],
        flops=4 * 10**9, moved=24 * MIB,
    )(
        g2m_src, halo_send, own_0, *returned_0, slope_m, grad_1, w_m[0], mesh_0, g_back, slope,
        points,
    )[0]
    early = sum_narrow_first(early).astype(F32)
    late = sum_wide_first(late).astype(F32)
    up_0, ms_1, up_1 = early[:WIDTH], early[WIDTH : 2 * WIDTH], early[2 * WIDTH :]
    ms_0, d_embed = late[:WIDTH], late[WIDTH : WIDTH + CHAN]
    return mesh_out, d_embed, jnp.stack([ms_0, ms_1]), jnp.stack([up_0, up_1])


def solution(mesh):
    split = P(AXES, None)
    return jax.shard_map(
        on_device,
        mesh=mesh,
        in_specs=(
            split, split, P(), split, P(AXES, None, None, None), split, P(AXES, None, None, None),
            split, P(), P(), split,
        ),
        out_specs=(split, P(), P(), P()),
        check_vma=False,
    )
```

```python
import jax
import jax.numpy as jnp
from jax import lax
from jax.experimental import pallas as pl
from jax.experimental.pallas import tpu as pltpu
from jax.sharding import PartitionSpec as P

CHAN = 227
WIDTH = 512
BLOCK = 64
GRID_BLOCKS = 128
MESH_BLOCKS = 16
SHOWN = 4
G_SLOTS = 8
M_SLOTS = 6
EXTENDED = MESH_BLOCKS + 4 * SHOWN
MESH_ROWS = MESH_BLOCKS * BLOCK
GRID_ROWS = GRID_BLOCKS * BLOCK
SPLIT = 112
PACKED = CHAN - SPLIT
TAIL = 256
DEVICES = 128
SLAB = 4 * WIDTH
EARLY = 3 * SLAB // DEVICES
LATE = (SLAB + 4 * TAIL) // DEVICES
AXES = ("wide", "narrow")
BF16 = jnp.bfloat16
F32 = jnp.float32
MIB = 1 << 20

VM = pl.BlockSpec(memory_space=pltpu.VMEM)
SM = pl.BlockSpec(memory_space=pltpu.SMEM)


def kernel_call(body, outs, ins, scratch=(), flops=0, moved=0, limit=56):
    return pl.pallas_call(
        body,
        out_shape=[jax.ShapeDtypeStruct(shape, dtype) for shape, dtype in outs],
        in_specs=ins,
        out_specs=[VM] * len(outs),
        scratch_shapes=list(scratch),
        compiler_params=pltpu.CompilerParams(vmem_limit_bytes=limit * MIB),
        cost_estimate=pl.CostEstimate(flops=flops, bytes_accessed=moved, transcendentals=0),
    )


def times(left, right, left_dim=1, right_dim=0):
    return lax.dot_general(
        left, right, (((left_dim,), (right_dim,)), ((), ())), preferred_element_type=F32
    )


def sigmoid(values):
    return 0.5 * jnp.tanh(0.5 * values) + 0.5


def silu_grad(values):
    s = sigmoid(values)
    return s * (1.0 + values * (1.0 - s))


def swap_halves(tile):
    return jnp.concatenate([tile[:, BLOCK:], tile[:, :BLOCK]], axis=1)


def low_lanes(rows):
    return lax.broadcasted_iota(jnp.int32, (rows, 2 * BLOCK), 1) < BLOCK


def rows_of(block):
    return pl.ds(pl.multiple_of(block * BLOCK, BLOCK), BLOCK)


def chunk(step, size):
    return pl.ds(pl.multiple_of(step * size, size), size)


def pack_body(send, features, out):
    low = low_lanes(PACKED)
    step = pl.program_id(0)

    def one(j, carry):
        block = send[0, step * 16 + j]
        lanes = chunk(block // 2, 2 * BLOCK)

        @pl.when(block % 2 == 0)
        def _():
            out[j] = jnp.where(low, features[0:PACKED, lanes], swap_halves(features[SPLIT:CHAN, lanes]))

        @pl.when(block % 2 == 1)
        def _():
            out[j] = jnp.where(low, swap_halves(features[0:PACKED, lanes]), features[SPLIT:CHAN, lanes])

        return carry

    lax.fori_loop(0, 16, one, 0, unroll=4)


def scatter_back(coeffs, gradient, source, table, slots, blocks):
    def clear(i, carry):
        table[i] = jnp.zeros((BLOCK, WIDTH), F32)
        return carry

    lax.fori_loop(0, blocks, clear, 0, unroll=4)

    def one(b, carry):
        parts = times(coeffs[b], gradient[rows_of(b), :], 0, 0)
        for k in range(slots):
            at = source[b, k]
            table[at] = table[at] + parts[k * BLOCK : (k + 1) * BLOCK]
        return carry

    lax.fori_loop(0, MESH_BLOCKS, one, 0)


def gather_mix(coeffs, pick, slots, b):
    picked = jnp.concatenate([pick(b, k) for k in range(slots)], axis=0)
    return times(coeffs[b], picked)


def add_returned(own, returned, shown, take):
    for h in range(SHOWN):
        at = shown[0, h]
        extra = (returned[0][h].astype(F32) + returned[1][h].astype(F32)) + (
            returned[2][h].astype(F32) + returned[3][h].astype(F32)
        )
        take[rows_of(at), :] = take[rows_of(at), :] + extra


def write_halo(table, own, halos):
    for i in range(MESH_BLOCKS):
        own[i * BLOCK : (i + 1) * BLOCK, :] = table[i].astype(own.dtype)
    for e in range(4):
        for h in range(SHOWN):
            halos[e][h] = table[MESH_BLOCKS + e * SHOWN + h].astype(BF16)


def early_back_body(source, cot, up, coeffs, own, h0, h1, h2, h3, table, lowered):
    def step(c, carry):
        rows = chunk(c, 256)
        lowered[rows, :] = times(cot[rows, :], up[...], 1, 1).astype(BF16)
        return carry

    lax.fori_loop(0, MESH_ROWS // 256, step, 0)
    scatter_back(coeffs, lowered, source, table, M_SLOTS, EXTENDED)
    write_halo(table, own, (h0, h1, h2, h3))


def encode_body(
    source, shown, packed, weight, coeffs, message, points, slope, mesh, sent, slope_m, mine, embedded
):
    step = pl.program_id(0)
    low = low_lanes(PACKED)
    for p in range(4):
        a = packed[2 * p]
        b = packed[2 * p + 1]
        lanes = slice(p * 128, p * 128 + 128)
        points[0:SPLIT, lanes] = jnp.where(low, a, swap_halves(b))[0:SPLIT]
        points[SPLIT:CHAN, lanes] = jnp.where(low, swap_halves(a), b)
    pre = times(points[...], weight[...], 0, 0)
    s = sigmoid(pre)
    e = pre * s
    embedded[chunk(step, 512), :] = e.astype(BF16)
    slope[...] = (s + e * (1.0 - s)).astype(BF16)

    @pl.when(step == GRID_ROWS // 512 - 1)
    def _():
        def mix(b, carry):
            pick = lambda b, k: embedded[rows_of(source[b, k]), :]
            mesh[rows_of(b), :] = gather_mix(coeffs, pick, G_SLOTS, b).astype(BF16)
            return carry

        lax.fori_loop(0, MESH_BLOCKS, mix, 0, unroll=2)

        def talk(c, carry):
            rows = chunk(c, 256)
            pre = times(mesh[rows, :], message[...])
            s = sigmoid(pre)
            e = pre * s
            sent[rows, :] = e.astype(BF16)
            slope_m[rows, :] = (s + e * (1.0 - s)).astype(BF16)
            return carry

        lax.fori_loop(0, MESH_ROWS // 256, talk, 0)
        for h in range(SHOWN):
            mine[h] = sent[rows_of(shown[0, h]), :]


def extend(extended, sent, halos):
    extended[0:MESH_ROWS, :] = sent[...]
    for e in range(4):
        for h in range(SHOWN):
            at = MESH_ROWS + (e * SHOWN + h) * BLOCK
            extended[at : at + BLOCK, :] = halos[e][h]


def mix_mesh(coeffs, extended, source, aggregate):
    def mix(b, carry):
        pick = lambda b, k: extended[rows_of(source[b, k]), :]
        aggregate[rows_of(b), :] = gather_mix(coeffs, pick, M_SLOTS, b).astype(BF16)
        return carry

    lax.fori_loop(0, MESH_BLOCKS, mix, 0, unroll=2)


def forward_body(
    source, shown, sent, n0, n1, n2, n3, coeffs, mesh, up, message,
    aggregate, mesh_1, sent_1, slope_m, mine, extended,
):
    extend(extended, sent, (n0, n1, n2, n3))
    mix_mesh(coeffs, extended, source, aggregate)

    def step(c, carry):
        rows = chunk(c, 256)
        state = (mesh[rows, :].astype(F32) + times(aggregate[rows, :], up[...])).astype(BF16)
        mesh_1[rows, :] = state
        pre = times(state, message[...])
        s = sigmoid(pre)
        e = pre * s
        sent_1[rows, :] = e.astype(BF16)
        slope_m[rows, :] = (s + e * (1.0 - s)).astype(BF16)
        return carry

    lax.fori_loop(0, MESH_ROWS // 256, step, 0)
    for h in range(SHOWN):
        mine[h] = sent_1[rows_of(shown[0, h]), :]


def backward_body(
    source, shown, own, r0, r1, r2, r3, slope_m, cot, message, up, coeffs,
    grad_pre, grad_1, own_0, h0, h1, h2, h3, table, lowered, grad_msg,
):
    grad_msg[...] = own[...].astype(F32)
    add_returned(own, (r0, r1, r2, r3), shown, grad_msg)

    def step(c, carry):
        rows = chunk(c, 256)
        gp = (grad_msg[rows, :] * slope_m[rows, :].astype(F32)).astype(BF16)
        grad_pre[rows, :] = gp
        g = cot[rows, :].astype(F32) + times(gp, message[...], 1, 1)
        grad_1[rows, :] = g
        lowered[rows, :] = times(g.astype(BF16), up[...], 1, 1).astype(BF16)
        return carry

    lax.fori_loop(0, MESH_ROWS // 256, step, 0)
    scatter_back(coeffs, lowered, source, table, M_SLOTS, EXTENDED)
    write_halo(table, own_0, (h0, h1, h2, h3))


def write_slabs(out, first, values):
    rows = values.shape[0]
    for c in range(4):
        out[first + c * rows : first + (c + 1) * rows, :] = values[:, c * 128 : (c + 1) * 128].astype(BF16)


def grads_body(
    source, sent, n0, n1, n2, n3, coeffs, mesh, up, cot, aggregate_0, grad_1, grad_pre,
    mesh_out, grads, extended, aggregate,
):
    write_slabs(grads, 0, times(aggregate_0[...], grad_1[...].astype(BF16), 0, 0))
    write_slabs(grads, SLAB, times(mesh[...], grad_pre[...], 0, 0))
    extend(extended, sent, (n0, n1, n2, n3))
    mix_mesh(coeffs, extended, source, aggregate)

    def step(c, carry):
        rows = chunk(c, 256)
        update = times(aggregate[rows, :], up[...])
        mesh_out[rows, :] = (mesh[rows, :].astype(F32) + update).astype(BF16)
        return carry

    lax.fori_loop(0, MESH_ROWS // 256, step, 0)
    write_slabs(grads, 2 * SLAB, times(aggregate[...], cot[...], 0, 0))


def final_body(
    source, shown, own, r0, r1, r2, r3, slope_m, grad_1, message, mesh, coeffs, slope, points,
    grads, table, grad_pre, lowered, grad_msg, total,
):
    c = pl.program_id(0)

    @pl.when(c == 0)
    def _():
        grad_msg[...] = own[...].astype(F32)
        add_returned(own, (r0, r1, r2, r3), shown, grad_msg)

        def step(c, carry):
            rows = chunk(c, 256)
            gp = (grad_msg[rows, :] * slope_m[rows, :].astype(F32)).astype(BF16)
            grad_pre[rows, :] = gp
            lowered[rows, :] = (grad_1[rows, :] + times(gp, message[...], 1, 1)).astype(BF16)
            return carry

        lax.fori_loop(0, MESH_ROWS // 256, step, 0)
        scatter_back(coeffs, lowered, source, table, G_SLOTS, GRID_BLOCKS)
        write_slabs(grads, 0, times(mesh[...], grad_pre[...], 0, 0))
        total[...] = jnp.zeros_like(total)

    grad = table[pl.ds(pl.multiple_of(c * 8, 8), 8)].reshape(512, WIDTH).astype(BF16)
    grad = (grad.astype(F32) * slope[...].astype(F32)).astype(BF16)
    total[0:CHAN, :] = total[0:CHAN, :] + times(points[...], grad)

    @pl.when(c == GRID_ROWS // 512 - 1)
    def _():
        write_slabs(grads, SLAB, total[...])


def sum_body(early, late, out, total):
    total[0:EARLY, :] = jnp.sum(early[...].astype(F32), axis=0)
    total[EARLY : EARLY + LATE, :] = jnp.sum(late[...].astype(F32), axis=0)
    rounded = total[...].astype(BF16)

    def one(i, carry):
        out[i] = rounded
        return carry

    lax.fori_loop(0, DEVICES, one, 0, unroll=8)


def unpack_body(parts, d_embed, ms_grad, up_grad, early, late):
    def one(i, carry):
        part = parts[i].astype(F32)
        early[pl.ds(pl.multiple_of(i * EARLY, 8), EARLY), :] = part[0:EARLY]
        late[pl.ds(pl.multiple_of(i * LATE, 8), LATE), :] = part[EARLY : EARLY + LATE]
        return carry

    lax.fori_loop(0, DEVICES, one, 0, unroll=4)
    for c in range(4):
        columns = slice(c * 128, (c + 1) * 128)
        at = lambda first: slice(first + c * WIDTH, first + (c + 1) * WIDTH)
        up_grad[0, :, columns] = early[at(0), :]
        ms_grad[1, :, columns] = early[at(SLAB), :]
        up_grad[1, :, columns] = early[at(2 * SLAB), :]
        ms_grad[0, :, columns] = late[at(0), :]
        d_embed[:, columns] = late[SLAB + c * TAIL : SLAB + c * TAIL + CHAN, :]


def shift(value, axis, steps):
    count = lax.axis_size(axis)
    return lax.ppermute(value, axis, [(i, (i + steps) % count) for i in range(count)])


def show(mine):
    return (shift(mine, "wide", 1), shift(mine, "wide", -1), shift(mine, "narrow", 1), shift(mine, "narrow", -1))


def give_back(h0, h1, h2, h3):
    return (shift(h0, "wide", -1), shift(h1, "wide", 1), shift(h2, "narrow", -1), shift(h3, "narrow", 1))


def exchange(parts):
    return lax.all_to_all(parts, AXES, split_axis=0, concat_axis=0, tiled=True)


def on_device(
    grid_feat, grid_send, w_embed, g2m_src, g2m_coef, mesh_src, mesh_coef, halo_send,
    message_weight, update_weight, cotangent,
):
    rows_bf16 = ((MESH_ROWS, WIDTH), BF16)
    rows_f32 = ((MESH_ROWS, WIDTH), F32)
    halo = ((SHOWN, BLOCK, WIDTH), BF16)
    mesh_scratch = pltpu.VMEM((MESH_ROWS, WIDTH), BF16)
    mesh_scratch32 = pltpu.VMEM((MESH_ROWS, WIDTH), F32)
    extended_scratch = pltpu.VMEM((EXTENDED * BLOCK, WIDTH), BF16)
    table_scratch = pltpu.VMEM((EXTENDED, BLOCK, WIDTH), F32)
    w_m = (message_weight[0], message_weight[1])
    w_u = (update_weight[0], update_weight[1])

    packed = pl.pallas_call(
        pack_body,
        grid=(GRID_BLOCKS // 16,),
        out_shape=jax.ShapeDtypeStruct((GRID_BLOCKS, PACKED, 2 * BLOCK), BF16),
        in_specs=[SM, pl.BlockSpec((CHAN, GRID_ROWS), lambda i: (0, 0))],
        out_specs=pl.BlockSpec((16, PACKED, 2 * BLOCK), lambda i: (i, 0, 0)),
        compiler_params=pltpu.CompilerParams(vmem_limit_bytes=56 * MIB),
        cost_estimate=pl.CostEstimate(flops=0, bytes_accessed=8 * MIB, transcendentals=0),
    )(grid_send, grid_feat.T)
    received = exchange(packed)

    g_mix = g2m_coef.transpose(0, 2, 1, 3).reshape(MESH_BLOCKS, BLOCK, G_SLOTS * BLOCK)
    m_mix = mesh_coef.transpose(0, 2, 1, 3).reshape(MESH_BLOCKS, BLOCK, M_SLOTS * BLOCK)

    own_1, *halos = kernel_call(
        early_back_body, [rows_f32] + [halo] * 4, [SM] + [VM] * 3, [table_scratch, mesh_scratch],
        flops=2 * 10**9, moved=8 * MIB,
    )(mesh_src, cotangent, w_u[1], m_mix)
    returned_1 = give_back(*halos)

    received, g_mix, m_mix = lax.optimization_barrier((received, g_mix, m_mix))
    whole = lambda *shape: pl.BlockSpec(shape, lambda i: (0,) * len(shape))
    points, slope, mesh_0, sent_0, slope_0, mine_0 = pl.pallas_call(
        encode_body,
        grid=(GRID_ROWS // 512,),
        out_shape=[
            jax.ShapeDtypeStruct((CHAN, GRID_ROWS), BF16),
            jax.ShapeDtypeStruct((GRID_ROWS, WIDTH), BF16),
            jax.ShapeDtypeStruct((MESH_ROWS, WIDTH), BF16),
            jax.ShapeDtypeStruct((MESH_ROWS, WIDTH), BF16),
            jax.ShapeDtypeStruct((MESH_ROWS, WIDTH), BF16),
            jax.ShapeDtypeStruct((SHOWN, BLOCK, WIDTH), BF16),
        ],
        in_specs=[
            SM, SM,
            pl.BlockSpec((8, PACKED, 2 * BLOCK), lambda i: (i, 0, 0)),
            whole(CHAN, WIDTH), whole(MESH_BLOCKS, BLOCK, G_SLOTS * BLOCK), whole(WIDTH, WIDTH),
        ],
        out_specs=[
            pl.BlockSpec((CHAN, 512), lambda i: (0, i)),
            pl.BlockSpec((512, WIDTH), lambda i: (i, 0)),
            whole(MESH_ROWS, WIDTH), whole(MESH_ROWS, WIDTH), whole(MESH_ROWS, WIDTH),
            whole(SHOWN, BLOCK, WIDTH),
        ],
        scratch_shapes=[pltpu.VMEM((GRID_ROWS, WIDTH), BF16)],
        compiler_params=pltpu.CompilerParams(vmem_limit_bytes=56 * MIB),
        cost_estimate=pl.CostEstimate(flops=4 * 10**9, bytes_accessed=20 * MIB, transcendentals=0),
    )(g2m_src, halo_send, received, w_embed, g_mix, w_m[0])
    shown_0 = show(mine_0)

    aggregate_0, mesh_1, sent_1, slope_1, mine_1 = kernel_call(
        forward_body, [rows_bf16] * 4 + [halo], [SM, SM] + [VM] * 9, [extended_scratch],
        flops=2 * 10**9, moved=10 * MIB,
    )(mesh_src, halo_send, sent_0, *shown_0, m_mix, mesh_0, w_u[0], w_m[1])
    shown_1 = show(mine_1)

    grad_pre_1, grad_1, own_0, *halos = kernel_call(
        backward_body, [rows_bf16, rows_f32, rows_f32] + [halo] * 4, [SM, SM] + [VM] * 10,
        [table_scratch, mesh_scratch, mesh_scratch32], flops=2 * 10**9, moved=16 * MIB,
    )(mesh_src, halo_send, own_1, *returned_1, slope_1, cotangent, w_m[1], w_u[0], m_mix)
    returned_0 = give_back(*halos)

    mesh_out, early = kernel_call(
        grads_body, [rows_bf16, ((3 * SLAB, 128), BF16)], [SM] + [VM] * 12,
        [extended_scratch, mesh_scratch], flops=4 * 10**9, moved=14 * MIB,
    )(
        mesh_src, sent_1, *shown_1, m_mix, mesh_1, w_u[1], cotangent, aggregate_0, grad_1,
        grad_pre_1,
    )
    own_0, early = lax.optimization_barrier((own_0, early))
    early = exchange(early.reshape(DEVICES, EARLY, 128))

    late = pl.pallas_call(
        final_body,
        grid=(GRID_ROWS // 512,),
        out_shape=jax.ShapeDtypeStruct((SLAB + 4 * TAIL, 128), BF16),
        in_specs=[
            SM, SM, whole(MESH_ROWS, WIDTH), *[whole(SHOWN, BLOCK, WIDTH)] * 4,
            whole(MESH_ROWS, WIDTH), whole(MESH_ROWS, WIDTH), whole(WIDTH, WIDTH),
            whole(MESH_ROWS, WIDTH), whole(MESH_BLOCKS, BLOCK, G_SLOTS * BLOCK),
            pl.BlockSpec((512, WIDTH), lambda i: (i, 0)),
            pl.BlockSpec((CHAN, 512), lambda i: (0, i)),
        ],
        out_specs=whole(SLAB + 4 * TAIL, 128),
        scratch_shapes=[
            pltpu.VMEM((GRID_BLOCKS, BLOCK, WIDTH), F32),
            mesh_scratch, mesh_scratch, mesh_scratch32,
            pltpu.VMEM((TAIL, WIDTH), F32),
        ],
        compiler_params=pltpu.CompilerParams(vmem_limit_bytes=56 * MIB),
        cost_estimate=pl.CostEstimate(flops=4 * 10**9, bytes_accessed=24 * MIB, transcendentals=0),
    )(
        g2m_src, halo_send, own_0, *returned_0, slope_0, grad_1, w_m[0], mesh_0, g_mix, slope,
        points,
    )
    late = exchange(late.reshape(DEVICES, LATE, 128))

    totals = kernel_call(
        sum_body, [((DEVICES, EARLY + LATE, 128), BF16)], [VM, VM],
        [pltpu.VMEM((EARLY + LATE, 128), F32)], moved=5 * MIB,
    )(early, late)[0]
    d_embed, ms_grad, up_grad = kernel_call(
        unpack_body,
        [((CHAN, WIDTH), F32), ((2, WIDTH, WIDTH), F32), ((2, WIDTH, WIDTH), F32)],
        [VM],
        [pltpu.VMEM((3 * SLAB, 128), F32), pltpu.VMEM((SLAB + 4 * TAIL, 128), F32)],
        moved=7 * MIB,
    )(exchange(totals))
    return mesh_out, d_embed, ms_grad, up_grad


def solution(mesh):
    split = P(AXES, None)
    return jax.shard_map(
        on_device,
        mesh=mesh,
        in_specs=(
            split, split, P(), split, P(AXES, None, None, None), split, P(AXES, None, None, None),
            split, P(), P(), split,
        ),
        out_specs=(split, P(), P(), P()),
        check_vma=False,
    )
```

```python
import jax
import jax.numpy as jnp
from jax import lax
from jax.experimental import pallas as pl
from jax.experimental.pallas import tpu as pltpu
from jax.sharding import PartitionSpec as P

CHAN = 227
WIDTH = 512
BLOCK = 64
GRID_BLOCKS = 128
MESH_BLOCKS = 16
SHOWN = 4
G_SLOTS = 8
M_SLOTS = 6
EXTENDED = MESH_BLOCKS + 4 * SHOWN
MESH_ROWS = MESH_BLOCKS * BLOCK
GRID_ROWS = GRID_BLOCKS * BLOCK
SPLIT = 112
PACKED = CHAN - SPLIT
TAIL = 256
DEVICES = 128
SLAB = 4 * WIDTH
EARLY = 3 * SLAB // 16
LATE = (SLAB + 4 * TAIL) // 16
PART = (EARLY + LATE) // 8
HALF = 40
AXES = ("wide", "narrow")
BF16 = jnp.bfloat16
F32 = jnp.float32
MIB = 1 << 20

VM = pl.BlockSpec(memory_space=pltpu.VMEM)
SM = pl.BlockSpec(memory_space=pltpu.SMEM)


def kernel_call(body, outs, ins, scratch=(), flops=0, moved=0, limit=56):
    return pl.pallas_call(
        body,
        out_shape=[jax.ShapeDtypeStruct(shape, dtype) for shape, dtype in outs],
        in_specs=ins,
        out_specs=[VM] * len(outs),
        scratch_shapes=list(scratch),
        compiler_params=pltpu.CompilerParams(vmem_limit_bytes=limit * MIB),
        cost_estimate=pl.CostEstimate(flops=flops, bytes_accessed=moved, transcendentals=0),
    )


def times(left, right, left_dim=1, right_dim=0):
    return lax.dot_general(
        left, right, (((left_dim,), (right_dim,)), ((), ())), preferred_element_type=F32
    )


def sigmoid(values):
    return 0.5 * jnp.tanh(0.5 * values) + 0.5


def silu_grad(values):
    s = sigmoid(values)
    return s * (1.0 + values * (1.0 - s))


def swap_halves(tile):
    return pltpu.roll(tile, BLOCK, 1)


def low_lanes(rows):
    return lax.broadcasted_iota(jnp.int32, (rows, 2 * BLOCK), 1) < BLOCK


def rows_of(block):
    return pl.ds(pl.multiple_of(block * BLOCK, BLOCK), BLOCK)


def chunk(step, size):
    return pl.ds(pl.multiple_of(step * size, size), size)


def pack_body(send, features, out, target):
    step = pl.program_id(0)

    @pl.when(step == 0)
    def _():
        def invert(j, carry):
            target[send[0, j]] = j
            return carry

        lax.fori_loop(0, GRID_BLOCKS, invert, 0, unroll=8)

    low = low_lanes(PACKED)

    def pair(i, carry):
        lanes = chunk(i, 2 * BLOCK)
        first = features[0:PACKED, lanes]
        second = features[SPLIT:CHAN, lanes]
        at = step * 32 + 2 * i
        out[target[at]] = jnp.where(low, first, swap_halves(second))
        out[target[at + 1]] = jnp.where(low, swap_halves(first), second)
        return carry

    lax.fori_loop(0, 16, pair, 0, unroll=4)


def scatter_back(coeffs, gradient, source, table, slots, blocks):
    def clear(i, carry):
        table[i] = jnp.zeros((BLOCK, WIDTH), F32)
        return carry

    lax.fori_loop(0, blocks, clear, 0, unroll=4)

    def one(b, carry):
        parts = times(coeffs[b], gradient[rows_of(b), :], 0, 0)
        for k in range(slots):
            at = source[b, k]
            table[at] = table[at] + parts[k * BLOCK : (k + 1) * BLOCK]
        return carry

    lax.fori_loop(0, MESH_BLOCKS, one, 0)


def gather_mix(coeffs, pick, slots, b):
    picked = jnp.concatenate([pick(b, k) for k in range(slots)], axis=0)
    return times(coeffs[b], picked)


def add_returned(own, returned, shown, take):
    for h in range(SHOWN):
        at = shown[0, h]
        extra = (returned[0][h].astype(F32) + returned[1][h].astype(F32)) + (
            returned[2][h].astype(F32) + returned[3][h].astype(F32)
        )
        take[rows_of(at), :] = take[rows_of(at), :] + extra


def write_halo(table, own, halos):
    for i in range(MESH_BLOCKS):
        own[i * BLOCK : (i + 1) * BLOCK, :] = table[i].astype(own.dtype)
    for e in range(4):
        for h in range(SHOWN):
            halos[e][h] = table[MESH_BLOCKS + e * SHOWN + h].astype(BF16)


def early_back_body(source, cot, up, coeffs, own, h0, h1, h2, h3, table, lowered):
    def step(c, carry):
        rows = chunk(c, 256)
        lowered[rows, :] = times(cot[rows, :], up[...], 1, 1).astype(BF16)
        return carry

    lax.fori_loop(0, MESH_ROWS // 256, step, 0)
    scatter_back(coeffs, lowered, source, table, M_SLOTS, EXTENDED)
    write_halo(table, own, (h0, h1, h2, h3))


def encode_body(
    source, shown, packed, weight, coeffs, message, points, slope, table, mine, embedded, mesh
):
    step = pl.program_id(0)
    low = low_lanes(PACKED)

    def embed(c, carry):
        for p in range(4):
            a = packed[c * 8 + 2 * p]
            b = packed[c * 8 + 2 * p + 1]
            lanes = pl.ds(pl.multiple_of(c * 512 + p * 128, 128), 128)
            points[0:SPLIT, lanes] = jnp.where(low, a, swap_halves(b))[0:SPLIT]
            points[SPLIT:CHAN, lanes] = jnp.where(low, swap_halves(a), b)
        rows = chunk(c, 512)
        pre = times(points[:, rows], weight[...], 0, 0)
        s = sigmoid(pre)
        e = pre * s
        low_e = e.astype(BF16)
        table[rows, :] = low_e
        embedded[chunk(step * 4 + c, 512), :] = low_e
        slope[rows, :] = (s + e * (1.0 - s)).astype(BF16)
        return carry

    lax.fori_loop(0, 4, embed, 0)

    @pl.when(step == 3)
    def _():
        pick = lambda b, k: embedded[rows_of(source[b, k]), :]
        for h in range(SHOWN):
            row = gather_mix(coeffs, pick, G_SLOTS, shown[0, h])
            mesh[h * BLOCK : (h + 1) * BLOCK, :] = row.astype(BF16)
        pre = times(mesh[...], message[...])
        mine[...] = (pre * sigmoid(pre)).astype(BF16).reshape(SHOWN, BLOCK, WIDTH)


def mesh_body(source, embedded, coeffs, message, mesh, sent, slope_m):
    def mix(b, carry):
        pick = lambda b, k: embedded[rows_of(source[b, k]), :]
        mesh[rows_of(b), :] = gather_mix(coeffs, pick, G_SLOTS, b).astype(BF16)
        return carry

    lax.fori_loop(0, MESH_BLOCKS, mix, 0, unroll=2)

    def talk(c, carry):
        rows = chunk(c, 256)
        pre = times(mesh[rows, :], message[...])
        s = sigmoid(pre)
        e = pre * s
        sent[rows, :] = e.astype(BF16)
        slope_m[rows, :] = (s + e * (1.0 - s)).astype(BF16)
        return carry

    lax.fori_loop(0, MESH_ROWS // 256, talk, 0)


def extend(extended, sent, halos):
    extended[0:MESH_ROWS, :] = sent[...]
    for e in range(4):
        for h in range(SHOWN):
            at = MESH_ROWS + (e * SHOWN + h) * BLOCK
            extended[at : at + BLOCK, :] = halos[e][h]


def mix_mesh(coeffs, extended, source, aggregate):
    def mix(b, carry):
        pick = lambda b, k: extended[rows_of(source[b, k]), :]
        aggregate[rows_of(b), :] = gather_mix(coeffs, pick, M_SLOTS, b).astype(BF16)
        return carry

    lax.fori_loop(0, MESH_BLOCKS, mix, 0, unroll=2)


def forward_body(
    source, shown, sent, n0, n1, n2, n3, coeffs, mesh, up, message,
    aggregate, mesh_1, sent_1, slope_m, mine, extended,
):
    extend(extended, sent, (n0, n1, n2, n3))
    mix_mesh(coeffs, extended, source, aggregate)

    def step(c, carry):
        rows = chunk(c, 256)
        state = (mesh[rows, :].astype(F32) + times(aggregate[rows, :], up[...])).astype(BF16)
        mesh_1[rows, :] = state
        pre = times(state, message[...])
        s = sigmoid(pre)
        e = pre * s
        sent_1[rows, :] = e.astype(BF16)
        slope_m[rows, :] = (s + e * (1.0 - s)).astype(BF16)
        return carry

    lax.fori_loop(0, MESH_ROWS // 256, step, 0)
    for h in range(SHOWN):
        mine[h] = sent_1[rows_of(shown[0, h]), :]


def backward_body(
    source, shown, own, r0, r1, r2, r3, slope_m, cot, message, up, coeffs,
    grad_pre, grad_1, own_0, h0, h1, h2, h3, table, lowered, grad_msg,
):
    grad_msg[...] = own[...].astype(F32)
    add_returned(own, (r0, r1, r2, r3), shown, grad_msg)

    def step(c, carry):
        rows = chunk(c, 256)
        gp = (grad_msg[rows, :] * slope_m[rows, :].astype(F32)).astype(BF16)
        grad_pre[rows, :] = gp
        g = cot[rows, :].astype(F32) + times(gp, message[...], 1, 1)
        grad_1[rows, :] = g
        lowered[rows, :] = times(g.astype(BF16), up[...], 1, 1).astype(BF16)
        return carry

    lax.fori_loop(0, MESH_ROWS // 256, step, 0)
    scatter_back(coeffs, lowered, source, table, M_SLOTS, EXTENDED)
    write_halo(table, own_0, (h0, h1, h2, h3))


def write_slabs(out, first, values):
    rows = values.shape[0]
    for c in range(4):
        out[first + c * rows : first + (c + 1) * rows, :] = values[:, c * 128 : (c + 1) * 128].astype(BF16)


def grads_body(
    source, sent, n0, n1, n2, n3, coeffs, mesh, up, cot, aggregate_0, grad_1, grad_pre,
    mesh_out, grads, extended, aggregate,
):
    write_slabs(grads, 0, times(aggregate_0[...], grad_1[...].astype(BF16), 0, 0))
    write_slabs(grads, SLAB, times(mesh[...], grad_pre[...], 0, 0))
    extend(extended, sent, (n0, n1, n2, n3))
    mix_mesh(coeffs, extended, source, aggregate)

    def step(c, carry):
        rows = chunk(c, 256)
        update = times(aggregate[rows, :], up[...])
        mesh_out[rows, :] = (mesh[rows, :].astype(F32) + update).astype(BF16)
        return carry

    lax.fori_loop(0, MESH_ROWS // 256, step, 0)
    write_slabs(grads, 2 * SLAB, times(aggregate[...], cot[...], 0, 0))


def final_body(
    source, shown, own, r0, r1, r2, r3, slope_m, grad_1, message, mesh, coeffs, slope, points,
    grads, table, grad_pre, lowered, grad_msg, total,
):
    c = pl.program_id(0)

    @pl.when(c == 0)
    def _():
        grad_msg[...] = own[...].astype(F32)
        add_returned(own, (r0, r1, r2, r3), shown, grad_msg)

        def step(c, carry):
            rows = chunk(c, 256)
            gp = (grad_msg[rows, :] * slope_m[rows, :].astype(F32)).astype(BF16)
            grad_pre[rows, :] = gp
            lowered[rows, :] = (grad_1[rows, :] + times(gp, message[...], 1, 1)).astype(BF16)
            return carry

        lax.fori_loop(0, MESH_ROWS // 256, step, 0)
        scatter_back(coeffs, lowered, source, table, G_SLOTS, GRID_BLOCKS)
        write_slabs(grads, 0, times(mesh[...], grad_pre[...], 0, 0))
        total[...] = jnp.zeros_like(total)

    def grid_step(i, carry):
        rows = chunk(i, 512)
        grad = table[pl.ds(c * 32 + i * 8, 8)].reshape(512, WIDTH).astype(BF16)
        grad = (grad.astype(F32) * slope[rows, :].astype(F32)).astype(BF16)
        total[0:CHAN, :] = total[0:CHAN, :] + times(points[:, rows], grad)
        return carry

    lax.fori_loop(0, 4, grid_step, 0)

    @pl.when(c == 3)
    def _():
        write_slabs(grads, SLAB, total[...])


def sum_wide_body(early, late, out):
    out[0:EARLY, :] = jnp.sum(early[...].astype(F32), axis=0).astype(BF16)
    out[EARLY : EARLY + LATE, :] = jnp.sum(late[...].astype(F32), axis=0).astype(BF16)


def sum_narrow_body(parts, out):
    total = jnp.sum(parts[...].astype(F32), axis=0)
    halves = (total[0:HALF].astype(BF16), total[PART - HALF : PART].astype(BF16))

    def one(i, carry):
        out[2 * i] = halves[0]
        out[2 * i + 1] = halves[1]
        return carry

    lax.fori_loop(0, DEVICES // 2, one, 0, unroll=8)


def unpack_body(odd, own, other, d_embed, ms_grad, up_grad, sums):
    def one(i, carry):
        at = pl.multiple_of(i * PART, 8)

        @pl.when(odd[0] == 0)
        def _():
            sums[pl.ds(at + PART - HALF, HALF), :] = other[i].astype(F32)
            sums[pl.ds(at, HALF), :] = own[i].astype(F32)

        @pl.when(odd[0] == 1)
        def _():
            sums[pl.ds(at + PART - HALF, HALF), :] = own[i].astype(F32)
            sums[pl.ds(at, HALF), :] = other[i].astype(F32)

        return carry

    lax.fori_loop(0, DEVICES, one, 0)
    runs = EARLY + LATE

    def place(out, columns, first, rows, share, offset):
        done = 0
        while done < rows:
            w, r = divmod(first + done, share)
            take = min(rows - done, share - r)
            at = w * runs + offset + r
            out[done : done + take, columns] = sums[at : at + take, :]
            done += take

    for c in range(4):
        columns = slice(c * 128, (c + 1) * 128)
        place(up_grad.at[0], columns, c * WIDTH, WIDTH, EARLY, 0)
        place(ms_grad.at[1], columns, SLAB + c * WIDTH, WIDTH, EARLY, 0)
        place(up_grad.at[1], columns, 2 * SLAB + c * WIDTH, WIDTH, EARLY, 0)
        place(ms_grad.at[0], columns, c * WIDTH, WIDTH, LATE, EARLY)
        place(d_embed, columns, SLAB + c * TAIL, CHAN, LATE, EARLY)


def shift(value, axis, steps):
    count = lax.axis_size(axis)
    return lax.ppermute(value, axis, [(i, (i + steps) % count) for i in range(count)])


def show(mine):
    return (shift(mine, "wide", 1), shift(mine, "wide", -1), shift(mine, "narrow", 1), shift(mine, "narrow", -1))


def give_back(h0, h1, h2, h3):
    return (shift(h0, "wide", -1), shift(h1, "wide", 1), shift(h2, "narrow", -1), shift(h3, "narrow", 1))


def exchange(parts, axes):
    return lax.all_to_all(parts, axes, split_axis=0, concat_axis=0, tiled=True)


def on_device(
    grid_feat, grid_send, w_embed, g2m_src, g2m_coef, mesh_src, mesh_coef, halo_send,
    message_weight, update_weight, cotangent,
):
    rows_bf16 = ((MESH_ROWS, WIDTH), BF16)
    rows_f32 = ((MESH_ROWS, WIDTH), F32)
    halo = ((SHOWN, BLOCK, WIDTH), BF16)
    mesh_scratch = pltpu.VMEM((MESH_ROWS, WIDTH), BF16)
    mesh_scratch32 = pltpu.VMEM((MESH_ROWS, WIDTH), F32)
    extended_scratch = pltpu.VMEM((EXTENDED * BLOCK, WIDTH), BF16)
    table_scratch = pltpu.VMEM((EXTENDED, BLOCK, WIDTH), F32)
    w_m = (message_weight[0], message_weight[1])
    w_u = (update_weight[0], update_weight[1])

    packed = pl.pallas_call(
        pack_body,
        grid=(4,),
        out_shape=jax.ShapeDtypeStruct((GRID_BLOCKS, PACKED, 2 * BLOCK), BF16),
        in_specs=[SM, pl.BlockSpec((CHAN, GRID_ROWS // 4), lambda i: (0, i))],
        out_specs=pl.BlockSpec((GRID_BLOCKS, PACKED, 2 * BLOCK), lambda i: (0, 0, 0)),
        scratch_shapes=[pltpu.SMEM((GRID_BLOCKS,), jnp.int32)],
        compiler_params=pltpu.CompilerParams(vmem_limit_bytes=24 * MIB),
        cost_estimate=pl.CostEstimate(flops=0, bytes_accessed=8 * MIB, transcendentals=0),
    )(grid_send, grid_feat.T)
    packed, cotangent = lax.optimization_barrier((packed, cotangent))
    received = exchange(packed, AXES)

    g_mix = g2m_coef.transpose(0, 2, 1, 3).reshape(MESH_BLOCKS, BLOCK, G_SLOTS * BLOCK)
    m_mix = mesh_coef.transpose(0, 2, 1, 3).reshape(MESH_BLOCKS, BLOCK, M_SLOTS * BLOCK)

    own_1, *halos = kernel_call(
        early_back_body, [rows_f32] + [halo] * 4, [SM] + [VM] * 3, [table_scratch, mesh_scratch],
        flops=2 * 10**9, moved=8 * MIB, limit=20,
    )(mesh_src, cotangent, w_u[1], m_mix)
    returned_1 = give_back(*halos)

    received, g_mix, m_mix, own_1, *returned_1 = lax.optimization_barrier(
        (received, g_mix, m_mix, own_1, *returned_1)
    )
    whole = lambda *shape: pl.BlockSpec(shape, lambda i: (0,) * len(shape))
    points, slope, embedded, mine_0 = pl.pallas_call(
        encode_body,
        grid=(4,),
        out_shape=[
            jax.ShapeDtypeStruct((CHAN, GRID_ROWS), BF16),
            jax.ShapeDtypeStruct((GRID_ROWS, WIDTH), BF16),
            jax.ShapeDtypeStruct((GRID_ROWS, WIDTH), BF16),
            jax.ShapeDtypeStruct((SHOWN, BLOCK, WIDTH), BF16),
        ],
        in_specs=[
            SM, SM,
            pl.BlockSpec((32, PACKED, 2 * BLOCK), lambda i: (i, 0, 0)),
            whole(CHAN, WIDTH), whole(MESH_BLOCKS, BLOCK, G_SLOTS * BLOCK), whole(WIDTH, WIDTH),
        ],
        out_specs=[
            pl.BlockSpec((CHAN, 2048), lambda i: (0, i)),
            pl.BlockSpec((2048, WIDTH), lambda i: (i, 0)),
            pl.BlockSpec((2048, WIDTH), lambda i: (i, 0)),
            whole(SHOWN, BLOCK, WIDTH),
        ],
        scratch_shapes=[
            pltpu.VMEM((GRID_ROWS, WIDTH), BF16), pltpu.VMEM((SHOWN * BLOCK, WIDTH), BF16)
        ],
        compiler_params=pltpu.CompilerParams(vmem_limit_bytes=56 * MIB),
        cost_estimate=pl.CostEstimate(flops=4 * 10**9, bytes_accessed=26 * MIB, transcendentals=0),
    )(g2m_src, halo_send, received, w_embed, g_mix, w_m[0])
    shown_0 = show(mine_0)
    mesh_0, sent_0, slope_0 = kernel_call(
        mesh_body, [rows_bf16] * 3, [SM] + [VM] * 3, flops=2 * 10**9, moved=12 * MIB, limit=24,
    )(g2m_src, embedded, g_mix, w_m[0])

    aggregate_0, mesh_1, sent_1, slope_1, mine_1 = kernel_call(
        forward_body, [rows_bf16] * 4 + [halo], [SM, SM] + [VM] * 9, [extended_scratch],
        flops=2 * 10**9, moved=10 * MIB, limit=20,
    )(mesh_src, halo_send, sent_0, *shown_0, m_mix, mesh_0, w_u[0], w_m[1])
    shown_1 = show(mine_1)

    grad_pre_1, grad_1, own_0, *halos = kernel_call(
        backward_body, [rows_bf16, rows_f32, rows_f32] + [halo] * 4, [SM, SM] + [VM] * 10,
        [table_scratch, mesh_scratch, mesh_scratch32], flops=2 * 10**9, moved=16 * MIB, limit=28,
    )(mesh_src, halo_send, own_1, *returned_1, slope_1, cotangent, w_m[1], w_u[0], m_mix)
    returned_0 = give_back(*halos)

    mesh_out, early = kernel_call(
        grads_body, [rows_bf16, ((3 * SLAB, 128), BF16)], [SM] + [VM] * 12,
        [extended_scratch, mesh_scratch], flops=4 * 10**9, moved=14 * MIB, limit=24,
    )(
        mesh_src, sent_1, *shown_1, m_mix, mesh_1, w_u[1], cotangent, aggregate_0, grad_1,
        grad_pre_1,
    )
    own_0, early = lax.optimization_barrier((own_0, early))
    early = exchange(early.reshape(16, EARLY, 128), "wide")

    late = pl.pallas_call(
        final_body,
        grid=(4,),
        out_shape=jax.ShapeDtypeStruct((SLAB + 4 * TAIL, 128), BF16),
        in_specs=[
            SM, SM, whole(MESH_ROWS, WIDTH), *[whole(SHOWN, BLOCK, WIDTH)] * 4,
            whole(MESH_ROWS, WIDTH), whole(MESH_ROWS, WIDTH), whole(WIDTH, WIDTH),
            whole(MESH_ROWS, WIDTH), whole(MESH_BLOCKS, BLOCK, G_SLOTS * BLOCK),
            pl.BlockSpec((2048, WIDTH), lambda i: (i, 0)),
            pl.BlockSpec((CHAN, 2048), lambda i: (0, i)),
        ],
        out_specs=whole(SLAB + 4 * TAIL, 128),
        scratch_shapes=[
            pltpu.VMEM((GRID_BLOCKS, BLOCK, WIDTH), F32),
            mesh_scratch, mesh_scratch, mesh_scratch32,
            pltpu.VMEM((TAIL, WIDTH), F32),
        ],
        compiler_params=pltpu.CompilerParams(vmem_limit_bytes=50 * MIB),
        cost_estimate=pl.CostEstimate(flops=4 * 10**9, bytes_accessed=24 * MIB, transcendentals=0),
    )(
        g2m_src, halo_send, own_0, *returned_0, slope_0, grad_1, w_m[0], mesh_0, g_mix, slope,
        points,
    )
    late = exchange(late.reshape(16, LATE, 128), "wide")

    parts = kernel_call(
        sum_wide_body, [((EARLY + LATE, 128), BF16)], [VM, VM], moved=3 * MIB, limit=16
    )(early, late)[0]
    totals = kernel_call(
        sum_narrow_body, [((DEVICES, HALF, 128), BF16)], [VM], moved=2 * MIB, limit=16
    )(exchange(parts.reshape(8, PART, 128), "narrow"))[0]
    own = exchange(totals, AXES)
    other = lax.ppermute(own, "narrow", [(i, i ^ 1) for i in range(8)])
    d_embed, ms_grad, up_grad = kernel_call(
        unpack_body,
        [((CHAN, WIDTH), F32), ((2, WIDTH, WIDTH), F32), ((2, WIDTH, WIDTH), F32)],
        [SM, VM, VM],
        [pltpu.VMEM((DEVICES * PART, 128), F32)],
        moved=7 * MIB,
        limit=24,
    )((lax.axis_index("narrow") % 2).reshape(1).astype(jnp.int32), own, other)
    return mesh_out, d_embed, ms_grad, up_grad


def solution(mesh):
    split = P(AXES, None)
    return jax.shard_map(
        on_device,
        mesh=mesh,
        in_specs=(
            split, split, P(), split, P(AXES, None, None, None), split, P(AXES, None, None, None),
            split, P(), P(), split,
        ),
        out_specs=(split, P(), P(), P()),
        check_vma=False,
    )
```

```python
import jax
import jax.numpy as jnp
from jax import lax
from jax.experimental import pallas as pl
from jax.experimental.pallas import tpu as pltpu
from jax.sharding import PartitionSpec as P

CHAN = 227
WIDTH = 512
BLOCK = 64
GRID_BLOCKS = 128
MESH_BLOCKS = 16
SHOWN = 4
G_SLOTS = 8
M_SLOTS = 6
EXTENDED = MESH_BLOCKS + 4 * SHOWN
MESH_ROWS = MESH_BLOCKS * BLOCK
GRID_ROWS = GRID_BLOCKS * BLOCK
SPLIT = 112
PACKED = CHAN - SPLIT
TAIL = 256
DEVICES = 128
SLAB = 4 * WIDTH
EARLY = 3 * SLAB // DEVICES
LATE = (SLAB + 4 * TAIL) // DEVICES
PART = EARLY + LATE
HALF = 40
AXES = ("wide", "narrow")
BF16 = jnp.bfloat16
F32 = jnp.float32
MIB = 1 << 20

VM = pl.BlockSpec(memory_space=pltpu.VMEM)
SM = pl.BlockSpec(memory_space=pltpu.SMEM)


def kernel_call(body, outs, ins, scratch=(), flops=0, moved=0, limit=56):
    return pl.pallas_call(
        body,
        out_shape=[jax.ShapeDtypeStruct(shape, dtype) for shape, dtype in outs],
        in_specs=ins,
        out_specs=[VM] * len(outs),
        scratch_shapes=list(scratch),
        compiler_params=pltpu.CompilerParams(vmem_limit_bytes=limit * MIB),
        cost_estimate=pl.CostEstimate(flops=flops, bytes_accessed=moved, transcendentals=0),
    )


def times(left, right, left_dim=1, right_dim=0):
    return lax.dot_general(
        left, right, (((left_dim,), (right_dim,)), ((), ())), preferred_element_type=F32
    )


def sigmoid(values):
    return 0.5 * jnp.tanh(0.5 * values) + 0.5


def silu_grad(values):
    s = sigmoid(values)
    return s * (1.0 + values * (1.0 - s))


def swap_halves(tile):
    return pltpu.roll(tile, BLOCK, 1)


def low_lanes(rows):
    return lax.broadcasted_iota(jnp.int32, (rows, 2 * BLOCK), 1) < BLOCK


def rows_of(block):
    return pl.ds(pl.multiple_of(block * BLOCK, BLOCK), BLOCK)


def chunk(step, size):
    return pl.ds(pl.multiple_of(step * size, size), size)


def pack_body(send, features, out, target):
    step = pl.program_id(0)

    @pl.when(step == 0)
    def _():
        def invert(j, carry):
            target[send[0, j]] = j
            return carry

        lax.fori_loop(0, GRID_BLOCKS, invert, 0, unroll=8)

    low = low_lanes(PACKED)

    def pair(i, carry):
        lanes = chunk(i, 2 * BLOCK)
        first = features[0:PACKED, lanes]
        second = features[SPLIT:CHAN, lanes]
        at = step * 32 + 2 * i
        out[target[at]] = jnp.where(low, first, swap_halves(second))
        out[target[at + 1]] = jnp.where(low, swap_halves(first), second)
        return carry

    lax.fori_loop(0, 16, pair, 0, unroll=4)


def scatter_back(coeffs, gradient, source, table, slots, blocks):
    def clear(i, carry):
        table[i] = jnp.zeros((BLOCK, WIDTH), F32)
        return carry

    lax.fori_loop(0, blocks, clear, 0, unroll=4)

    def one(b, carry):
        parts = times(coeffs[b], gradient[rows_of(b), :], 0, 0)
        for k in range(slots):
            at = source[b, k]
            table[at] = table[at] + parts[k * BLOCK : (k + 1) * BLOCK]
        return carry

    lax.fori_loop(0, MESH_BLOCKS, one, 0)


def gather_mix(coeffs, pick, slots, b):
    picked = jnp.concatenate([pick(b, k) for k in range(slots)], axis=0)
    return times(coeffs[b], picked)


def add_returned(own, returned, shown, take):
    for h in range(SHOWN):
        at = shown[0, h]
        extra = (returned[0][h].astype(F32) + returned[1][h].astype(F32)) + (
            returned[2][h].astype(F32) + returned[3][h].astype(F32)
        )
        take[rows_of(at), :] = take[rows_of(at), :] + extra


def write_halo(table, own, halos):
    for i in range(MESH_BLOCKS):
        own[i * BLOCK : (i + 1) * BLOCK, :] = table[i].astype(own.dtype)
    for e in range(4):
        for h in range(SHOWN):
            halos[e][h] = table[MESH_BLOCKS + e * SHOWN + h].astype(BF16)


def early_back_body(source, cot, up, coeffs, own, h0, h1, h2, h3, table, lowered):
    def step(c, carry):
        rows = chunk(c, 256)
        lowered[rows, :] = times(cot[rows, :], up[...], 1, 1).astype(BF16)
        return carry

    lax.fori_loop(0, MESH_ROWS // 256, step, 0)
    scatter_back(coeffs, lowered, source, table, M_SLOTS, EXTENDED)
    write_halo(table, own, (h0, h1, h2, h3))


def encode_body(
    source, shown, packed, weight, coeffs, message, points, slope, table, mine, embedded, mesh
):
    step = pl.program_id(0)
    low = low_lanes(PACKED)

    def embed(c, carry):
        for p in range(4):
            a = packed[c * 8 + 2 * p]
            b = packed[c * 8 + 2 * p + 1]
            lanes = pl.ds(pl.multiple_of(c * 512 + p * 128, 128), 128)
            points[0:SPLIT, lanes] = jnp.where(low, a, swap_halves(b))[0:SPLIT]
            points[SPLIT:CHAN, lanes] = jnp.where(low, swap_halves(a), b)
        rows = chunk(c, 512)
        pre = times(points[:, rows], weight[...], 0, 0)
        s = sigmoid(pre)
        e = pre * s
        low_e = e.astype(BF16)
        table[rows, :] = low_e
        embedded[chunk(step * 4 + c, 512), :] = low_e
        slope[rows, :] = (s + e * (1.0 - s)).astype(BF16)
        return carry

    lax.fori_loop(0, 4, embed, 0)

    @pl.when(step == 3)
    def _():
        pick = lambda b, k: embedded[rows_of(source[b, k]), :]
        for h in range(SHOWN):
            row = gather_mix(coeffs, pick, G_SLOTS, shown[0, h])
            mesh[h * BLOCK : (h + 1) * BLOCK, :] = row.astype(BF16)
        pre = times(mesh[...], message[...])
        mine[...] = (pre * sigmoid(pre)).astype(BF16).reshape(SHOWN, BLOCK, WIDTH)


def mesh_body(source, embedded, coeffs, message, mesh, sent, slope_m):
    def mix(b, carry):
        pick = lambda b, k: embedded[rows_of(source[b, k]), :]
        mesh[rows_of(b), :] = gather_mix(coeffs, pick, G_SLOTS, b).astype(BF16)
        return carry

    lax.fori_loop(0, MESH_BLOCKS, mix, 0, unroll=2)

    def talk(c, carry):
        rows = chunk(c, 256)
        pre = times(mesh[rows, :], message[...])
        s = sigmoid(pre)
        e = pre * s
        sent[rows, :] = e.astype(BF16)
        slope_m[rows, :] = (s + e * (1.0 - s)).astype(BF16)
        return carry

    lax.fori_loop(0, MESH_ROWS // 256, talk, 0)


def extend(extended, sent, halos):
    extended[0:MESH_ROWS, :] = sent[...]
    for e in range(4):
        for h in range(SHOWN):
            at = MESH_ROWS + (e * SHOWN + h) * BLOCK
            extended[at : at + BLOCK, :] = halos[e][h]


def mix_mesh(coeffs, extended, source, aggregate):
    def mix(b, carry):
        pick = lambda b, k: extended[rows_of(source[b, k]), :]
        aggregate[rows_of(b), :] = gather_mix(coeffs, pick, M_SLOTS, b).astype(BF16)
        return carry

    lax.fori_loop(0, MESH_BLOCKS, mix, 0, unroll=2)


def forward_body(
    source, shown, sent, n0, n1, n2, n3, coeffs, mesh, up, message,
    aggregate, mesh_1, sent_1, slope_m, mine, extended,
):
    extend(extended, sent, (n0, n1, n2, n3))
    mix_mesh(coeffs, extended, source, aggregate)

    def step(c, carry):
        rows = chunk(c, 256)
        state = (mesh[rows, :].astype(F32) + times(aggregate[rows, :], up[...])).astype(BF16)
        mesh_1[rows, :] = state
        pre = times(state, message[...])
        s = sigmoid(pre)
        e = pre * s
        sent_1[rows, :] = e.astype(BF16)
        slope_m[rows, :] = (s + e * (1.0 - s)).astype(BF16)
        return carry

    lax.fori_loop(0, MESH_ROWS // 256, step, 0)
    for h in range(SHOWN):
        mine[h] = sent_1[rows_of(shown[0, h]), :]


def backward_body(
    source, shown, own, r0, r1, r2, r3, slope_m, cot, message, up, coeffs,
    grad_pre, grad_1, own_0, h0, h1, h2, h3, table, lowered, grad_msg,
):
    grad_msg[...] = own[...].astype(F32)
    add_returned(own, (r0, r1, r2, r3), shown, grad_msg)

    def step(c, carry):
        rows = chunk(c, 256)
        gp = (grad_msg[rows, :] * slope_m[rows, :].astype(F32)).astype(BF16)
        grad_pre[rows, :] = gp
        g = cot[rows, :].astype(F32) + times(gp, message[...], 1, 1)
        grad_1[rows, :] = g
        lowered[rows, :] = times(g.astype(BF16), up[...], 1, 1).astype(BF16)
        return carry

    lax.fori_loop(0, MESH_ROWS // 256, step, 0)
    scatter_back(coeffs, lowered, source, table, M_SLOTS, EXTENDED)
    write_halo(table, own_0, (h0, h1, h2, h3))


def write_slabs(out, first, values):
    rows = values.shape[0]
    for c in range(4):
        out[first + c * rows : first + (c + 1) * rows, :] = values[:, c * 128 : (c + 1) * 128].astype(BF16)


def grads_body(
    source, sent, n0, n1, n2, n3, coeffs, mesh, up, cot, aggregate_0, grad_1, grad_pre,
    mesh_out, grads, extended, aggregate,
):
    write_slabs(grads, 0, times(aggregate_0[...], grad_1[...].astype(BF16), 0, 0))
    write_slabs(grads, SLAB, times(mesh[...], grad_pre[...], 0, 0))
    extend(extended, sent, (n0, n1, n2, n3))
    mix_mesh(coeffs, extended, source, aggregate)

    def step(c, carry):
        rows = chunk(c, 256)
        update = times(aggregate[rows, :], up[...])
        mesh_out[rows, :] = (mesh[rows, :].astype(F32) + update).astype(BF16)
        return carry

    lax.fori_loop(0, MESH_ROWS // 256, step, 0)
    write_slabs(grads, 2 * SLAB, times(aggregate[...], cot[...], 0, 0))


def final_body(
    source, shown, own, r0, r1, r2, r3, slope_m, grad_1, message, mesh, coeffs, slope, points,
    grads, table, grad_pre, lowered, grad_msg, total,
):
    c = pl.program_id(0)

    @pl.when(c == 0)
    def _():
        grad_msg[...] = own[...].astype(F32)
        add_returned(own, (r0, r1, r2, r3), shown, grad_msg)

        def step(c, carry):
            rows = chunk(c, 256)
            gp = (grad_msg[rows, :] * slope_m[rows, :].astype(F32)).astype(BF16)
            grad_pre[rows, :] = gp
            lowered[rows, :] = (grad_1[rows, :] + times(gp, message[...], 1, 1)).astype(BF16)
            return carry

        lax.fori_loop(0, MESH_ROWS // 256, step, 0)
        scatter_back(coeffs, lowered, source, table, G_SLOTS, GRID_BLOCKS)
        write_slabs(grads, 0, times(mesh[...], grad_pre[...], 0, 0))
        total[...] = jnp.zeros_like(total)

    def grid_step(i, carry):
        rows = chunk(i, 512)
        grad = table[pl.ds(c * 32 + i * 8, 8)].reshape(512, WIDTH).astype(BF16)
        grad = (grad.astype(F32) * slope[rows, :].astype(F32)).astype(BF16)
        total[0:CHAN, :] = total[0:CHAN, :] + times(points[:, rows], grad)
        return carry

    lax.fori_loop(0, 4, grid_step, 0)

    @pl.when(c == 3)
    def _():
        write_slabs(grads, SLAB, total[...])


def sum_body(early, late, out, total):
    total[0:EARLY, :] = jnp.sum(early[...].astype(F32), axis=0)
    total[EARLY:PART, :] = jnp.sum(late[...].astype(F32), axis=0)
    halves = (total[0:HALF, :].astype(BF16), total[PART - HALF : PART, :].astype(BF16))

    def one(i, carry):
        out[2 * i] = halves[0]
        out[2 * i + 1] = halves[1]
        return carry

    lax.fori_loop(0, DEVICES // 2, one, 0, unroll=8)


def unpack_body(odd, own, other, d_embed, ms_grad, up_grad):
    slabs = []
    for out, rows in ((up_grad.at[0], WIDTH), (ms_grad.at[1], WIDTH), (up_grad.at[1], WIDTH)):
        slabs += [(out, slice(c * 128, c * 128 + 128), rows) for c in range(4)]
    late_slabs = [(ms_grad.at[0], slice(c * 128, c * 128 + 128), WIDTH) for c in range(4)]
    late_slabs += [(d_embed, slice(c * 128, c * 128 + 128), TAIL) for c in range(4)]

    def place(values, slabs, first):
        begin = 0
        for out, columns, rows in slabs:
            low, high = max(first, begin), min(first + values.shape[0], begin + rows)
            limit = min(high, begin + out.shape[0])
            if low < limit:
                out[low - begin : limit - begin, columns] = values[low - first : limit - first]
            begin += rows

    def unpack(lower, upper):
        for q in range(DEVICES):
            low = lower[q].astype(F32)
            high = upper[q].astype(F32)
            place(low, slabs, q * EARLY)
            place(high[2 * HALF - PART : HALF - LATE], slabs, q * EARLY + HALF)
            place(high[HALF - LATE :], late_slabs, q * LATE)

    @pl.when(odd[0] == 0)
    def _():
        unpack(own, other)

    @pl.when(odd[0] == 1)
    def _():
        unpack(other, own)


def shift(value, axis, steps):
    count = lax.axis_size(axis)
    return lax.ppermute(value, axis, [(i, (i + steps) % count) for i in range(count)])


def show(mine):
    return (shift(mine, "wide", 1), shift(mine, "wide", -1), shift(mine, "narrow", 1), shift(mine, "narrow", -1))


def give_back(h0, h1, h2, h3):
    return (shift(h0, "wide", -1), shift(h1, "wide", 1), shift(h2, "narrow", -1), shift(h3, "narrow", 1))


def exchange(parts):
    return lax.all_to_all(parts, AXES, split_axis=0, concat_axis=0, tiled=True)


def on_device(
    grid_feat, grid_send, w_embed, g2m_src, g2m_coef, mesh_src, mesh_coef, halo_send,
    message_weight, update_weight, cotangent,
):
    rows_bf16 = ((MESH_ROWS, WIDTH), BF16)
    rows_f32 = ((MESH_ROWS, WIDTH), F32)
    halo = ((SHOWN, BLOCK, WIDTH), BF16)
    mesh_scratch = pltpu.VMEM((MESH_ROWS, WIDTH), BF16)
    mesh_scratch32 = pltpu.VMEM((MESH_ROWS, WIDTH), F32)
    extended_scratch = pltpu.VMEM((EXTENDED * BLOCK, WIDTH), BF16)
    table_scratch = pltpu.VMEM((EXTENDED, BLOCK, WIDTH), F32)
    w_m = (message_weight[0], message_weight[1])
    w_u = (update_weight[0], update_weight[1])

    packed = pl.pallas_call(
        pack_body,
        grid=(4,),
        out_shape=jax.ShapeDtypeStruct((GRID_BLOCKS, PACKED, 2 * BLOCK), BF16),
        in_specs=[SM, pl.BlockSpec((CHAN, GRID_ROWS // 4), lambda i: (0, i))],
        out_specs=pl.BlockSpec((GRID_BLOCKS, PACKED, 2 * BLOCK), lambda i: (0, 0, 0)),
        scratch_shapes=[pltpu.SMEM((GRID_BLOCKS,), jnp.int32)],
        compiler_params=pltpu.CompilerParams(vmem_limit_bytes=56 * MIB),
        cost_estimate=pl.CostEstimate(flops=0, bytes_accessed=8 * MIB, transcendentals=0),
    )(grid_send, grid_feat.T)
    packed, cotangent = lax.optimization_barrier((packed, cotangent))
    received = exchange(packed)

    g_mix = g2m_coef.transpose(0, 2, 1, 3).reshape(MESH_BLOCKS, BLOCK, G_SLOTS * BLOCK)
    m_mix = mesh_coef.transpose(0, 2, 1, 3).reshape(MESH_BLOCKS, BLOCK, M_SLOTS * BLOCK)

    own_1, *halos = kernel_call(
        early_back_body, [rows_f32] + [halo] * 4, [SM] + [VM] * 3, [table_scratch, mesh_scratch],
        flops=2 * 10**9, moved=8 * MIB, limit=20,
    )(mesh_src, cotangent, w_u[1], m_mix)
    returned_1 = give_back(*halos)

    received, g_mix, m_mix, own_1, *returned_1 = lax.optimization_barrier(
        (received, g_mix, m_mix, own_1, *returned_1)
    )
    whole = lambda *shape: pl.BlockSpec(shape, lambda i: (0,) * len(shape))
    points, slope, embedded, mine_0 = pl.pallas_call(
        encode_body,
        grid=(4,),
        out_shape=[
            pltpu.HBM((CHAN, GRID_ROWS), BF16),
            pltpu.HBM((GRID_ROWS, WIDTH), BF16),
            jax.ShapeDtypeStruct((GRID_ROWS, WIDTH), BF16),
            jax.ShapeDtypeStruct((SHOWN, BLOCK, WIDTH), BF16),
        ],
        in_specs=[
            SM, SM,
            pl.BlockSpec((32, PACKED, 2 * BLOCK), lambda i: (i, 0, 0)),
            VM, VM, VM,
        ],
        out_specs=[
            pl.BlockSpec((CHAN, 2048), lambda i: (0, i)),
            pl.BlockSpec((2048, WIDTH), lambda i: (i, 0)),
            pl.BlockSpec((2048, WIDTH), lambda i: (i, 0)),
            whole(SHOWN, BLOCK, WIDTH),
        ],
        scratch_shapes=[
            pltpu.VMEM((GRID_ROWS, WIDTH), BF16), pltpu.VMEM((SHOWN * BLOCK, WIDTH), BF16)
        ],
        compiler_params=pltpu.CompilerParams(vmem_limit_bytes=28 * MIB),
        cost_estimate=pl.CostEstimate(flops=4 * 10**9, bytes_accessed=26 * MIB, transcendentals=0),
    )(g2m_src, halo_send, received, w_embed, g_mix, w_m[0])
    shown_0 = show(mine_0)
    mesh_0, sent_0, slope_0 = kernel_call(
        mesh_body, [rows_bf16] * 3, [SM] + [VM] * 3, flops=2 * 10**9, moved=12 * MIB, limit=24,
    )(g2m_src, embedded, g_mix, w_m[0])

    aggregate_0, mesh_1, sent_1, slope_1, mine_1 = kernel_call(
        forward_body, [rows_bf16] * 4 + [halo], [SM, SM] + [VM] * 9, [extended_scratch],
        flops=2 * 10**9, moved=10 * MIB, limit=20,
    )(mesh_src, halo_send, sent_0, *shown_0, m_mix, mesh_0, w_u[0], w_m[1])
    shown_1 = show(mine_1)

    grad_pre_1, grad_1, own_0, *halos = kernel_call(
        backward_body, [rows_bf16, rows_f32, rows_f32] + [halo] * 4, [SM, SM] + [VM] * 10,
        [table_scratch, mesh_scratch, mesh_scratch32], flops=2 * 10**9, moved=16 * MIB, limit=28,
    )(mesh_src, halo_send, own_1, *returned_1, slope_1, cotangent, w_m[1], w_u[0], m_mix)
    returned_0 = give_back(*halos)

    mesh_out, early = kernel_call(
        grads_body, [rows_bf16, ((3 * SLAB, 128), BF16)], [SM] + [VM] * 12,
        [extended_scratch, mesh_scratch], flops=4 * 10**9, moved=14 * MIB, limit=24,
    )(
        mesh_src, sent_1, *shown_1, m_mix, mesh_1, w_u[1], cotangent, aggregate_0, grad_1,
        grad_pre_1,
    )
    own_0, early = lax.optimization_barrier((own_0, early))
    early = exchange(early.reshape(DEVICES, EARLY, 128))

    late = pl.pallas_call(
        final_body,
        grid=(4,),
        out_shape=jax.ShapeDtypeStruct((SLAB + 4 * TAIL, 128), BF16),
        in_specs=[
            SM, SM, *[VM] * 10,
            pl.BlockSpec((2048, WIDTH), lambda i: (i, 0)),
            pl.BlockSpec((CHAN, 2048), lambda i: (0, i)),
        ],
        out_specs=whole(SLAB + 4 * TAIL, 128),
        scratch_shapes=[
            pltpu.VMEM((GRID_BLOCKS, BLOCK, WIDTH), F32),
            mesh_scratch, mesh_scratch, mesh_scratch32,
            pltpu.VMEM((TAIL, WIDTH), F32),
        ],
        compiler_params=pltpu.CompilerParams(vmem_limit_bytes=34 * MIB),
        cost_estimate=pl.CostEstimate(flops=4 * 10**9, bytes_accessed=24 * MIB, transcendentals=0),
    )(
        g2m_src, halo_send, own_0, *returned_0, slope_0, grad_1, w_m[0], mesh_0, g_mix, slope,
        points,
    )
    late, early = lax.optimization_barrier((late, early))
    late = exchange(late.reshape(DEVICES, LATE, 128))

    totals = kernel_call(
        sum_body, [((DEVICES, HALF, 128), BF16)], [VM, VM], [pltpu.VMEM((PART, 128), F32)],
        moved=4 * MIB, limit=16,
    )(early, late)[0]
    own = exchange(totals)
    other = lax.ppermute(own, "narrow", [(i, i ^ 1) for i in range(8)])
    d_embed, ms_grad, up_grad = kernel_call(
        unpack_body,
        [((CHAN, WIDTH), F32), ((2, WIDTH, WIDTH), F32), ((2, WIDTH, WIDTH), F32)],
        [SM, VM, VM],
        moved=7 * MIB,
        limit=24,
    )((lax.axis_index("narrow") % 2).reshape(1).astype(jnp.int32), own, other)
    return mesh_out, d_embed, ms_grad, up_grad


def solution(mesh):
    split = P(AXES, None)
    return jax.shard_map(
        on_device,
        mesh=mesh,
        in_specs=(
            split, split, P(), split, P(AXES, None, None, None), split, P(AXES, None, None, None),
            split, P(), P(), split,
        ),
        out_specs=(split, P(), P(), P()),
        check_vma=False,
    )
```

```python
import jax
import jax.numpy as jnp
from jax import lax
from jax.experimental import pallas as pl
from jax.experimental.pallas import tpu as pltpu
from jax.sharding import PartitionSpec as P

CHAN = 227
WIDTH = 512
BLOCK = 64
GRID_BLOCKS = 128
MESH_BLOCKS = 16
SHOWN = 4
G_SLOTS = 8
M_SLOTS = 6
EXTENDED = MESH_BLOCKS + 4 * SHOWN
MESH_ROWS = MESH_BLOCKS * BLOCK
GRID_ROWS = GRID_BLOCKS * BLOCK
SPLIT = 112
PACKED = CHAN - SPLIT
DEVICES = 128
COLUMNS = WIDTH // 2
SLABS = 2 * WIDTH
EARLY = 3 * SLABS // DEVICES
LATE = 2 * SLABS // DEVICES
PART = LATE + EARLY
AXES = ("wide", "narrow")
BF16 = jnp.bfloat16
F32 = jnp.float32
MIB = 1 << 20

VM = pl.BlockSpec(memory_space=pltpu.VMEM)
SM = pl.BlockSpec(memory_space=pltpu.SMEM)


def kernel_call(body, outs, ins, scratch=(), flops=0, moved=0, limit=56):
    return pl.pallas_call(
        body,
        out_shape=[jax.ShapeDtypeStruct(shape, dtype) for shape, dtype in outs],
        in_specs=ins,
        out_specs=[VM] * len(outs),
        scratch_shapes=list(scratch),
        compiler_params=pltpu.CompilerParams(vmem_limit_bytes=limit * MIB),
        cost_estimate=pl.CostEstimate(flops=flops, bytes_accessed=moved, transcendentals=0),
    )


def times(left, right, left_dim=1, right_dim=0):
    return lax.dot_general(
        left, right, (((left_dim,), (right_dim,)), ((), ())), preferred_element_type=F32
    )


def sigmoid(values):
    return 0.5 * jnp.tanh(0.5 * values) + 0.5


def silu_grad(values):
    s = sigmoid(values)
    return s * (1.0 + values * (1.0 - s))


def swap_halves(tile):
    return pltpu.roll(tile, BLOCK, 1)


def low_lanes(rows):
    return lax.broadcasted_iota(jnp.int32, (rows, 2 * BLOCK), 1) < BLOCK


def rows_of(block):
    return pl.ds(pl.multiple_of(block * BLOCK, BLOCK), BLOCK)


def chunk(step, size):
    return pl.ds(pl.multiple_of(step * size, size), size)


def pack_body(send, features, out, target):
    step = pl.program_id(0)

    @pl.when(step == 0)
    def _():
        def invert(j, carry):
            target[send[0, j]] = j
            return carry

        lax.fori_loop(0, GRID_BLOCKS, invert, 0, unroll=8)

    low = low_lanes(PACKED)

    def pair(i, carry):
        lanes = chunk(i, 2 * BLOCK)
        first = features[0:PACKED, lanes]
        second = features[SPLIT:CHAN, lanes]
        at = step * 32 + 2 * i
        out[target[at]] = jnp.where(low, first, swap_halves(second))
        out[target[at + 1]] = jnp.where(low, swap_halves(first), second)
        return carry

    lax.fori_loop(0, 16, pair, 0, unroll=4)


def scatter_back(coeffs, gradient, source, table, slots, blocks):
    def clear(i, carry):
        table[i] = jnp.zeros((BLOCK, WIDTH), F32)
        return carry

    lax.fori_loop(0, blocks, clear, 0, unroll=4)

    def one(b, carry):
        parts = times(coeffs[b], gradient[rows_of(b), :], 0, 0)
        for k in range(slots):
            at = source[b, k]
            table[at] = table[at] + parts[k * BLOCK : (k + 1) * BLOCK]
        return carry

    lax.fori_loop(0, MESH_BLOCKS, one, 0)


def gather_mix(coeffs, pick, slots, b):
    picked = jnp.concatenate([pick(b, k) for k in range(slots)], axis=0)
    return times(coeffs[b], picked)


def add_returned(own, returned, shown, take):
    for h in range(SHOWN):
        at = shown[0, h]
        extra = (returned[0][h].astype(F32) + returned[1][h].astype(F32)) + (
            returned[2][h].astype(F32) + returned[3][h].astype(F32)
        )
        take[rows_of(at), :] = take[rows_of(at), :] + extra


def write_halo(table, own, halos):
    for i in range(MESH_BLOCKS):
        own[i * BLOCK : (i + 1) * BLOCK, :] = table[i].astype(own.dtype)
    for e in range(4):
        for h in range(SHOWN):
            halos[e][h] = table[MESH_BLOCKS + e * SHOWN + h].astype(BF16)


def early_back_body(source, cot, up, coeffs, own, h0, h1, h2, h3, table, lowered):
    def step(c, carry):
        rows = chunk(c, 256)
        lowered[rows, :] = times(cot[rows, :], up[...], 1, 1).astype(BF16)
        return carry

    lax.fori_loop(0, MESH_ROWS // 256, step, 0)
    scatter_back(coeffs, lowered, source, table, M_SLOTS, EXTENDED)
    write_halo(table, own, (h0, h1, h2, h3))


def encode_body(
    source, shown, packed, weight, coeffs, message, points, slope, table, mine, embedded, mesh
):
    step = pl.program_id(0)
    low = low_lanes(PACKED)

    def embed(c, carry):
        for p in range(4):
            a = packed[c * 8 + 2 * p]
            b = packed[c * 8 + 2 * p + 1]
            lanes = pl.ds(pl.multiple_of(c * 512 + p * 128, 128), 128)
            points[0:SPLIT, lanes] = jnp.where(low, a, swap_halves(b))[0:SPLIT]
            points[SPLIT:CHAN, lanes] = jnp.where(low, swap_halves(a), b)
        rows = chunk(c, 512)
        pre = times(points[:, rows], weight[...], 0, 0)
        s = sigmoid(pre)
        e = pre * s
        low_e = e.astype(BF16)
        table[rows, :] = low_e
        embedded[chunk(step * 4 + c, 512), :] = low_e
        slope[rows, :] = (s + e * (1.0 - s)).astype(BF16)
        return carry

    lax.fori_loop(0, 4, embed, 0, unroll=2)

    @pl.when(step == 3)
    def _():
        pick = lambda b, k: embedded[rows_of(source[b, k]), :]
        for h in range(SHOWN):
            row = gather_mix(coeffs, pick, G_SLOTS, shown[0, h])
            mesh[h * BLOCK : (h + 1) * BLOCK, :] = row.astype(BF16)
        pre = times(mesh[...], message[...])
        mine[...] = (pre * sigmoid(pre)).astype(BF16).reshape(SHOWN, BLOCK, WIDTH)


def mesh_body(source, embedded, coeffs, message, mesh, sent, slope_m):
    def mix(b, carry):
        pick = lambda b, k: embedded[rows_of(source[b, k]), :]
        mesh[rows_of(b), :] = gather_mix(coeffs, pick, G_SLOTS, b).astype(BF16)
        return carry

    lax.fori_loop(0, MESH_BLOCKS, mix, 0, unroll=2)

    def talk(c, carry):
        rows = chunk(c, 256)
        pre = times(mesh[rows, :], message[...])
        s = sigmoid(pre)
        e = pre * s
        sent[rows, :] = e.astype(BF16)
        slope_m[rows, :] = (s + e * (1.0 - s)).astype(BF16)
        return carry

    lax.fori_loop(0, MESH_ROWS // 256, talk, 0)


def extend(extended, sent, halos):
    extended[0:MESH_ROWS, :] = sent[...]
    for e in range(4):
        for h in range(SHOWN):
            at = MESH_ROWS + (e * SHOWN + h) * BLOCK
            extended[at : at + BLOCK, :] = halos[e][h]


def mix_mesh(coeffs, extended, source, aggregate):
    def mix(b, carry):
        pick = lambda b, k: extended[rows_of(source[b, k]), :]
        aggregate[rows_of(b), :] = gather_mix(coeffs, pick, M_SLOTS, b).astype(BF16)
        return carry

    lax.fori_loop(0, MESH_BLOCKS, mix, 0, unroll=2)


def forward_body(
    source, shown, sent, n0, n1, n2, n3, coeffs, mesh, up, message,
    aggregate, mesh_1, sent_1, slope_m, mine, extended,
):
    extend(extended, sent, (n0, n1, n2, n3))
    mix_mesh(coeffs, extended, source, aggregate)

    def step(c, carry):
        rows = chunk(c, 256)
        state = (mesh[rows, :].astype(F32) + times(aggregate[rows, :], up[...])).astype(BF16)
        mesh_1[rows, :] = state
        pre = times(state, message[...])
        s = sigmoid(pre)
        e = pre * s
        sent_1[rows, :] = e.astype(BF16)
        slope_m[rows, :] = (s + e * (1.0 - s)).astype(BF16)
        return carry

    lax.fori_loop(0, MESH_ROWS // 256, step, 0)
    for h in range(SHOWN):
        mine[h] = sent_1[rows_of(shown[0, h]), :]


def backward_body(
    source, shown, own, r0, r1, r2, r3, slope_m, cot, message, up, coeffs,
    grad_pre, grad_1, own_0, h0, h1, h2, h3, table, lowered, grad_msg,
):
    grad_msg[...] = own[...].astype(F32)
    add_returned(own, (r0, r1, r2, r3), shown, grad_msg)

    def step(c, carry):
        rows = chunk(c, 256)
        gp = (grad_msg[rows, :] * slope_m[rows, :].astype(F32)).astype(BF16)
        grad_pre[rows, :] = gp
        g = cot[rows, :].astype(F32) + times(gp, message[...], 1, 1)
        grad_1[rows, :] = g
        lowered[rows, :] = times(g.astype(BF16), up[...], 1, 1).astype(BF16)
        return carry

    lax.fori_loop(0, MESH_ROWS // 256, step, 0)
    scatter_back(coeffs, lowered, source, table, M_SLOTS, EXTENDED)
    write_halo(table, own_0, (h0, h1, h2, h3))


def write_slabs(odd, keep, give, first, values):
    def write(out, column):
        for c in range(2):
            at = first + c * WIDTH
            slab = values[:, column + c * 128 : column + (c + 1) * 128]
            out[at : at + values.shape[0], :] = slab.astype(BF16)

    @pl.when(odd[0] == 0)
    def _():
        write(keep, 0)
        write(give, COLUMNS)

    @pl.when(odd[0] == 1)
    def _():
        write(keep, COLUMNS)
        write(give, 0)


def grads_body(
    odd, source, sent, n0, n1, n2, n3, coeffs, mesh, up, cot, aggregate_0, grad_1, grad_pre,
    mesh_out, keep, give, extended, aggregate,
):
    write_slabs(odd, keep, give, 0, times(aggregate_0[...], grad_1[...].astype(BF16), 0, 0))
    write_slabs(odd, keep, give, SLABS, times(mesh[...], grad_pre[...], 0, 0))
    extend(extended, sent, (n0, n1, n2, n3))
    mix_mesh(coeffs, extended, source, aggregate)

    def step(c, carry):
        rows = chunk(c, 256)
        update = times(aggregate[rows, :], up[...])
        mesh_out[rows, :] = (mesh[rows, :].astype(F32) + update).astype(BF16)
        return carry

    lax.fori_loop(0, MESH_ROWS // 256, step, 0)
    write_slabs(odd, keep, give, 2 * SLABS, times(aggregate[...], cot[...], 0, 0))


def final_body(
    odd, source, shown, own, r0, r1, r2, r3, slope_m, grad_1, message, mesh, coeffs, slope, points,
    keep, give, table, grad_pre, lowered, grad_msg, total,
):
    c = pl.program_id(0)

    @pl.when(c == 0)
    def _():
        grad_msg[...] = own[...].astype(F32)
        add_returned(own, (r0, r1, r2, r3), shown, grad_msg)

        def step(c, carry):
            rows = chunk(c, 256)
            gp = (grad_msg[rows, :] * slope_m[rows, :].astype(F32)).astype(BF16)
            grad_pre[rows, :] = gp
            lowered[rows, :] = (grad_1[rows, :] + times(gp, message[...], 1, 1)).astype(BF16)
            return carry

        lax.fori_loop(0, MESH_ROWS // 256, step, 0)
        scatter_back(coeffs, lowered, source, table, G_SLOTS, GRID_BLOCKS)
        write_slabs(odd, keep, give, 0, times(mesh[...], grad_pre[...], 0, 0))
        total[...] = jnp.zeros_like(total)

    def grid_step(i, carry):
        rows = chunk(i, 512)
        grad = table[pl.ds(c * 32 + i * 8, 8)].reshape(512, WIDTH).astype(BF16)
        grad = (grad.astype(F32) * slope[rows, :].astype(F32)).astype(BF16)
        total[0:CHAN, :] = total[0:CHAN, :] + times(points[:, rows], grad)
        return carry

    lax.fori_loop(0, 4, grid_step, 0)

    @pl.when(c == 3)
    def _():
        write_slabs(odd, keep, give, SLABS, total[...])


def pair_body(late, late_other, early, early_other, out):
    def one(i, carry):
        out[i, 0:LATE, :] = (late[i].astype(F32) + late_other[i].astype(F32)).astype(BF16)
        out[i, LATE:PART, :] = (early[i].astype(F32) + early_other[i].astype(F32)).astype(BF16)
        return carry

    lax.fori_loop(0, DEVICES, one, 0, unroll=8)


def sum_body(parts, out):
    zero = jnp.zeros((PART, 128), F32)

    def add(i, carry):
        return carry[0] + parts[2 * i].astype(F32), carry[1] + parts[2 * i + 1].astype(F32)

    even, odd = lax.fori_loop(0, DEVICES // 2, add, (zero, zero), unroll=8)
    even, odd = even.astype(BF16), odd.astype(BF16)

    def one(i, carry):
        out[2 * i] = even
        out[2 * i + 1] = odd
        return carry

    lax.fori_loop(0, DEVICES // 2, one, 0, unroll=8)


def unpack_body(odd, own, other, d_embed, ms_grad, up_grad):
    def place(values, outs, column, first):
        begin = 0
        for out in outs:
            for c in range(2):
                low = max(first, begin)
                high = min(first + values.shape[0], begin + out.shape[0])
                if low < high:
                    at = column + c * 128
                    out[low - begin : high - begin, at : at + 128] = values[low - first : high - first]
                begin += WIDTH

    def unpack(parts, column):
        for q in range(DEVICES):
            values = parts[q].astype(F32)
            place(values[0:LATE], (ms_grad.at[0], d_embed), column, q * LATE)
            place(values[LATE:PART], (up_grad.at[0], ms_grad.at[1], up_grad.at[1]), column, q * EARLY)

    @pl.when(odd[0] == 0)
    def _():
        unpack(own, 0)
        unpack(other, COLUMNS)

    @pl.when(odd[0] == 1)
    def _():
        unpack(other, 0)
        unpack(own, COLUMNS)


def shift(value, axis, steps):
    count = lax.axis_size(axis)
    return lax.ppermute(value, axis, [(i, (i + steps) % count) for i in range(count)])


def show(mine):
    return (shift(mine, "wide", 1), shift(mine, "wide", -1), shift(mine, "narrow", 1), shift(mine, "narrow", -1))


def give_back(h0, h1, h2, h3):
    return (shift(h0, "wide", -1), shift(h1, "wide", 1), shift(h2, "narrow", -1), shift(h3, "narrow", 1))


def swap_cores(value):
    return lax.ppermute(value, "narrow", [(i, i ^ 1) for i in range(lax.axis_size("narrow"))])


def exchange(parts):
    return lax.all_to_all(parts, AXES, split_axis=0, concat_axis=0, tiled=True)


def on_device(
    grid_feat, grid_send, w_embed, g2m_src, g2m_coef, mesh_src, mesh_coef, halo_send,
    message_weight, update_weight, cotangent,
):
    rows_bf16 = ((MESH_ROWS, WIDTH), BF16)
    rows_f32 = ((MESH_ROWS, WIDTH), F32)
    halo = ((SHOWN, BLOCK, WIDTH), BF16)
    mesh_scratch = pltpu.VMEM((MESH_ROWS, WIDTH), BF16)
    mesh_scratch32 = pltpu.VMEM((MESH_ROWS, WIDTH), F32)
    extended_scratch = pltpu.VMEM((EXTENDED * BLOCK, WIDTH), BF16)
    table_scratch = pltpu.VMEM((EXTENDED, BLOCK, WIDTH), F32)
    odd = (lax.axis_index("narrow") % 2).reshape(1).astype(jnp.int32)
    w_m = (message_weight[0], message_weight[1])
    w_u = (update_weight[0], update_weight[1])

    packed = pl.pallas_call(
        pack_body,
        grid=(4,),
        out_shape=jax.ShapeDtypeStruct((GRID_BLOCKS, PACKED, 2 * BLOCK), BF16),
        in_specs=[SM, pl.BlockSpec((CHAN, GRID_ROWS // 4), lambda i: (0, i))],
        out_specs=pl.BlockSpec((GRID_BLOCKS, PACKED, 2 * BLOCK), lambda i: (0, 0, 0)),
        scratch_shapes=[pltpu.SMEM((GRID_BLOCKS,), jnp.int32)],
        compiler_params=pltpu.CompilerParams(vmem_limit_bytes=56 * MIB),
        cost_estimate=pl.CostEstimate(flops=0, bytes_accessed=8 * MIB, transcendentals=0),
    )(grid_send, grid_feat.T)
    packed, cotangent = lax.optimization_barrier((packed, cotangent))
    received = exchange(packed)

    g_mix = g2m_coef.transpose(0, 2, 1, 3).reshape(MESH_BLOCKS, BLOCK, G_SLOTS * BLOCK)
    m_mix = mesh_coef.transpose(0, 2, 1, 3).reshape(MESH_BLOCKS, BLOCK, M_SLOTS * BLOCK)

    own_1, *halos = kernel_call(
        early_back_body, [rows_f32] + [halo] * 4, [SM] + [VM] * 3, [table_scratch, mesh_scratch],
        flops=2 * 10**9, moved=8 * MIB, limit=20,
    )(mesh_src, cotangent, w_u[1], m_mix)
    returned_1 = give_back(*halos)

    received, g_mix, m_mix, own_1, *returned_1 = lax.optimization_barrier(
        (received, g_mix, m_mix, own_1, *returned_1)
    )
    whole = lambda *shape: pl.BlockSpec(shape, lambda i: (0,) * len(shape))
    points, slope, embedded, mine_0 = pl.pallas_call(
        encode_body,
        grid=(4,),
        out_shape=[
            pltpu.HBM((CHAN, GRID_ROWS), BF16),
            pltpu.HBM((GRID_ROWS, WIDTH), BF16),
            jax.ShapeDtypeStruct((GRID_ROWS, WIDTH), BF16),
            jax.ShapeDtypeStruct((SHOWN, BLOCK, WIDTH), BF16),
        ],
        in_specs=[
            SM, SM,
            pl.BlockSpec((32, PACKED, 2 * BLOCK), lambda i: (i, 0, 0)),
            VM, VM, VM,
        ],
        out_specs=[
            pl.BlockSpec((CHAN, 2048), lambda i: (0, i)),
            pl.BlockSpec((2048, WIDTH), lambda i: (i, 0)),
            pl.BlockSpec((2048, WIDTH), lambda i: (i, 0)),
            whole(SHOWN, BLOCK, WIDTH),
        ],
        scratch_shapes=[
            pltpu.VMEM((GRID_ROWS, WIDTH), BF16), pltpu.VMEM((SHOWN * BLOCK, WIDTH), BF16)
        ],
        compiler_params=pltpu.CompilerParams(vmem_limit_bytes=28 * MIB),
        cost_estimate=pl.CostEstimate(flops=4 * 10**9, bytes_accessed=26 * MIB, transcendentals=0),
    )(g2m_src, halo_send, received, w_embed, g_mix, w_m[0])
    shown_0 = show(mine_0)
    mesh_0, sent_0, slope_0 = kernel_call(
        mesh_body, [rows_bf16] * 3, [SM] + [VM] * 3, flops=2 * 10**9, moved=12 * MIB, limit=24,
    )(g2m_src, embedded, g_mix, w_m[0])

    aggregate_0, mesh_1, sent_1, slope_1, mine_1 = kernel_call(
        forward_body, [rows_bf16] * 4 + [halo], [SM, SM] + [VM] * 9, [extended_scratch],
        flops=2 * 10**9, moved=10 * MIB, limit=20,
    )(mesh_src, halo_send, sent_0, *shown_0, m_mix, mesh_0, w_u[0], w_m[1])
    shown_1 = show(mine_1)

    grad_pre_1, grad_1, own_0, *halos = kernel_call(
        backward_body, [rows_bf16, rows_f32, rows_f32] + [halo] * 4, [SM, SM] + [VM] * 10,
        [table_scratch, mesh_scratch, mesh_scratch32], flops=2 * 10**9, moved=16 * MIB, limit=28,
    )(mesh_src, halo_send, own_1, *returned_1, slope_1, cotangent, w_m[1], w_u[0], m_mix)
    returned_0 = give_back(*halos)

    mesh_out, early, early_give = kernel_call(
        grads_body, [rows_bf16, ((3 * SLABS, 128), BF16), ((3 * SLABS, 128), BF16)],
        [SM, SM] + [VM] * 12, [extended_scratch, mesh_scratch], flops=4 * 10**9, moved=14 * MIB,
        limit=24,
    )(
        odd, mesh_src, sent_1, *shown_1, m_mix, mesh_1, w_u[1], cotangent, aggregate_0, grad_1,
        grad_pre_1,
    )
    early_other = swap_cores(early_give)

    late, late_give = pl.pallas_call(
        final_body,
        grid=(4,),
        out_shape=[jax.ShapeDtypeStruct((2 * SLABS, 128), BF16)] * 2,
        in_specs=[
            SM, SM, SM, *[VM] * 10,
            pl.BlockSpec((2048, WIDTH), lambda i: (i, 0)),
            pl.BlockSpec((CHAN, 2048), lambda i: (0, i)),
        ],
        out_specs=[VM, VM],
        scratch_shapes=[
            pltpu.VMEM((GRID_BLOCKS, BLOCK, WIDTH), F32),
            mesh_scratch, mesh_scratch, mesh_scratch32,
            pltpu.VMEM((WIDTH, WIDTH), F32),
        ],
        compiler_params=pltpu.CompilerParams(vmem_limit_bytes=34 * MIB),
        cost_estimate=pl.CostEstimate(flops=4 * 10**9, bytes_accessed=24 * MIB, transcendentals=0),
    )(
        odd, g2m_src, halo_send, own_0, *returned_0, slope_0, grad_1, w_m[0], mesh_0, g_mix, slope,
        points,
    )
    late_other = swap_cores(late_give)

    by_device = lambda part: part.reshape(DEVICES, -1, 128)
    pairs = kernel_call(
        pair_body, [((DEVICES, PART, 128), BF16)], [VM] * 4, moved=6 * MIB, limit=16
    )(by_device(late), by_device(late_other), by_device(early), by_device(early_other))[0]
    totals = kernel_call(
        sum_body, [((DEVICES, PART, 128), BF16)], [VM], moved=3 * MIB, limit=16
    )(exchange(pairs))[0]
    own = exchange(totals)
    d_embed, ms_grad, up_grad = kernel_call(
        unpack_body,
        [((CHAN, WIDTH), F32), ((2, WIDTH, WIDTH), F32), ((2, WIDTH, WIDTH), F32)],
        [SM, VM, VM], moved=7 * MIB, limit=24,
    )(odd, own, swap_cores(own))
    return mesh_out, d_embed, ms_grad, up_grad


def solution(mesh):
    split = P(AXES, None)
    return jax.shard_map(
        on_device,
        mesh=mesh,
        in_specs=(
            split, split, P(), split, P(AXES, None, None, None), split, P(AXES, None, None, None),
            split, P(), P(), split,
        ),
        out_specs=(split, P(), P(), P()),
        check_vma=False,
    )
```

```python
import jax
import jax.numpy as jnp
from jax import lax
from jax.experimental import pallas as pl
from jax.experimental.pallas import tpu as pltpu
from jax.sharding import Mesh, PartitionSpec as P

CHAN = 227
WIDTH = 512
BLOCK = 64
GRID_BLOCKS = 128
MESH_BLOCKS = 16
SHOWN = 4
G_SLOTS = 8
M_SLOTS = 6
EXTENDED = MESH_BLOCKS + 4 * SHOWN
MESH_ROWS = MESH_BLOCKS * BLOCK
GRID_ROWS = GRID_BLOCKS * BLOCK
SPLIT = 112
PACKED = CHAN - SPLIT
DEVICES = 128
CHIPS = DEVICES // 2
COLUMNS = WIDTH // 2
SLABS = 2 * WIDTH
TAIL = 256
EARLY = 3 * SLABS // CHIPS
LATE = (SLABS + 2 * TAIL) // CHIPS
PART = EARLY + LATE
NARROW = ("x", "core")
AXES = ("wide", "x", "core")
CHIP_AXES = ("wide", "x")
BF16 = jnp.bfloat16
F32 = jnp.float32
MIB = 1 << 20

VM = pl.BlockSpec(memory_space=pltpu.VMEM)
SM = pl.BlockSpec(memory_space=pltpu.SMEM)


def kernel_call(body, outs, ins, scratch=(), flops=0, moved=0, limit=56):
    return pl.pallas_call(
        body,
        out_shape=[jax.ShapeDtypeStruct(shape, dtype) for shape, dtype in outs],
        in_specs=ins,
        out_specs=[VM] * len(outs),
        scratch_shapes=list(scratch),
        compiler_params=pltpu.CompilerParams(vmem_limit_bytes=limit * MIB),
        cost_estimate=pl.CostEstimate(flops=flops, bytes_accessed=moved, transcendentals=0),
    )


def times(left, right, left_dim=1, right_dim=0):
    return lax.dot_general(
        left, right, (((left_dim,), (right_dim,)), ((), ())), preferred_element_type=F32
    )


def sigmoid(values):
    return 0.5 * jnp.tanh(0.5 * values) + 0.5


def silu_grad(values):
    s = sigmoid(values)
    return s * (1.0 + values * (1.0 - s))


def swap_halves(tile):
    return pltpu.roll(tile, BLOCK, 1)


def low_lanes(rows):
    return lax.broadcasted_iota(jnp.int32, (rows, 2 * BLOCK), 1) < BLOCK


def rows_of(block):
    return pl.ds(pl.multiple_of(block * BLOCK, BLOCK), BLOCK)


def chunk(step, size):
    return pl.ds(pl.multiple_of(step * size, size), size)


def pack_body(send, features, out, target):
    step = pl.program_id(0)

    @pl.when(step == 0)
    def _():
        def invert(j, carry):
            target[send[0, j]] = j
            return carry

        lax.fori_loop(0, GRID_BLOCKS, invert, 0, unroll=8)

    low = low_lanes(PACKED)

    def pair(i, carry):
        lanes = chunk(i, 2 * BLOCK)
        first = features[0:PACKED, lanes]
        second = features[SPLIT:CHAN, lanes]
        at = step * 32 + 2 * i
        out[target[at]] = jnp.where(low, first, swap_halves(second))
        out[target[at + 1]] = jnp.where(low, swap_halves(first), second)
        return carry

    lax.fori_loop(0, 16, pair, 0, unroll=4)


def scatter_back(coeffs, gradient, source, table, slots, blocks):
    def clear(i, carry):
        table[i] = jnp.zeros((BLOCK, WIDTH), F32)
        return carry

    lax.fori_loop(0, blocks, clear, 0, unroll=4)

    def one(b, carry):
        parts = times(coeffs[b], gradient[rows_of(b), :], 0, 0)
        for k in range(slots):
            at = source[b, k]
            table[at] = table[at] + parts[k * BLOCK : (k + 1) * BLOCK]
        return carry

    lax.fori_loop(0, MESH_BLOCKS, one, 0, unroll=2)


def gather_mix(coeffs, pick, slots, b):
    picked = jnp.concatenate([pick(b, k) for k in range(slots)], axis=0)
    return times(coeffs[b], picked)


def add_returned(own, returned, shown, take):
    for h in range(SHOWN):
        at = shown[0, h]
        extra = (returned[0][h].astype(F32) + returned[1][h].astype(F32)) + (
            returned[2][h].astype(F32) + returned[3][h].astype(F32)
        )
        take[rows_of(at), :] = take[rows_of(at), :] + extra


def write_halo(table, own, halos):
    for i in range(MESH_BLOCKS):
        own[i * BLOCK : (i + 1) * BLOCK, :] = table[i].astype(own.dtype)
    for e in range(4):
        for h in range(SHOWN):
            halos[e][h] = table[MESH_BLOCKS + e * SHOWN + h].astype(BF16)


def early_back_body(source, cot, up, coeffs, own, h0, h1, h2, h3, table, lowered):
    def step(c, carry):
        rows = chunk(c, 256)
        lowered[rows, :] = times(cot[rows, :], up[...], 1, 1).astype(BF16)
        return carry

    lax.fori_loop(0, MESH_ROWS // 256, step, 0, unroll=2)
    scatter_back(coeffs, lowered, source, table, M_SLOTS, EXTENDED)
    write_halo(table, own, (h0, h1, h2, h3))


def encode_body(
    source, shown, packed, weight, coeffs, message, points, slope, table, mine, embedded, mesh
):
    step = pl.program_id(0)
    low = low_lanes(PACKED)

    def embed(c, carry):
        for p in range(4):
            a = packed[c * 8 + 2 * p]
            b = packed[c * 8 + 2 * p + 1]
            lanes = pl.ds(pl.multiple_of(c * 512 + p * 128, 128), 128)
            points[0:SPLIT, lanes] = jnp.where(low, a, swap_halves(b))[0:SPLIT]
            points[SPLIT:CHAN, lanes] = jnp.where(low, swap_halves(a), b)
        rows = chunk(c, 512)
        pre = times(points[:, rows], weight[...], 0, 0)
        s = sigmoid(pre)
        e = pre * s
        low_e = e.astype(BF16)
        table[rows, :] = low_e
        embedded[chunk(step * 4 + c, 512), :] = low_e
        slope[rows, :] = (s + e * (1.0 - s)).astype(BF16)
        return carry

    lax.fori_loop(0, 4, embed, 0, unroll=4)

    @pl.when(step == 3)
    def _():
        pick = lambda b, k: embedded[rows_of(source[b, k]), :]
        for h in range(SHOWN):
            row = gather_mix(coeffs, pick, G_SLOTS, shown[0, h])
            mesh[h * BLOCK : (h + 1) * BLOCK, :] = row.astype(BF16)
        pre = times(mesh[...], message[...])
        mine[...] = (pre * sigmoid(pre)).astype(BF16).reshape(SHOWN, BLOCK, WIDTH)


def mesh_body(source, embedded, coeffs, message, mesh, sent, slope_m):
    def mix(b, carry):
        pick = lambda b, k: embedded[rows_of(source[b, k]), :]
        mesh[rows_of(b), :] = gather_mix(coeffs, pick, G_SLOTS, b).astype(BF16)
        return carry

    lax.fori_loop(0, MESH_BLOCKS, mix, 0, unroll=4)

    def talk(c, carry):
        rows = chunk(c, 256)
        pre = times(mesh[rows, :], message[...])
        s = sigmoid(pre)
        e = pre * s
        sent[rows, :] = e.astype(BF16)
        slope_m[rows, :] = (s + e * (1.0 - s)).astype(BF16)
        return carry

    lax.fori_loop(0, MESH_ROWS // 256, talk, 0)


def extend(extended, sent, halos):
    extended[0:MESH_ROWS, :] = sent[...]
    for e in range(4):
        for h in range(SHOWN):
            at = MESH_ROWS + (e * SHOWN + h) * BLOCK
            extended[at : at + BLOCK, :] = halos[e][h]


def mix_mesh(coeffs, extended, source, aggregate):
    def mix(b, carry):
        pick = lambda b, k: extended[rows_of(source[b, k]), :]
        aggregate[rows_of(b), :] = gather_mix(coeffs, pick, M_SLOTS, b).astype(BF16)
        return carry

    lax.fori_loop(0, MESH_BLOCKS, mix, 0, unroll=4)


def forward_body(
    source, shown, sent, n0, n1, n2, n3, coeffs, mesh, up, message,
    aggregate, mesh_1, sent_1, slope_m, mine, extended,
):
    extend(extended, sent, (n0, n1, n2, n3))
    mix_mesh(coeffs, extended, source, aggregate)

    def step(c, carry):
        rows = chunk(c, 256)
        state = (mesh[rows, :].astype(F32) + times(aggregate[rows, :], up[...])).astype(BF16)
        mesh_1[rows, :] = state
        pre = times(state, message[...])
        s = sigmoid(pre)
        e = pre * s
        sent_1[rows, :] = e.astype(BF16)
        slope_m[rows, :] = (s + e * (1.0 - s)).astype(BF16)
        return carry

    lax.fori_loop(0, MESH_ROWS // 256, step, 0, unroll=2)
    for h in range(SHOWN):
        mine[h] = sent_1[rows_of(shown[0, h]), :]


def backward_body(
    source, shown, own, r0, r1, r2, r3, slope_m, cot, message, up, coeffs,
    grad_pre, grad_1, own_0, h0, h1, h2, h3, table, lowered, grad_msg,
):
    grad_msg[...] = own[...].astype(F32)
    add_returned(own, (r0, r1, r2, r3), shown, grad_msg)

    def step(c, carry):
        rows = chunk(c, 256)
        gp = (grad_msg[rows, :] * slope_m[rows, :].astype(F32)).astype(BF16)
        grad_pre[rows, :] = gp
        g = cot[rows, :].astype(F32) + times(gp, message[...], 1, 1)
        grad_1[rows, :] = g
        lowered[rows, :] = times(g.astype(BF16), up[...], 1, 1).astype(BF16)
        return carry

    lax.fori_loop(0, MESH_ROWS // 256, step, 0, unroll=2)
    scatter_back(coeffs, lowered, source, table, M_SLOTS, EXTENDED)
    write_halo(table, own_0, (h0, h1, h2, h3))


def write_slabs(odd, keep, give, first, values):
    def write(out, column):
        for c in range(2):
            at = first + c * values.shape[0]
            slab = values[:, column + c * 128 : column + (c + 1) * 128]
            out[at : at + values.shape[0], :] = slab.astype(BF16)

    @pl.when(odd[0] == 0)
    def _():
        write(keep, 0)
        write(give, COLUMNS)

    @pl.when(odd[0] == 1)
    def _():
        write(keep, COLUMNS)
        write(give, 0)


def grads_body(
    odd, source, sent, n0, n1, n2, n3, coeffs, mesh, up, cot, aggregate_0, grad_1, grad_pre,
    mesh_out, keep, give, extended, aggregate,
):
    write_slabs(odd, keep, give, 0, times(aggregate_0[...], grad_1[...].astype(BF16), 0, 0))
    write_slabs(odd, keep, give, SLABS, times(mesh[...], grad_pre[...], 0, 0))
    extend(extended, sent, (n0, n1, n2, n3))
    mix_mesh(coeffs, extended, source, aggregate)

    def step(c, carry):
        rows = chunk(c, 256)
        update = times(aggregate[rows, :], up[...])
        mesh_out[rows, :] = (mesh[rows, :].astype(F32) + update).astype(BF16)
        return carry

    lax.fori_loop(0, MESH_ROWS // 256, step, 0, unroll=2)
    write_slabs(odd, keep, give, 2 * SLABS, times(aggregate[...], cot[...], 0, 0))


def final_body(
    odd, source, shown, own, r0, r1, r2, r3, slope_m, grad_1, message, mesh, coeffs, slope, points,
    keep, give, table, grad_pre, lowered, grad_msg, total,
):
    c = pl.program_id(0)

    @pl.when(c == 0)
    def _():
        grad_msg[...] = own[...].astype(F32)
        add_returned(own, (r0, r1, r2, r3), shown, grad_msg)

        def step(c, carry):
            rows = chunk(c, 256)
            gp = (grad_msg[rows, :] * slope_m[rows, :].astype(F32)).astype(BF16)
            grad_pre[rows, :] = gp
            lowered[rows, :] = (grad_1[rows, :] + times(gp, message[...], 1, 1)).astype(BF16)
            return carry

        lax.fori_loop(0, MESH_ROWS // 256, step, 0, unroll=2)
        scatter_back(coeffs, lowered, source, table, G_SLOTS, GRID_BLOCKS)
        write_slabs(odd, keep, give, 0, times(mesh[...], grad_pre[...], 0, 0))
        total[...] = jnp.zeros_like(total)

    def grid_step(i, carry):
        rows = chunk(i, 512)
        grad = table[pl.ds(c * 32 + i * 8, 8)].reshape(512, WIDTH).astype(BF16)
        grad = (grad.astype(F32) * slope[rows, :].astype(F32)).astype(BF16)
        total[0:CHAN, :] = total[0:CHAN, :] + times(points[:, rows], grad)
        return carry

    lax.fori_loop(0, 4, grid_step, 0, unroll=4)

    @pl.when(c == 3)
    def _():
        write_slabs(odd, keep, give, SLABS, total[...])


def pair_body(early, early_other, late, late_other, out):
    def one(i, carry):
        out[i, 0:EARLY, :] = (early[i].astype(F32) + early_other[i].astype(F32)).astype(BF16)
        out[i, EARLY:PART, :] = (late[i].astype(F32) + late_other[i].astype(F32)).astype(BF16)
        return carry

    lax.fori_loop(0, CHIPS, one, 0, unroll=8)


def sum_body(parts, out):
    def add(i, carry):
        return carry + parts[i].astype(F32)

    total = lax.fori_loop(0, CHIPS, add, jnp.zeros((PART, 128), F32), unroll=8).astype(BF16)

    def one(i, carry):
        out[i] = total
        return carry

    lax.fori_loop(0, CHIPS, one, 0, unroll=8)


def unpack_body(odd, own, other, d_embed, ms_grad, up_grad):
    def place(values, outs, column, first):
        begin = 0
        for out, rows in outs:
            for c in range(2):
                low = max(first, begin)
                high = min(first + values.shape[0], begin + out.shape[0])
                if low < high:
                    at = column + c * 128
                    out[low - begin : high - begin, at : at + 128] = values[low - first : high - first]
                begin += rows

    def unpack(parts, column):
        early = ((up_grad.at[0], WIDTH), (ms_grad.at[1], WIDTH), (up_grad.at[1], WIDTH))
        late = ((ms_grad.at[0], WIDTH), (d_embed, TAIL))
        for q in range(CHIPS):
            values = parts[q].astype(F32)
            place(values[0:EARLY], early, column, q * EARLY)
            place(values[EARLY:PART], late, column, q * LATE)

    @pl.when(odd[0] == 0)
    def _():
        unpack(own, 0)
        unpack(other, COLUMNS)

    @pl.when(odd[0] == 1)
    def _():
        unpack(other, 0)
        unpack(own, COLUMNS)


def shift(value, axis, steps):
    axis = NARROW if axis == "narrow" else axis
    count = lax.axis_size(axis)
    return lax.ppermute(value, axis, [(i, (i + steps) % count) for i in range(count)])


def show(mine):
    return (shift(mine, "wide", 1), shift(mine, "wide", -1), shift(mine, "narrow", 1), shift(mine, "narrow", -1))


def give_back(h0, h1, h2, h3):
    return (shift(h0, "wide", -1), shift(h1, "wide", 1), shift(h2, "narrow", -1), shift(h3, "narrow", 1))


def swap_cores(value):
    return lax.ppermute(value, "core", [(0, 1), (1, 0)])


def exchange(parts, axes):
    return lax.all_to_all(parts, axes, split_axis=0, concat_axis=0, tiled=True)


def on_device(
    grid_feat, grid_send, w_embed, g2m_src, g2m_coef, mesh_src, mesh_coef, halo_send,
    message_weight, update_weight, cotangent,
):
    rows_bf16 = ((MESH_ROWS, WIDTH), BF16)
    rows_f32 = ((MESH_ROWS, WIDTH), F32)
    halo = ((SHOWN, BLOCK, WIDTH), BF16)
    mesh_scratch = pltpu.VMEM((MESH_ROWS, WIDTH), BF16)
    mesh_scratch32 = pltpu.VMEM((MESH_ROWS, WIDTH), F32)
    extended_scratch = pltpu.VMEM((EXTENDED * BLOCK, WIDTH), BF16)
    table_scratch = pltpu.VMEM((EXTENDED, BLOCK, WIDTH), F32)
    odd = lax.axis_index("core").reshape(1).astype(jnp.int32)
    w_m = (message_weight[0], message_weight[1])
    w_u = (update_weight[0], update_weight[1])

    packed = pl.pallas_call(
        pack_body,
        grid=(4,),
        out_shape=jax.ShapeDtypeStruct((GRID_BLOCKS, PACKED, 2 * BLOCK), BF16),
        in_specs=[SM, pl.BlockSpec((CHAN, GRID_ROWS // 4), lambda i: (0, i))],
        out_specs=pl.BlockSpec((GRID_BLOCKS, PACKED, 2 * BLOCK), lambda i: (0, 0, 0)),
        scratch_shapes=[pltpu.SMEM((GRID_BLOCKS,), jnp.int32)],
        compiler_params=pltpu.CompilerParams(vmem_limit_bytes=56 * MIB),
        cost_estimate=pl.CostEstimate(flops=0, bytes_accessed=8 * MIB, transcendentals=0),
    )(grid_send, grid_feat.T)
    packed, cotangent, odd = lax.optimization_barrier((packed, cotangent, odd))
    received = exchange(packed, AXES)

    g_mix = g2m_coef.transpose(0, 2, 1, 3).reshape(MESH_BLOCKS, BLOCK, G_SLOTS * BLOCK)
    m_mix = mesh_coef.transpose(0, 2, 1, 3).reshape(MESH_BLOCKS, BLOCK, M_SLOTS * BLOCK)

    own_1, *halos = kernel_call(
        early_back_body, [rows_f32] + [halo] * 4, [SM] + [VM] * 3, [table_scratch, mesh_scratch],
        flops=2 * 10**9, moved=8 * MIB, limit=20,
    )(mesh_src, cotangent, w_u[1], m_mix)
    returned_1 = give_back(*halos)

    received, g_mix, m_mix, own_1, *returned_1 = lax.optimization_barrier(
        (received, g_mix, m_mix, own_1, *returned_1)
    )
    whole = lambda *shape: pl.BlockSpec(shape, lambda i: (0,) * len(shape))
    points, slope, embedded, mine_0 = pl.pallas_call(
        encode_body,
        grid=(4,),
        out_shape=[
            pltpu.HBM((CHAN, GRID_ROWS), BF16),
            pltpu.HBM((GRID_ROWS, WIDTH), BF16),
            jax.ShapeDtypeStruct((GRID_ROWS, WIDTH), BF16),
            jax.ShapeDtypeStruct((SHOWN, BLOCK, WIDTH), BF16),
        ],
        in_specs=[
            SM, SM,
            pl.BlockSpec((32, PACKED, 2 * BLOCK), lambda i: (i, 0, 0)),
            VM, VM, VM,
        ],
        out_specs=[
            pl.BlockSpec((CHAN, 2048), lambda i: (0, i)),
            pl.BlockSpec((2048, WIDTH), lambda i: (i, 0)),
            pl.BlockSpec((2048, WIDTH), lambda i: (i, 0)),
            whole(SHOWN, BLOCK, WIDTH),
        ],
        scratch_shapes=[
            pltpu.VMEM((GRID_ROWS, WIDTH), BF16), pltpu.VMEM((SHOWN * BLOCK, WIDTH), BF16)
        ],
        compiler_params=pltpu.CompilerParams(vmem_limit_bytes=28 * MIB),
        cost_estimate=pl.CostEstimate(flops=4 * 10**9, bytes_accessed=26 * MIB, transcendentals=0),
    )(g2m_src, halo_send, received, w_embed, g_mix, w_m[0])
    shown_0 = show(mine_0)
    mesh_0, sent_0, slope_0 = kernel_call(
        mesh_body, [rows_bf16] * 3, [SM] + [VM] * 3, flops=2 * 10**9, moved=12 * MIB, limit=24,
    )(g2m_src, embedded, g_mix, w_m[0])

    aggregate_0, mesh_1, sent_1, slope_1, mine_1 = kernel_call(
        forward_body, [rows_bf16] * 4 + [halo], [SM, SM] + [VM] * 9, [extended_scratch],
        flops=2 * 10**9, moved=10 * MIB, limit=20,
    )(mesh_src, halo_send, sent_0, *shown_0, m_mix, mesh_0, w_u[0], w_m[1])
    shown_1 = show(mine_1)

    grad_pre_1, grad_1, own_0, *halos = kernel_call(
        backward_body, [rows_bf16, rows_f32, rows_f32] + [halo] * 4, [SM, SM] + [VM] * 10,
        [table_scratch, mesh_scratch, mesh_scratch32], flops=2 * 10**9, moved=16 * MIB, limit=28,
    )(mesh_src, halo_send, own_1, *returned_1, slope_1, cotangent, w_m[1], w_u[0], m_mix)
    returned_0 = give_back(*halos)

    mesh_out, early, early_give = kernel_call(
        grads_body, [rows_bf16, ((3 * SLABS, 128), BF16), ((3 * SLABS, 128), BF16)],
        [SM, SM] + [VM] * 12, [extended_scratch, mesh_scratch], flops=4 * 10**9, moved=14 * MIB,
        limit=24,
    )(
        odd, mesh_src, sent_1, *shown_1, m_mix, mesh_1, w_u[1], cotangent, aggregate_0, grad_1,
        grad_pre_1,
    )
    early_other = swap_cores(early_give)

    late, late_give = pl.pallas_call(
        final_body,
        grid=(4,),
        out_shape=[jax.ShapeDtypeStruct((SLABS + 2 * TAIL, 128), BF16)] * 2,
        in_specs=[
            SM, SM, SM, *[VM] * 10,
            pl.BlockSpec((2048, WIDTH), lambda i: (i, 0)),
            pl.BlockSpec((CHAN, 2048), lambda i: (0, i)),
        ],
        out_specs=[VM, VM],
        scratch_shapes=[
            pltpu.VMEM((GRID_BLOCKS, BLOCK, WIDTH), F32),
            mesh_scratch, mesh_scratch, mesh_scratch32,
            pltpu.VMEM((TAIL, WIDTH), F32),
        ],
        compiler_params=pltpu.CompilerParams(vmem_limit_bytes=34 * MIB),
        cost_estimate=pl.CostEstimate(flops=4 * 10**9, bytes_accessed=24 * MIB, transcendentals=0),
    )(
        odd, g2m_src, halo_send, own_0, *returned_0, slope_0, grad_1, w_m[0], mesh_0, g_mix, slope,
        points,
    )
    late_other = swap_cores(late_give)

    by_chip = lambda part: part.reshape(CHIPS, -1, 128)
    pairs = kernel_call(
        pair_body, [((CHIPS, PART, 128), BF16)], [VM] * 4, moved=6 * MIB, limit=16
    )(by_chip(early), by_chip(early_other), by_chip(late), by_chip(late_other))[0]
    totals = kernel_call(
        sum_body, [((CHIPS, PART, 128), BF16)], [VM], moved=3 * MIB, limit=16
    )(exchange(pairs, CHIP_AXES))[0]
    own = exchange(totals, CHIP_AXES)
    d_embed, ms_grad, up_grad = kernel_call(
        unpack_body,
        [((CHAN, WIDTH), F32), ((2, WIDTH, WIDTH), F32), ((2, WIDTH, WIDTH), F32)],
        [SM, VM, VM], moved=7 * MIB, limit=24,
    )(odd, own, swap_cores(own))
    return mesh_out, d_embed, ms_grad, up_grad


def solution(mesh):
    by_core = Mesh(mesh.devices.reshape(16, 4, 2), AXES)
    split = P(AXES, None)
    return jax.shard_map(
        on_device,
        mesh=by_core,
        in_specs=(
            split, split, P(), split, P(AXES, None, None, None), split, P(AXES, None, None, None),
            split, P(), P(), split,
        ),
        out_specs=(split, P(), P(), P()),
        check_vma=False,
    )
```

```python
import jax
import jax.numpy as jnp
from jax import lax
from jax.experimental import pallas as pl
from jax.experimental.pallas import tpu as pltpu
from jax.sharding import Mesh, PartitionSpec as P

CHAN = 227
WIDTH = 512
BLOCK = 64
GRID_BLOCKS = 128
MESH_BLOCKS = 16
SHOWN = 4
G_SLOTS = 8
M_SLOTS = 6
EXTENDED = MESH_BLOCKS + 4 * SHOWN
MESH_ROWS = MESH_BLOCKS * BLOCK
GRID_ROWS = GRID_BLOCKS * BLOCK
SPLIT = 112
PACKED = CHAN - SPLIT
DEVICES = 128
CHIPS = DEVICES // 2
COLUMNS = WIDTH // 2
SLABS = 2 * WIDTH
TAIL = 256
EARLY = 3 * SLABS // CHIPS
LATE = (SLABS + 2 * TAIL) // CHIPS
PART = EARLY + LATE
NARROW = ("x", "core")
AXES = ("wide", "x", "core")
CHIP_AXES = ("wide", "x")
BF16 = jnp.bfloat16
F32 = jnp.float32
MIB = 1 << 20

VM = pl.BlockSpec(memory_space=pltpu.VMEM)
SM = pl.BlockSpec(memory_space=pltpu.SMEM)


def kernel_call(body, outs, ins, scratch=(), flops=0, moved=0, limit=56):
    return pl.pallas_call(
        body,
        out_shape=[jax.ShapeDtypeStruct(shape, dtype) for shape, dtype in outs],
        in_specs=ins,
        out_specs=[VM] * len(outs),
        scratch_shapes=list(scratch),
        compiler_params=pltpu.CompilerParams(vmem_limit_bytes=limit * MIB),
        cost_estimate=pl.CostEstimate(flops=flops, bytes_accessed=moved, transcendentals=0),
    )


def times(left, right, left_dim=1, right_dim=0):
    return lax.dot_general(
        left, right, (((left_dim,), (right_dim,)), ((), ())), preferred_element_type=F32
    )


def sigmoid(values):
    return 0.5 * jnp.tanh(0.5 * values) + 0.5


def silu_grad(values):
    s = sigmoid(values)
    return s * (1.0 + values * (1.0 - s))


def swap_halves(tile):
    return pltpu.roll(tile, BLOCK, 1)


def low_lanes(rows):
    return lax.broadcasted_iota(jnp.int32, (rows, 2 * BLOCK), 1) < BLOCK


def rows_of(block):
    return pl.ds(pl.multiple_of(block * BLOCK, BLOCK), BLOCK)


def chunk(step, size):
    return pl.ds(pl.multiple_of(step * size, size), size)


def pack_body(send, features, out, target):
    step = pl.program_id(0)

    @pl.when(step == 0)
    def _():
        def invert(j, carry):
            target[send[0, j]] = j
            return carry

        lax.fori_loop(0, GRID_BLOCKS, invert, 0, unroll=8)

    low = low_lanes(PACKED)

    def pair(i, carry):
        lanes = chunk(i, 2 * BLOCK)
        first = features[0:PACKED, lanes]
        second = features[SPLIT:CHAN, lanes]
        at = step * 32 + 2 * i
        out[target[at]] = jnp.where(low, first, swap_halves(second))
        out[target[at + 1]] = jnp.where(low, swap_halves(first), second)
        return carry

    lax.fori_loop(0, 16, pair, 0, unroll=8)


def scatter_back(coeffs, gradient, source, table, slots, blocks):
    def clear(i, carry):
        table[i] = jnp.zeros((BLOCK, WIDTH), F32)
        return carry

    lax.fori_loop(0, blocks, clear, 0, unroll=16)

    def one(b, carry):
        parts = times(coeffs[b], gradient[rows_of(b), :], 0, 0)
        for k in range(slots):
            at = source[b, k]
            table[at] = table[at] + parts[k * BLOCK : (k + 1) * BLOCK]
        return carry

    lax.fori_loop(0, MESH_BLOCKS, one, 0, unroll=4)


def gather_mix(coeffs, pick, slots, b):
    picked = jnp.concatenate([pick(b, k) for k in range(slots)], axis=0)
    return times(coeffs[b], picked)


def add_returned(own, returned, shown, take):
    for h in range(SHOWN):
        at = shown[0, h]
        extra = (returned[0][h].astype(F32) + returned[1][h].astype(F32)) + (
            returned[2][h].astype(F32) + returned[3][h].astype(F32)
        )
        take[rows_of(at), :] = take[rows_of(at), :] + extra


def write_halo(table, own, halos):
    for i in range(MESH_BLOCKS):
        own[i * BLOCK : (i + 1) * BLOCK, :] = table[i].astype(own.dtype)
    for e in range(4):
        for h in range(SHOWN):
            halos[e][h] = table[MESH_BLOCKS + e * SHOWN + h].astype(BF16)


def early_back_body(source, cot, up, coeffs, own, h0, h1, h2, h3, table, lowered):
    def step(c, carry):
        rows = chunk(c, 256)
        lowered[rows, :] = times(cot[rows, :], up[...], 1, 1).astype(BF16)
        return carry

    lax.fori_loop(0, MESH_ROWS // 256, step, 0, unroll=4)
    scatter_back(coeffs, lowered, source, table, M_SLOTS, EXTENDED)
    write_halo(table, own, (h0, h1, h2, h3))


def encode_body(
    source, shown, packed, weight, coeffs, message, points, slope, table, mine, embedded, mesh
):
    step = pl.program_id(0)
    low = low_lanes(PACKED)

    def embed(c, carry):
        for p in range(4):
            a = packed[c * 8 + 2 * p]
            b = packed[c * 8 + 2 * p + 1]
            lanes = pl.ds(pl.multiple_of(c * 512 + p * 128, 128), 128)
            points[0:SPLIT, lanes] = jnp.where(low, a, swap_halves(b))[0:SPLIT]
            points[SPLIT:CHAN, lanes] = jnp.where(low, swap_halves(a), b)
        rows = chunk(c, 512)
        pre = times(points[:, rows], weight[...], 0, 0)
        s = sigmoid(pre)
        e = pre * s
        low_e = e.astype(BF16)
        table[rows, :] = low_e
        embedded[chunk(step * 4 + c, 512), :] = low_e
        slope[rows, :] = (s + e * (1.0 - s)).astype(BF16)
        return carry

    lax.fori_loop(0, 4, embed, 0, unroll=4)

    @pl.when(step == 3)
    def _():
        pick = lambda b, k: embedded[rows_of(source[b, k]), :]
        for h in range(SHOWN):
            row = gather_mix(coeffs, pick, G_SLOTS, shown[0, h])
            mesh[h * BLOCK : (h + 1) * BLOCK, :] = row.astype(BF16)
        pre = times(mesh[...], message[...])
        mine[...] = (pre * sigmoid(pre)).astype(BF16).reshape(SHOWN, BLOCK, WIDTH)


def mesh_body(source, embedded, coeffs, message, mesh, sent, slope_m):
    def mix(b, carry):
        pick = lambda b, k: embedded[rows_of(source[b, k]), :]
        mesh[rows_of(b), :] = gather_mix(coeffs, pick, G_SLOTS, b).astype(BF16)
        return carry

    lax.fori_loop(0, MESH_BLOCKS, mix, 0, unroll=8)

    def talk(c, carry):
        rows = chunk(c, 256)
        pre = times(mesh[rows, :], message[...])
        s = sigmoid(pre)
        e = pre * s
        sent[rows, :] = e.astype(BF16)
        slope_m[rows, :] = (s + e * (1.0 - s)).astype(BF16)
        return carry

    lax.fori_loop(0, MESH_ROWS // 256, talk, 0, unroll=4)


def extend(extended, sent, halos):
    extended[0:MESH_ROWS, :] = sent[...]
    for e in range(4):
        for h in range(SHOWN):
            at = MESH_ROWS + (e * SHOWN + h) * BLOCK
            extended[at : at + BLOCK, :] = halos[e][h]


def mix_mesh(coeffs, extended, source, aggregate):
    def mix(b, carry):
        pick = lambda b, k: extended[rows_of(source[b, k]), :]
        aggregate[rows_of(b), :] = gather_mix(coeffs, pick, M_SLOTS, b).astype(BF16)
        return carry

    lax.fori_loop(0, MESH_BLOCKS, mix, 0, unroll=8)


def forward_body(
    source, shown, sent, n0, n1, n2, n3, coeffs, mesh, up, message,
    aggregate, mesh_1, sent_1, slope_m, mine, extended,
):
    extend(extended, sent, (n0, n1, n2, n3))
    mix_mesh(coeffs, extended, source, aggregate)

    def step(c, carry):
        rows = chunk(c, 256)
        state = (mesh[rows, :].astype(F32) + times(aggregate[rows, :], up[...])).astype(BF16)
        mesh_1[rows, :] = state
        pre = times(state, message[...])
        s = sigmoid(pre)
        e = pre * s
        sent_1[rows, :] = e.astype(BF16)
        slope_m[rows, :] = (s + e * (1.0 - s)).astype(BF16)
        return carry

    lax.fori_loop(0, MESH_ROWS // 256, step, 0, unroll=4)
    for h in range(SHOWN):
        mine[h] = sent_1[rows_of(shown[0, h]), :]


def backward_body(
    source, shown, own, r0, r1, r2, r3, slope_m, cot, message, up, coeffs,
    grad_pre, grad_1, own_0, h0, h1, h2, h3, table, lowered, grad_msg,
):
    grad_msg[...] = own[...].astype(F32)
    add_returned(own, (r0, r1, r2, r3), shown, grad_msg)

    def step(c, carry):
        rows = chunk(c, 256)
        gp = (grad_msg[rows, :] * slope_m[rows, :].astype(F32)).astype(BF16)
        grad_pre[rows, :] = gp
        g = cot[rows, :].astype(F32) + times(gp, message[...], 1, 1)
        grad_1[rows, :] = g
        lowered[rows, :] = times(g.astype(BF16), up[...], 1, 1).astype(BF16)
        return carry

    lax.fori_loop(0, MESH_ROWS // 256, step, 0, unroll=4)
    scatter_back(coeffs, lowered, source, table, M_SLOTS, EXTENDED)
    write_halo(table, own_0, (h0, h1, h2, h3))


def write_slabs(odd, keep, give, first, values):
    def write(out, column):
        for c in range(2):
            at = first + c * values.shape[0]
            slab = values[:, column + c * 128 : column + (c + 1) * 128]
            out[at : at + values.shape[0], :] = slab.astype(BF16)

    @pl.when(odd[0] == 0)
    def _():
        write(keep, 0)
        write(give, COLUMNS)

    @pl.when(odd[0] == 1)
    def _():
        write(keep, COLUMNS)
        write(give, 0)


def grads_body(
    odd, source, sent, n0, n1, n2, n3, coeffs, mesh, up, cot, aggregate_0, grad_1, grad_pre,
    mesh_out, keep, give, extended, aggregate,
):
    write_slabs(odd, keep, give, 0, times(aggregate_0[...], grad_1[...].astype(BF16), 0, 0))
    write_slabs(odd, keep, give, SLABS, times(mesh[...], grad_pre[...], 0, 0))
    extend(extended, sent, (n0, n1, n2, n3))
    mix_mesh(coeffs, extended, source, aggregate)

    def step(c, carry):
        rows = chunk(c, 256)
        update = times(aggregate[rows, :], up[...])
        mesh_out[rows, :] = (mesh[rows, :].astype(F32) + update).astype(BF16)
        return carry

    lax.fori_loop(0, MESH_ROWS // 256, step, 0, unroll=4)
    write_slabs(odd, keep, give, 2 * SLABS, times(aggregate[...], cot[...], 0, 0))


def final_body(
    odd, source, shown, own, r0, r1, r2, r3, slope_m, grad_1, message, mesh, coeffs, slope, points,
    keep, give, table, grad_pre, lowered, grad_msg, total,
):
    c = pl.program_id(0)

    @pl.when(c == 0)
    def _():
        grad_msg[...] = own[...].astype(F32)
        add_returned(own, (r0, r1, r2, r3), shown, grad_msg)

        def step(c, carry):
            rows = chunk(c, 256)
            gp = (grad_msg[rows, :] * slope_m[rows, :].astype(F32)).astype(BF16)
            grad_pre[rows, :] = gp
            lowered[rows, :] = (grad_1[rows, :] + times(gp, message[...], 1, 1)).astype(BF16)
            return carry

        lax.fori_loop(0, MESH_ROWS // 256, step, 0, unroll=4)
        scatter_back(coeffs, lowered, source, table, G_SLOTS, GRID_BLOCKS)
        write_slabs(odd, keep, give, 0, times(mesh[...], grad_pre[...], 0, 0))
        total[...] = jnp.zeros_like(total)

    def grid_step(i, carry):
        rows = chunk(i, 512)
        grad = table[pl.ds(c * 32 + i * 8, 8)].reshape(512, WIDTH).astype(BF16)
        grad = (grad.astype(F32) * slope[rows, :].astype(F32)).astype(BF16)
        total[0:CHAN, :] = total[0:CHAN, :] + times(points[:, rows], grad)
        return carry

    lax.fori_loop(0, 4, grid_step, 0, unroll=4)

    @pl.when(c == 3)
    def _():
        write_slabs(odd, keep, give, SLABS, total[...])


def pair_body(early, early_other, late, late_other, out):
    def one(i, carry):
        out[i, 0:EARLY, :] = (early[i].astype(F32) + early_other[i].astype(F32)).astype(BF16)
        out[i, EARLY:PART, :] = (late[i].astype(F32) + late_other[i].astype(F32)).astype(BF16)
        return carry

    lax.fori_loop(0, CHIPS, one, 0, unroll=8)


def sum_body(parts, out):
    def add(i, carry):
        return carry + parts[i].astype(F32)

    total = lax.fori_loop(0, CHIPS, add, jnp.zeros((PART, 128), F32), unroll=8).astype(BF16)

    def one(i, carry):
        out[i] = total
        return carry

    lax.fori_loop(0, CHIPS, one, 0, unroll=8)


def unpack_body(odd, own, other, d_embed, ms_grad, up_grad):
    def place(values, outs, column, first):
        begin = 0
        for out, rows in outs:
            for c in range(2):
                low = max(first, begin)
                high = min(first + values.shape[0], begin + out.shape[0])
                if low < high:
                    at = column + c * 128
                    out[low - begin : high - begin, at : at + 128] = values[low - first : high - first]
                begin += rows

    def unpack(parts, column):
        early = ((up_grad.at[0], WIDTH), (ms_grad.at[1], WIDTH), (up_grad.at[1], WIDTH))
        late = ((ms_grad.at[0], WIDTH), (d_embed, TAIL))
        for q in range(CHIPS):
            values = parts[q].astype(F32)
            place(values[0:EARLY], early, column, q * EARLY)
            place(values[EARLY:PART], late, column, q * LATE)

    @pl.when(odd[0] == 0)
    def _():
        unpack(own, 0)
        unpack(other, COLUMNS)

    @pl.when(odd[0] == 1)
    def _():
        unpack(other, 0)
        unpack(own, COLUMNS)


def shift(value, axis, steps):
    axis = NARROW if axis == "narrow" else axis
    count = lax.axis_size(axis)
    return lax.ppermute(value, axis, [(i, (i + steps) % count) for i in range(count)])


def show(mine):
    return (shift(mine, "wide", 1), shift(mine, "wide", -1), shift(mine, "narrow", 1), shift(mine, "narrow", -1))


def give_back(h0, h1, h2, h3):
    return (shift(h0, "wide", -1), shift(h1, "wide", 1), shift(h2, "narrow", -1), shift(h3, "narrow", 1))


def swap_cores(value):
    return lax.ppermute(value, "core", [(0, 1), (1, 0)])


def exchange(parts, axes):
    return lax.all_to_all(parts, axes, split_axis=0, concat_axis=0, tiled=True)


def on_device(
    grid_feat, grid_send, w_embed, g2m_src, g2m_coef, mesh_src, mesh_coef, halo_send,
    message_weight, update_weight, cotangent,
):
    rows_bf16 = ((MESH_ROWS, WIDTH), BF16)
    rows_f32 = ((MESH_ROWS, WIDTH), F32)
    halo = ((SHOWN, BLOCK, WIDTH), BF16)
    mesh_scratch = pltpu.VMEM((MESH_ROWS, WIDTH), BF16)
    mesh_scratch32 = pltpu.VMEM((MESH_ROWS, WIDTH), F32)
    extended_scratch = pltpu.VMEM((EXTENDED * BLOCK, WIDTH), BF16)
    table_scratch = pltpu.VMEM((EXTENDED, BLOCK, WIDTH), F32)
    odd = lax.axis_index("core").reshape(1).astype(jnp.int32)
    w_m = (message_weight[0], message_weight[1])
    w_u = (update_weight[0], update_weight[1])

    packed = pl.pallas_call(
        pack_body,
        grid=(4,),
        out_shape=jax.ShapeDtypeStruct((GRID_BLOCKS, PACKED, 2 * BLOCK), BF16),
        in_specs=[SM, pl.BlockSpec((CHAN, GRID_ROWS // 4), lambda i: (0, i))],
        out_specs=pl.BlockSpec((GRID_BLOCKS, PACKED, 2 * BLOCK), lambda i: (0, 0, 0)),
        scratch_shapes=[pltpu.SMEM((GRID_BLOCKS,), jnp.int32)],
        compiler_params=pltpu.CompilerParams(vmem_limit_bytes=56 * MIB),
        cost_estimate=pl.CostEstimate(flops=0, bytes_accessed=8 * MIB, transcendentals=0),
    )(grid_send, grid_feat.T)
    packed, cotangent, odd = lax.optimization_barrier((packed, cotangent, odd))
    received = exchange(packed, AXES)

    g_mix = g2m_coef.transpose(0, 2, 1, 3).reshape(MESH_BLOCKS, BLOCK, G_SLOTS * BLOCK)
    m_mix = mesh_coef.transpose(0, 2, 1, 3).reshape(MESH_BLOCKS, BLOCK, M_SLOTS * BLOCK)

    own_1, *halos = kernel_call(
        early_back_body, [rows_f32] + [halo] * 4, [SM] + [VM] * 3, [table_scratch, mesh_scratch],
        flops=2 * 10**9, moved=8 * MIB, limit=20,
    )(mesh_src, cotangent, w_u[1], m_mix)
    returned_1 = give_back(*halos)

    received, g_mix, m_mix, own_1 = lax.optimization_barrier((received, g_mix, m_mix, own_1))
    whole = lambda *shape: pl.BlockSpec(shape, lambda i: (0,) * len(shape))
    points, slope, embedded, mine_0 = pl.pallas_call(
        encode_body,
        grid=(4,),
        out_shape=[
            pltpu.HBM((CHAN, GRID_ROWS), BF16),
            pltpu.HBM((GRID_ROWS, WIDTH), BF16),
            jax.ShapeDtypeStruct((GRID_ROWS, WIDTH), BF16),
            jax.ShapeDtypeStruct((SHOWN, BLOCK, WIDTH), BF16),
        ],
        in_specs=[
            SM, SM,
            pl.BlockSpec((32, PACKED, 2 * BLOCK), lambda i: (i, 0, 0)),
            VM, VM, VM,
        ],
        out_specs=[
            pl.BlockSpec((CHAN, 2048), lambda i: (0, i)),
            pl.BlockSpec((2048, WIDTH), lambda i: (i, 0)),
            pl.BlockSpec((2048, WIDTH), lambda i: (i, 0)),
            whole(SHOWN, BLOCK, WIDTH),
        ],
        scratch_shapes=[
            pltpu.VMEM((GRID_ROWS, WIDTH), BF16), pltpu.VMEM((SHOWN * BLOCK, WIDTH), BF16)
        ],
        compiler_params=pltpu.CompilerParams(vmem_limit_bytes=28 * MIB),
        cost_estimate=pl.CostEstimate(flops=4 * 10**9, bytes_accessed=26 * MIB, transcendentals=0),
    )(g2m_src, halo_send, received, w_embed, g_mix, w_m[0])
    shown_0 = show(mine_0)
    mesh_0, sent_0, slope_0 = kernel_call(
        mesh_body, [rows_bf16] * 3, [SM] + [VM] * 3, flops=2 * 10**9, moved=12 * MIB, limit=24,
    )(g2m_src, embedded, g_mix, w_m[0])

    aggregate_0, mesh_1, sent_1, slope_1, mine_1 = kernel_call(
        forward_body, [rows_bf16] * 4 + [halo], [SM, SM] + [VM] * 9, [extended_scratch],
        flops=2 * 10**9, moved=10 * MIB, limit=20,
    )(mesh_src, halo_send, sent_0, *shown_0, m_mix, mesh_0, w_u[0], w_m[1])
    shown_1 = show(mine_1)

    grad_pre_1, grad_1, own_0, *halos = kernel_call(
        backward_body, [rows_bf16, rows_f32, rows_f32] + [halo] * 4, [SM, SM] + [VM] * 10,
        [table_scratch, mesh_scratch, mesh_scratch32], flops=2 * 10**9, moved=16 * MIB, limit=28,
    )(mesh_src, halo_send, own_1, *returned_1, slope_1, cotangent, w_m[1], w_u[0], m_mix)
    returned_0 = give_back(*halos)

    mesh_out, early, early_give = kernel_call(
        grads_body, [rows_bf16, ((3 * SLABS, 128), BF16), ((3 * SLABS, 128), BF16)],
        [SM, SM] + [VM] * 12, [extended_scratch, mesh_scratch], flops=4 * 10**9, moved=14 * MIB,
        limit=24,
    )(
        odd, mesh_src, sent_1, *shown_1, m_mix, mesh_1, w_u[1], cotangent, aggregate_0, grad_1,
        grad_pre_1,
    )
    early_other = swap_cores(early_give)

    late, late_give = pl.pallas_call(
        final_body,
        grid=(4,),
        out_shape=[jax.ShapeDtypeStruct((SLABS + 2 * TAIL, 128), BF16)] * 2,
        in_specs=[
            SM, SM, SM, *[VM] * 10,
            pl.BlockSpec((2048, WIDTH), lambda i: (i, 0)),
            pl.BlockSpec((CHAN, 2048), lambda i: (0, i)),
        ],
        out_specs=[VM, VM],
        scratch_shapes=[
            pltpu.VMEM((GRID_BLOCKS, BLOCK, WIDTH), F32),
            mesh_scratch, mesh_scratch, mesh_scratch32,
            pltpu.VMEM((TAIL, WIDTH), F32),
        ],
        compiler_params=pltpu.CompilerParams(vmem_limit_bytes=34 * MIB),
        cost_estimate=pl.CostEstimate(flops=4 * 10**9, bytes_accessed=24 * MIB, transcendentals=0),
    )(
        odd, g2m_src, halo_send, own_0, *returned_0, slope_0, grad_1, w_m[0], mesh_0, g_mix, slope,
        points,
    )
    late_other = swap_cores(late_give)

    by_chip = lambda part: part.reshape(CHIPS, -1, 128)
    pairs = kernel_call(
        pair_body, [((CHIPS, PART, 128), BF16)], [VM] * 4, moved=6 * MIB, limit=16
    )(by_chip(early), by_chip(early_other), by_chip(late), by_chip(late_other))[0]
    totals = kernel_call(
        sum_body, [((CHIPS, PART, 128), BF16)], [VM], moved=3 * MIB, limit=16
    )(exchange(pairs, CHIP_AXES))[0]
    own = exchange(totals, CHIP_AXES)
    d_embed, ms_grad, up_grad = kernel_call(
        unpack_body,
        [((CHAN, WIDTH), F32), ((2, WIDTH, WIDTH), F32), ((2, WIDTH, WIDTH), F32)],
        [SM, VM, VM], moved=7 * MIB, limit=24,
    )(odd, own, swap_cores(own))
    return mesh_out, d_embed, ms_grad, up_grad


def solution(mesh):
    by_core = Mesh(mesh.devices.reshape(16, 4, 2), AXES)
    split = P(AXES, None)
    return jax.shard_map(
        on_device,
        mesh=by_core,
        in_specs=(
            split, split, P(), split, P(AXES, None, None, None), split, P(AXES, None, None, None),
            split, P(), P(), split,
        ),
        out_specs=(split, P(), P(), P()),
        check_vma=False,
    )
```

```python
import jax
import jax.numpy as jnp
from jax import lax
from jax.experimental import pallas as pl
from jax.experimental.pallas import tpu as pltpu
from jax.sharding import Mesh, PartitionSpec as P

CHAN = 227
WIDTH = 512
BLOCK = 64
GRID_BLOCKS = 128
MESH_BLOCKS = 16
SHOWN = 4
G_SLOTS = 8
M_SLOTS = 6
EXTENDED = MESH_BLOCKS + 4 * SHOWN
MESH_ROWS = MESH_BLOCKS * BLOCK
GRID_ROWS = GRID_BLOCKS * BLOCK
SPLIT = 112
PACKED = CHAN - SPLIT
DEVICES = 128
CHIPS = DEVICES // 2
COLUMNS = WIDTH // 2
SLABS = 2 * WIDTH
TAIL = 256
EARLY = 3 * SLABS // CHIPS
LATE = (SLABS + 2 * TAIL) // CHIPS
PART = EARLY + LATE
NARROW = ("x", "core")
AXES = ("wide", "x", "core")
CHIP_AXES = ("wide", "x")
BF16 = jnp.bfloat16
F32 = jnp.float32
MIB = 1 << 20

VM = pl.BlockSpec(memory_space=pltpu.VMEM)
SM = pl.BlockSpec(memory_space=pltpu.SMEM)


def kernel_call(body, outs, ins, scratch=(), flops=0, moved=0, limit=56):
    return pl.pallas_call(
        body,
        out_shape=[jax.ShapeDtypeStruct(shape, dtype) for shape, dtype in outs],
        in_specs=ins,
        out_specs=[VM] * len(outs),
        scratch_shapes=list(scratch),
        compiler_params=pltpu.CompilerParams(vmem_limit_bytes=limit * MIB),
        cost_estimate=pl.CostEstimate(flops=flops, bytes_accessed=moved, transcendentals=0),
    )


def times(left, right, left_dim=1, right_dim=0):
    return lax.dot_general(
        left, right, (((left_dim,), (right_dim,)), ((), ())), preferred_element_type=F32
    )


def sigmoid(values):
    return 0.5 * jnp.tanh(0.5 * values) + 0.5


def silu_grad(values):
    s = sigmoid(values)
    return s * (1.0 + values * (1.0 - s))


def swap_halves(tile):
    return pltpu.roll(tile, BLOCK, 1)


def low_lanes(rows):
    return lax.broadcasted_iota(jnp.int32, (rows, 2 * BLOCK), 1) < BLOCK


def rows_of(block):
    return pl.ds(pl.multiple_of(block * BLOCK, BLOCK), BLOCK)


def chunk(step, size):
    return pl.ds(pl.multiple_of(step * size, size), size)


def pack_body(send, features, out, target):
    step = pl.program_id(0)

    @pl.when(step == 0)
    def _():
        def invert(j, carry):
            target[send[0, j]] = j
            return carry

        lax.fori_loop(0, GRID_BLOCKS, invert, 0, unroll=8)

    low = low_lanes(PACKED)

    def pair(i, carry):
        lanes = chunk(i, 2 * BLOCK)
        first = features[0:PACKED, lanes]
        second = features[SPLIT:CHAN, lanes]
        at = step * 32 + 2 * i
        out[target[at]] = jnp.where(low, first, swap_halves(second))
        out[target[at + 1]] = jnp.where(low, swap_halves(first), second)
        return carry

    lax.fori_loop(0, 16, pair, 0, unroll=8)


def scatter_back(coeffs, gradient, source, table, slots, blocks):
    def clear(i, carry):
        table[i] = jnp.zeros((BLOCK, WIDTH), F32)
        return carry

    lax.fori_loop(0, blocks, clear, 0, unroll=16)

    def one(b, carry):
        parts = times(coeffs[b], gradient[rows_of(b), :], 0, 0)
        for k in range(slots):
            at = source[b, k]
            table[at] = table[at] + parts[k * BLOCK : (k + 1) * BLOCK]
        return carry

    lax.fori_loop(0, MESH_BLOCKS, one, 0, unroll=4)


def gather_mix(coeffs, pick, slots, b):
    picked = jnp.concatenate([pick(b, k) for k in range(slots)], axis=0)
    return times(coeffs[b], picked)


def add_returned(own, returned, shown, take):
    for h in range(SHOWN):
        at = shown[0, h]
        extra = (returned[0][h].astype(F32) + returned[1][h].astype(F32)) + (
            returned[2][h].astype(F32) + returned[3][h].astype(F32)
        )
        take[rows_of(at), :] = take[rows_of(at), :] + extra


def write_halo(table, own, halos):
    for i in range(MESH_BLOCKS):
        own[i * BLOCK : (i + 1) * BLOCK, :] = table[i].astype(own.dtype)
    for e in range(4):
        for h in range(SHOWN):
            halos[e][h] = table[MESH_BLOCKS + e * SHOWN + h].astype(BF16)


def early_back_body(source, cot, up, coeffs, own, h0, h1, h2, h3, table, lowered):
    def step(c, carry):
        rows = chunk(c, 256)
        lowered[rows, :] = times(cot[rows, :], up[...], 1, 1).astype(BF16)
        return carry

    lax.fori_loop(0, MESH_ROWS // 256, step, 0, unroll=4)
    scatter_back(coeffs, lowered, source, table, M_SLOTS, EXTENDED)
    write_halo(table, own, (h0, h1, h2, h3))


def encode_body(
    source, shown, packed, weight, coeffs, message, points, slope, table, mine, embedded, mesh
):
    step = pl.program_id(0)
    low = low_lanes(PACKED)

    def embed(c, carry):
        for p in range(4):
            a = packed[c * 8 + 2 * p]
            b = packed[c * 8 + 2 * p + 1]
            lanes = pl.ds(pl.multiple_of(c * 512 + p * 128, 128), 128)
            points[0:SPLIT, lanes] = jnp.where(low, a, swap_halves(b))[0:SPLIT]
            points[SPLIT:CHAN, lanes] = jnp.where(low, swap_halves(a), b)
        rows = chunk(c, 512)
        pre = times(points[:, rows], weight[...], 0, 0)
        s = sigmoid(pre)
        e = pre * s
        low_e = e.astype(BF16)
        table[rows, :] = low_e
        embedded[chunk(step * 4 + c, 512), :] = low_e
        slope[rows, :] = (s + e * (1.0 - s)).astype(BF16)
        return carry

    lax.fori_loop(0, 4, embed, 0, unroll=4)

    @pl.when(step == 3)
    def _():
        pick = lambda b, k: embedded[rows_of(source[b, k]), :]
        for h in range(SHOWN):
            row = gather_mix(coeffs, pick, G_SLOTS, shown[0, h])
            mesh[h * BLOCK : (h + 1) * BLOCK, :] = row.astype(BF16)
        pre = times(mesh[...], message[...])
        mine[...] = (pre * sigmoid(pre)).astype(BF16).reshape(SHOWN, BLOCK, WIDTH)


def mesh_body(source, embedded, coeffs, message, mesh, sent, slope_m):
    def mix(b, carry):
        pick = lambda b, k: embedded[rows_of(source[b, k]), :]
        mesh[rows_of(b), :] = gather_mix(coeffs, pick, G_SLOTS, b).astype(BF16)
        return carry

    lax.fori_loop(0, MESH_BLOCKS, mix, 0, unroll=8)

    def talk(c, carry):
        rows = chunk(c, 256)
        pre = times(mesh[rows, :], message[...])
        s = sigmoid(pre)
        e = pre * s
        sent[rows, :] = e.astype(BF16)
        slope_m[rows, :] = (s + e * (1.0 - s)).astype(BF16)
        return carry

    lax.fori_loop(0, MESH_ROWS // 256, talk, 0, unroll=4)


def extend(extended, sent, halos):
    extended[0:MESH_ROWS, :] = sent[...]
    for e in range(4):
        for h in range(SHOWN):
            at = MESH_ROWS + (e * SHOWN + h) * BLOCK
            extended[at : at + BLOCK, :] = halos[e][h]


def mix_mesh(coeffs, extended, source, aggregate):
    def mix(b, carry):
        pick = lambda b, k: extended[rows_of(source[b, k]), :]
        aggregate[rows_of(b), :] = gather_mix(coeffs, pick, M_SLOTS, b).astype(BF16)
        return carry

    lax.fori_loop(0, MESH_BLOCKS, mix, 0, unroll=8)


def forward_body(
    source, shown, sent, n0, n1, n2, n3, coeffs, mesh, up, message,
    aggregate, mesh_1, sent_1, slope_m, mine, extended,
):
    extend(extended, sent, (n0, n1, n2, n3))
    mix_mesh(coeffs, extended, source, aggregate)

    def step(c, carry):
        rows = chunk(c, 256)
        state = (mesh[rows, :].astype(F32) + times(aggregate[rows, :], up[...])).astype(BF16)
        mesh_1[rows, :] = state
        pre = times(state, message[...])
        s = sigmoid(pre)
        e = pre * s
        sent_1[rows, :] = e.astype(BF16)
        slope_m[rows, :] = (s + e * (1.0 - s)).astype(BF16)
        return carry

    lax.fori_loop(0, MESH_ROWS // 256, step, 0, unroll=4)
    for h in range(SHOWN):
        mine[h] = sent_1[rows_of(shown[0, h]), :]


def backward_body(
    source, shown, own, r0, r1, r2, r3, slope_m, cot, message, up, coeffs,
    grad_pre, grad_1, own_0, h0, h1, h2, h3, table, lowered, grad_msg,
):
    grad_msg[...] = own[...].astype(F32)
    add_returned(own, (r0, r1, r2, r3), shown, grad_msg)

    def step(c, carry):
        rows = chunk(c, 256)
        gp = (grad_msg[rows, :] * slope_m[rows, :].astype(F32)).astype(BF16)
        grad_pre[rows, :] = gp
        g = cot[rows, :].astype(F32) + times(gp, message[...], 1, 1)
        grad_1[rows, :] = g
        lowered[rows, :] = times(g.astype(BF16), up[...], 1, 1).astype(BF16)
        return carry

    lax.fori_loop(0, MESH_ROWS // 256, step, 0, unroll=4)
    scatter_back(coeffs, lowered, source, table, M_SLOTS, EXTENDED)
    write_halo(table, own_0, (h0, h1, h2, h3))


def write_slabs(odd, keep, give, first, values):
    def write(out, column):
        for c in range(2):
            at = first + c * values.shape[0]
            slab = values[:, column + c * 128 : column + (c + 1) * 128]
            out[at : at + values.shape[0], :] = slab.astype(BF16)

    @pl.when(odd[0] == 0)
    def _():
        write(keep, 0)
        write(give, COLUMNS)

    @pl.when(odd[0] == 1)
    def _():
        write(keep, COLUMNS)
        write(give, 0)


def grads_body(
    odd, source, sent, n0, n1, n2, n3, coeffs, mesh, up, cot, aggregate_0, grad_1, grad_pre,
    mesh_out, keep, give, extended, aggregate,
):
    write_slabs(odd, keep, give, 0, times(aggregate_0[...], grad_1[...].astype(BF16), 0, 0))
    write_slabs(odd, keep, give, SLABS, times(mesh[...], grad_pre[...], 0, 0))
    extend(extended, sent, (n0, n1, n2, n3))
    mix_mesh(coeffs, extended, source, aggregate)

    def step(c, carry):
        rows = chunk(c, 256)
        update = times(aggregate[rows, :], up[...])
        mesh_out[rows, :] = (mesh[rows, :].astype(F32) + update).astype(BF16)
        return carry

    lax.fori_loop(0, MESH_ROWS // 256, step, 0, unroll=4)
    write_slabs(odd, keep, give, 2 * SLABS, times(aggregate[...], cot[...], 0, 0))


def final_body(
    odd, source, shown, own, r0, r1, r2, r3, slope_m, grad_1, message, mesh, coeffs, slope, points,
    keep, give, table, grad_pre, lowered, grad_msg, total,
):
    c = pl.program_id(0)

    @pl.when(c == 0)
    def _():
        grad_msg[...] = own[...].astype(F32)
        add_returned(own, (r0, r1, r2, r3), shown, grad_msg)

        def step(c, carry):
            rows = chunk(c, 256)
            gp = (grad_msg[rows, :] * slope_m[rows, :].astype(F32)).astype(BF16)
            grad_pre[rows, :] = gp
            lowered[rows, :] = (grad_1[rows, :] + times(gp, message[...], 1, 1)).astype(BF16)
            return carry

        lax.fori_loop(0, MESH_ROWS // 256, step, 0, unroll=4)
        scatter_back(coeffs, lowered, source, table, G_SLOTS, GRID_BLOCKS)
        write_slabs(odd, keep, give, 0, times(mesh[...], grad_pre[...], 0, 0))
        total[...] = jnp.zeros_like(total)

    def grid_step(i, carry):
        rows = chunk(i, 512)
        grad = table[pl.ds(c * 32 + i * 8, 8)].reshape(512, WIDTH).astype(BF16)
        grad = (grad.astype(F32) * slope[rows, :].astype(F32)).astype(BF16)
        total[0:CHAN, :] = total[0:CHAN, :] + times(points[:, rows], grad)
        return carry

    lax.fori_loop(0, 4, grid_step, 0, unroll=4)

    @pl.when(c == 3)
    def _():
        write_slabs(odd, keep, give, SLABS, total[...])


def pair_body(early, early_other, late, late_other, out):
    def one(i, carry):
        out[i, 0:EARLY, :] = (early[i].astype(F32) + early_other[i].astype(F32)).astype(BF16)
        out[i, EARLY:PART, :] = (late[i].astype(F32) + late_other[i].astype(F32)).astype(BF16)
        return carry

    lax.fori_loop(0, CHIPS, one, 0, unroll=8)


def sum_body(parts, out):
    def add(i, carry):
        return carry + parts[i].astype(F32)

    total = lax.fori_loop(0, CHIPS, add, jnp.zeros((PART, 128), F32), unroll=8).astype(BF16)

    def one(i, carry):
        out[i] = total
        return carry

    lax.fori_loop(0, CHIPS, one, 0, unroll=8)


def unpack_body(odd, own, other, d_embed, ms_grad, up_grad):
    def place(values, outs, column, first):
        begin = 0
        for out, rows in outs:
            for c in range(2):
                low = max(first, begin)
                high = min(first + values.shape[0], begin + out.shape[0])
                if low < high:
                    at = column + c * 128
                    out[low - begin : high - begin, at : at + 128] = values[low - first : high - first]
                begin += rows

    def unpack(parts, column):
        early = ((up_grad.at[0], WIDTH), (ms_grad.at[1], WIDTH), (up_grad.at[1], WIDTH))
        late = ((ms_grad.at[0], WIDTH), (d_embed, TAIL))
        for q in range(CHIPS):
            values = parts[q].astype(F32)
            place(values[0:EARLY], early, column, q * EARLY)
            place(values[EARLY:PART], late, column, q * LATE)

    @pl.when(odd[0] == 0)
    def _():
        unpack(own, 0)
        unpack(other, COLUMNS)

    @pl.when(odd[0] == 1)
    def _():
        unpack(other, 0)
        unpack(own, COLUMNS)


def shift(value, axis, steps):
    axis = NARROW if axis == "narrow" else axis
    count = lax.axis_size(axis)
    return lax.ppermute(value, axis, [(i, (i + steps) % count) for i in range(count)])


def show(mine):
    return (shift(mine, "wide", 1), shift(mine, "wide", -1), shift(mine, "narrow", 1), shift(mine, "narrow", -1))


def give_back(h0, h1, h2, h3):
    return (shift(h0, "wide", -1), shift(h1, "wide", 1), shift(h2, "narrow", -1), shift(h3, "narrow", 1))


def swap_cores(value):
    return lax.ppermute(value, "core", [(0, 1), (1, 0)])


def exchange(parts, axes):
    return lax.all_to_all(parts, axes, split_axis=0, concat_axis=0, tiled=True)


def on_device(
    grid_feat, grid_send, w_embed, g2m_src, g2m_coef, mesh_src, mesh_coef, halo_send,
    message_weight, update_weight, cotangent,
):
    rows_bf16 = ((MESH_ROWS, WIDTH), BF16)
    rows_f32 = ((MESH_ROWS, WIDTH), F32)
    halo = ((SHOWN, BLOCK, WIDTH), BF16)
    mesh_scratch = pltpu.VMEM((MESH_ROWS, WIDTH), BF16)
    mesh_scratch32 = pltpu.VMEM((MESH_ROWS, WIDTH), F32)
    extended_scratch = pltpu.VMEM((EXTENDED * BLOCK, WIDTH), BF16)
    table_scratch = pltpu.VMEM((EXTENDED, BLOCK, WIDTH), F32)
    odd = lax.axis_index("core").reshape(1).astype(jnp.int32)
    w_m = (message_weight[0], message_weight[1])
    w_u = (update_weight[0], update_weight[1])

    packed = pl.pallas_call(
        pack_body,
        grid=(4,),
        out_shape=jax.ShapeDtypeStruct((GRID_BLOCKS, PACKED, 2 * BLOCK), BF16),
        in_specs=[SM, pl.BlockSpec((CHAN, GRID_ROWS // 4), lambda i: (0, i))],
        out_specs=pl.BlockSpec((GRID_BLOCKS, PACKED, 2 * BLOCK), lambda i: (0, 0, 0)),
        scratch_shapes=[pltpu.SMEM((GRID_BLOCKS,), jnp.int32)],
        compiler_params=pltpu.CompilerParams(vmem_limit_bytes=56 * MIB),
        cost_estimate=pl.CostEstimate(flops=0, bytes_accessed=8 * MIB, transcendentals=0),
    )(grid_send, grid_feat.T)
    packed, cotangent, odd = lax.optimization_barrier((packed, cotangent, odd))
    received = exchange(packed, AXES)

    g_mix = g2m_coef.transpose(0, 2, 1, 3).reshape(MESH_BLOCKS, BLOCK, G_SLOTS * BLOCK)
    m_mix = mesh_coef.transpose(0, 2, 1, 3).reshape(MESH_BLOCKS, BLOCK, M_SLOTS * BLOCK)

    own_1, *halos = kernel_call(
        early_back_body, [rows_f32] + [halo] * 4, [SM] + [VM] * 3, [table_scratch, mesh_scratch],
        flops=2 * 10**9, moved=8 * MIB, limit=20,
    )(mesh_src, cotangent, w_u[1], m_mix)
    returned_1 = give_back(*halos)

    received, g_mix, m_mix, *returned_1 = lax.optimization_barrier(
        (received, g_mix, m_mix, *returned_1)
    )
    whole = lambda *shape: pl.BlockSpec(shape, lambda i: (0,) * len(shape))
    points, slope, embedded, mine_0 = pl.pallas_call(
        encode_body,
        grid=(4,),
        out_shape=[
            pltpu.HBM((CHAN, GRID_ROWS), BF16),
            pltpu.HBM((GRID_ROWS, WIDTH), BF16),
            jax.ShapeDtypeStruct((GRID_ROWS, WIDTH), BF16),
            jax.ShapeDtypeStruct((SHOWN, BLOCK, WIDTH), BF16),
        ],
        in_specs=[
            SM, SM,
            pl.BlockSpec((32, PACKED, 2 * BLOCK), lambda i: (i, 0, 0)),
            VM, VM, VM,
        ],
        out_specs=[
            pl.BlockSpec((CHAN, 2048), lambda i: (0, i)),
            pl.BlockSpec((2048, WIDTH), lambda i: (i, 0)),
            pl.BlockSpec((2048, WIDTH), lambda i: (i, 0)),
            whole(SHOWN, BLOCK, WIDTH),
        ],
        scratch_shapes=[
            pltpu.VMEM((GRID_ROWS, WIDTH), BF16), pltpu.VMEM((SHOWN * BLOCK, WIDTH), BF16)
        ],
        compiler_params=pltpu.CompilerParams(vmem_limit_bytes=28 * MIB),
        cost_estimate=pl.CostEstimate(flops=4 * 10**9, bytes_accessed=26 * MIB, transcendentals=0),
    )(g2m_src, halo_send, received, w_embed, g_mix, w_m[0])
    shown_0 = show(mine_0)
    mesh_0, sent_0, slope_0 = kernel_call(
        mesh_body, [rows_bf16] * 3, [SM] + [VM] * 3, flops=2 * 10**9, moved=12 * MIB, limit=24,
    )(g2m_src, embedded, g_mix, w_m[0])

    aggregate_0, mesh_1, sent_1, slope_1, mine_1 = kernel_call(
        forward_body, [rows_bf16] * 4 + [halo], [SM, SM] + [VM] * 9, [extended_scratch],
        flops=2 * 10**9, moved=10 * MIB, limit=20,
    )(mesh_src, halo_send, sent_0, *shown_0, m_mix, mesh_0, w_u[0], w_m[1])
    shown_1 = show(mine_1)

    grad_pre_1, grad_1, own_0, *halos = kernel_call(
        backward_body, [rows_bf16, rows_f32, rows_f32] + [halo] * 4, [SM, SM] + [VM] * 10,
        [table_scratch, mesh_scratch, mesh_scratch32], flops=2 * 10**9, moved=16 * MIB, limit=28,
    )(mesh_src, halo_send, own_1, *returned_1, slope_1, cotangent, w_m[1], w_u[0], m_mix)
    returned_0 = give_back(*halos)

    mesh_out, early, early_give = kernel_call(
        grads_body, [rows_bf16, ((3 * SLABS, 128), BF16), ((3 * SLABS, 128), BF16)],
        [SM, SM] + [VM] * 12, [extended_scratch, mesh_scratch], flops=4 * 10**9, moved=14 * MIB,
        limit=24,
    )(
        odd, mesh_src, sent_1, *shown_1, m_mix, mesh_1, w_u[1], cotangent, aggregate_0, grad_1,
        grad_pre_1,
    )
    early_other = swap_cores(early_give)

    late, late_give = pl.pallas_call(
        final_body,
        grid=(4,),
        out_shape=[jax.ShapeDtypeStruct((SLABS + 2 * TAIL, 128), BF16)] * 2,
        in_specs=[
            SM, SM, SM, *[VM] * 10,
            pl.BlockSpec((2048, WIDTH), lambda i: (i, 0)),
            pl.BlockSpec((CHAN, 2048), lambda i: (0, i)),
        ],
        out_specs=[VM, VM],
        scratch_shapes=[
            pltpu.VMEM((GRID_BLOCKS, BLOCK, WIDTH), F32),
            mesh_scratch, mesh_scratch, mesh_scratch32,
            pltpu.VMEM((TAIL, WIDTH), F32),
        ],
        compiler_params=pltpu.CompilerParams(vmem_limit_bytes=34 * MIB),
        cost_estimate=pl.CostEstimate(flops=4 * 10**9, bytes_accessed=24 * MIB, transcendentals=0),
    )(
        odd, g2m_src, halo_send, own_0, *returned_0, slope_0, grad_1, w_m[0], mesh_0, g_mix, slope,
        points,
    )
    late_other = swap_cores(late_give)

    by_chip = lambda part: part.reshape(CHIPS, -1, 128)
    pairs = kernel_call(
        pair_body, [((CHIPS, PART, 128), BF16)], [VM] * 4, moved=6 * MIB, limit=16
    )(by_chip(early), by_chip(early_other), by_chip(late), by_chip(late_other))[0]
    totals = kernel_call(
        sum_body, [((CHIPS, PART, 128), BF16)], [VM], moved=3 * MIB, limit=16
    )(exchange(pairs, CHIP_AXES))[0]
    own = exchange(totals, CHIP_AXES)
    d_embed, ms_grad, up_grad = kernel_call(
        unpack_body,
        [((CHAN, WIDTH), F32), ((2, WIDTH, WIDTH), F32), ((2, WIDTH, WIDTH), F32)],
        [SM, VM, VM], moved=7 * MIB, limit=24,
    )(odd, own, swap_cores(own))
    return mesh_out, d_embed, ms_grad, up_grad


def solution(mesh):
    by_core = Mesh(mesh.devices.reshape(16, 4, 2), AXES)
    split = P(AXES, None)
    return jax.shard_map(
        on_device,
        mesh=by_core,
        in_specs=(
            split, split, P(), split, P(AXES, None, None, None), split, P(AXES, None, None, None),
            split, P(), P(), split,
        ),
        out_specs=(split, P(), P(), P()),
        check_vma=False,
    )
```

```python
import jax
import jax.numpy as jnp
from jax import lax
from jax.experimental import pallas as pl
from jax.experimental.pallas import tpu as pltpu
from jax.sharding import Mesh, PartitionSpec as P

CHAN = 227
WIDTH = 512
BLOCK = 64
GRID_BLOCKS = 128
MESH_BLOCKS = 16
SHOWN = 4
G_SLOTS = 8
M_SLOTS = 6
EXTENDED = MESH_BLOCKS + 4 * SHOWN
MESH_ROWS = MESH_BLOCKS * BLOCK
GRID_ROWS = GRID_BLOCKS * BLOCK
SPLIT = 112
PACKED = CHAN - SPLIT
DEVICES = 128
CHIPS = DEVICES // 2
COLUMNS = WIDTH // 2
SLABS = 2 * WIDTH
TAIL = 256
EARLY = 3 * SLABS // CHIPS
LATE = (SLABS + 2 * TAIL) // CHIPS
PART = EARLY + LATE
NARROW = ("x", "core")
AXES = ("wide", "x", "core")
CHIP_AXES = ("wide", "x")
BF16 = jnp.bfloat16
F32 = jnp.float32
MIB = 1 << 20

VM = pl.BlockSpec(memory_space=pltpu.VMEM)
SM = pl.BlockSpec(memory_space=pltpu.SMEM)


def kernel_call(body, outs, ins, scratch=(), flops=0, moved=0, limit=56):
    return pl.pallas_call(
        body,
        out_shape=[jax.ShapeDtypeStruct(shape, dtype) for shape, dtype in outs],
        in_specs=ins,
        out_specs=[VM] * len(outs),
        scratch_shapes=list(scratch),
        compiler_params=pltpu.CompilerParams(vmem_limit_bytes=limit * MIB),
        cost_estimate=pl.CostEstimate(flops=flops, bytes_accessed=moved, transcendentals=0),
    )


def times(left, right, left_dim=1, right_dim=0):
    return lax.dot_general(
        left, right, (((left_dim,), (right_dim,)), ((), ())), preferred_element_type=F32
    )


def sigmoid(values):
    return 0.5 * jnp.tanh(0.5 * values) + 0.5


def silu_grad(values):
    s = sigmoid(values)
    return s * (1.0 + values * (1.0 - s))


def swap_halves(tile):
    return pltpu.roll(tile, BLOCK, 1)


def low_lanes(rows):
    return lax.broadcasted_iota(jnp.int32, (rows, 2 * BLOCK), 1) < BLOCK


def rows_of(block):
    return pl.ds(pl.multiple_of(block * BLOCK, BLOCK), BLOCK)


def chunk(step, size):
    return pl.ds(pl.multiple_of(step * size, size), size)


def pack_body(send, features, out, target):
    step = pl.program_id(0)

    @pl.when(step == 0)
    def _():
        def invert(j, carry):
            target[send[0, j]] = j
            return carry

        lax.fori_loop(0, GRID_BLOCKS, invert, 0, unroll=8)

    low = low_lanes(PACKED)

    def pair(i, carry):
        lanes = chunk(i, 2 * BLOCK)
        first = features[0:PACKED, lanes]
        second = features[SPLIT:CHAN, lanes]
        at = step * 32 + 2 * i
        out[target[at]] = jnp.where(low, first, swap_halves(second))
        out[target[at + 1]] = jnp.where(low, swap_halves(first), second)
        return carry

    lax.fori_loop(0, 16, pair, 0, unroll=8)


def scatter_back(coeffs, gradient, source, table, slots, blocks):
    def clear(i, carry):
        table[i] = jnp.zeros((BLOCK, WIDTH), F32)
        return carry

    lax.fori_loop(0, blocks, clear, 0, unroll=16)

    def one(b, carry):
        parts = times(coeffs[b], gradient[rows_of(b), :], 0, 0)
        for k in range(slots):
            at = source[b, k]
            table[at] = table[at] + parts[k * BLOCK : (k + 1) * BLOCK]
        return carry

    lax.fori_loop(0, MESH_BLOCKS, one, 0, unroll=4)


def gather_mix(coeffs, pick, slots, b):
    picked = jnp.concatenate([pick(b, k) for k in range(slots)], axis=0)
    return times(coeffs[b], picked)


def add_returned(own, returned, shown, take):
    for h in range(SHOWN):
        at = shown[0, h]
        extra = (returned[0][h].astype(F32) + returned[1][h].astype(F32)) + (
            returned[2][h].astype(F32) + returned[3][h].astype(F32)
        )
        take[rows_of(at), :] = take[rows_of(at), :] + extra


def write_halo(table, own, halos):
    for i in range(MESH_BLOCKS):
        own[i * BLOCK : (i + 1) * BLOCK, :] = table[i].astype(own.dtype)
    for e in range(4):
        for h in range(SHOWN):
            halos[e][h] = table[MESH_BLOCKS + e * SHOWN + h].astype(BF16)


def early_back_body(source, cot, up, coeffs, own, h0, h1, h2, h3, table, lowered):
    def step(c, carry):
        rows = chunk(c, 256)
        lowered[rows, :] = times(cot[rows, :], up[...], 1, 1).astype(BF16)
        return carry

    lax.fori_loop(0, MESH_ROWS // 256, step, 0, unroll=4)
    scatter_back(coeffs, lowered, source, table, M_SLOTS, EXTENDED)
    write_halo(table, own, (h0, h1, h2, h3))


def encode_body(
    source, shown, packed, weight, coeffs, message, points, slope, table, mine, embedded, mesh
):
    step = pl.program_id(0)
    low = low_lanes(PACKED)

    def embed(c, carry):
        for p in range(4):
            a = packed[c * 8 + 2 * p]
            b = packed[c * 8 + 2 * p + 1]
            lanes = pl.ds(pl.multiple_of(c * 512 + p * 128, 128), 128)
            points[0:SPLIT, lanes] = jnp.where(low, a, swap_halves(b))[0:SPLIT]
            points[SPLIT:CHAN, lanes] = jnp.where(low, swap_halves(a), b)
        rows = chunk(c, 512)
        pre = times(points[:, rows], weight[...], 0, 0)
        s = sigmoid(pre)
        e = pre * s
        low_e = e.astype(BF16)
        table[rows, :] = low_e
        embedded[chunk(step * 4 + c, 512), :] = low_e
        slope[rows, :] = (s + e * (1.0 - s)).astype(BF16)
        return carry

    lax.fori_loop(0, 4, embed, 0, unroll=4)

    @pl.when(step == 3)
    def _():
        pick = lambda b, k: embedded[rows_of(source[b, k]), :]
        for h in range(SHOWN):
            row = gather_mix(coeffs, pick, G_SLOTS, shown[0, h])
            mesh[h * BLOCK : (h + 1) * BLOCK, :] = row.astype(BF16)
        pre = times(mesh[...], message[...])
        mine[...] = (pre * sigmoid(pre)).astype(BF16).reshape(SHOWN, BLOCK, WIDTH)


def mesh_body(source, embedded, coeffs, message, mesh, sent, slope_m):
    def mix(b, carry):
        pick = lambda b, k: embedded[rows_of(source[b, k]), :]
        mesh[rows_of(b), :] = gather_mix(coeffs, pick, G_SLOTS, b).astype(BF16)
        return carry

    lax.fori_loop(0, MESH_BLOCKS, mix, 0, unroll=8)

    def talk(c, carry):
        rows = chunk(c, 256)
        pre = times(mesh[rows, :], message[...])
        s = sigmoid(pre)
        e = pre * s
        sent[rows, :] = e.astype(BF16)
        slope_m[rows, :] = (s + e * (1.0 - s)).astype(BF16)
        return carry

    lax.fori_loop(0, MESH_ROWS // 256, talk, 0, unroll=4)


def extend(extended, sent, halos):
    extended[0:MESH_ROWS, :] = sent[...]
    for e in range(4):
        for h in range(SHOWN):
            at = MESH_ROWS + (e * SHOWN + h) * BLOCK
            extended[at : at + BLOCK, :] = halos[e][h]


def mix_mesh(coeffs, extended, source, aggregate):
    def mix(b, carry):
        pick = lambda b, k: extended[rows_of(source[b, k]), :]
        aggregate[rows_of(b), :] = gather_mix(coeffs, pick, M_SLOTS, b).astype(BF16)
        return carry

    lax.fori_loop(0, MESH_BLOCKS, mix, 0, unroll=8)


def forward_body(
    source, shown, sent, n0, n1, n2, n3, coeffs, mesh, up, message,
    aggregate, mesh_1, sent_1, slope_m, mine, extended,
):
    extend(extended, sent, (n0, n1, n2, n3))
    mix_mesh(coeffs, extended, source, aggregate)

    def step(c, carry):
        rows = chunk(c, 256)
        state = (mesh[rows, :].astype(F32) + times(aggregate[rows, :], up[...])).astype(BF16)
        mesh_1[rows, :] = state
        pre = times(state, message[...])
        s = sigmoid(pre)
        e = pre * s
        sent_1[rows, :] = e.astype(BF16)
        slope_m[rows, :] = (s + e * (1.0 - s)).astype(BF16)
        return carry

    lax.fori_loop(0, MESH_ROWS // 256, step, 0, unroll=4)
    for h in range(SHOWN):
        mine[h] = sent_1[rows_of(shown[0, h]), :]


def backward_body(
    source, shown, own, r0, r1, r2, r3, slope_m, cot, message, up, coeffs,
    grad_pre, grad_1, own_0, h0, h1, h2, h3, table, lowered, grad_msg,
):
    grad_msg[...] = own[...].astype(F32)
    add_returned(own, (r0, r1, r2, r3), shown, grad_msg)

    def step(c, carry):
        rows = chunk(c, 256)
        gp = (grad_msg[rows, :] * slope_m[rows, :].astype(F32)).astype(BF16)
        grad_pre[rows, :] = gp
        g = cot[rows, :].astype(F32) + times(gp, message[...], 1, 1)
        grad_1[rows, :] = g
        lowered[rows, :] = times(g.astype(BF16), up[...], 1, 1).astype(BF16)
        return carry

    lax.fori_loop(0, MESH_ROWS // 256, step, 0, unroll=4)
    scatter_back(coeffs, lowered, source, table, M_SLOTS, EXTENDED)
    write_halo(table, own_0, (h0, h1, h2, h3))


def write_slabs(odd, keep, give, first, values):
    def write(out, column):
        for c in range(2):
            at = first + c * values.shape[0]
            slab = values[:, column + c * 128 : column + (c + 1) * 128]
            out[at : at + values.shape[0], :] = slab.astype(BF16)

    @pl.when(odd[0] == 0)
    def _():
        write(keep, 0)
        write(give, COLUMNS)

    @pl.when(odd[0] == 1)
    def _():
        write(keep, COLUMNS)
        write(give, 0)


def grads_body(
    odd, source, sent, n0, n1, n2, n3, coeffs, mesh, up, cot, aggregate_0, grad_1, grad_pre,
    mesh_out, keep, give, extended, aggregate,
):
    write_slabs(odd, keep, give, 0, times(aggregate_0[...], grad_1[...].astype(BF16), 0, 0))
    write_slabs(odd, keep, give, SLABS, times(mesh[...], grad_pre[...], 0, 0))
    extend(extended, sent, (n0, n1, n2, n3))
    mix_mesh(coeffs, extended, source, aggregate)

    def step(c, carry):
        rows = chunk(c, 256)
        update = times(aggregate[rows, :], up[...])
        mesh_out[rows, :] = (mesh[rows, :].astype(F32) + update).astype(BF16)
        return carry

    lax.fori_loop(0, MESH_ROWS // 256, step, 0, unroll=4)
    write_slabs(odd, keep, give, 2 * SLABS, times(aggregate[...], cot[...], 0, 0))


def final_body(
    odd, source, shown, own, r0, r1, r2, r3, slope_m, grad_1, message, mesh, coeffs, slope, points,
    keep, give, table, grad_pre, lowered, grad_msg, total,
):
    c = pl.program_id(0)

    @pl.when(c == 0)
    def _():
        grad_msg[...] = own[...].astype(F32)
        add_returned(own, (r0, r1, r2, r3), shown, grad_msg)

        def step(c, carry):
            rows = chunk(c, 256)
            gp = (grad_msg[rows, :] * slope_m[rows, :].astype(F32)).astype(BF16)
            grad_pre[rows, :] = gp
            lowered[rows, :] = (grad_1[rows, :] + times(gp, message[...], 1, 1)).astype(BF16)
            return carry

        lax.fori_loop(0, MESH_ROWS // 256, step, 0, unroll=4)
        scatter_back(coeffs, lowered, source, table, G_SLOTS, GRID_BLOCKS)
        write_slabs(odd, keep, give, 0, times(mesh[...], grad_pre[...], 0, 0))
        total[...] = jnp.zeros_like(total)

    def grid_step(i, carry):
        rows = chunk(i, 512)
        grad = table[pl.ds(c * 32 + i * 8, 8)].reshape(512, WIDTH).astype(BF16)
        grad = (grad.astype(F32) * slope[rows, :].astype(F32)).astype(BF16)
        total[0:CHAN, :] = total[0:CHAN, :] + times(points[:, rows], grad)
        return carry

    lax.fori_loop(0, 4, grid_step, 0, unroll=4)

    @pl.when(c == 3)
    def _():
        write_slabs(odd, keep, give, SLABS, total[...])


def pair_body(early, early_other, late, late_other, out):
    def one(i, carry):
        out[i, 0:EARLY, :] = (early[i].astype(F32) + early_other[i].astype(F32)).astype(BF16)
        out[i, EARLY:PART, :] = (late[i].astype(F32) + late_other[i].astype(F32)).astype(BF16)
        return carry

    lax.fori_loop(0, CHIPS, one, 0, unroll=8)


def sum_body(parts, out):
    def add(i, carry):
        return carry + parts[i].astype(F32)

    total = lax.fori_loop(0, CHIPS, add, jnp.zeros((PART, 128), F32), unroll=8).astype(BF16)

    def one(i, carry):
        out[i] = total
        return carry

    lax.fori_loop(0, CHIPS, one, 0, unroll=8)


def unpack_body(odd, own, other, d_embed, ms_grad, up_grad):
    def place(values, outs, column, first):
        begin = 0
        for out, rows in outs:
            for c in range(2):
                low = max(first, begin)
                high = min(first + values.shape[0], begin + out.shape[0])
                if low < high:
                    at = column + c * 128
                    out[low - begin : high - begin, at : at + 128] = values[low - first : high - first]
                begin += rows

    def unpack(parts, column):
        early = ((up_grad.at[0], WIDTH), (ms_grad.at[1], WIDTH), (up_grad.at[1], WIDTH))
        late = ((ms_grad.at[0], WIDTH), (d_embed, TAIL))
        for q in range(CHIPS):
            values = parts[q].astype(F32)
            place(values[0:EARLY], early, column, q * EARLY)
            place(values[EARLY:PART], late, column, q * LATE)

    @pl.when(odd[0] == 0)
    def _():
        unpack(own, 0)
        unpack(other, COLUMNS)

    @pl.when(odd[0] == 1)
    def _():
        unpack(other, 0)
        unpack(own, COLUMNS)


def shift(value, axis, steps):
    axis = NARROW if axis == "narrow" else axis
    count = lax.axis_size(axis)
    return lax.ppermute(value, axis, [(i, (i + steps) % count) for i in range(count)])


def show(mine):
    return (shift(mine, "wide", 1), shift(mine, "wide", -1), shift(mine, "narrow", 1), shift(mine, "narrow", -1))


def give_back(h0, h1, h2, h3):
    return (shift(h0, "wide", -1), shift(h1, "wide", 1), shift(h2, "narrow", -1), shift(h3, "narrow", 1))


def swap_cores(value):
    return lax.ppermute(value, "core", [(0, 1), (1, 0)])


def exchange(parts, axes):
    return lax.all_to_all(parts, axes, split_axis=0, concat_axis=0, tiled=True)


def on_device(
    grid_feat, grid_send, w_embed, g2m_src, g2m_coef, mesh_src, mesh_coef, halo_send,
    message_weight, update_weight, cotangent,
):
    rows_bf16 = ((MESH_ROWS, WIDTH), BF16)
    rows_f32 = ((MESH_ROWS, WIDTH), F32)
    halo = ((SHOWN, BLOCK, WIDTH), BF16)
    mesh_scratch = pltpu.VMEM((MESH_ROWS, WIDTH), BF16)
    mesh_scratch32 = pltpu.VMEM((MESH_ROWS, WIDTH), F32)
    extended_scratch = pltpu.VMEM((EXTENDED * BLOCK, WIDTH), BF16)
    table_scratch = pltpu.VMEM((EXTENDED, BLOCK, WIDTH), F32)
    odd = lax.axis_index("core").reshape(1).astype(jnp.int32)
    w_m = (message_weight[0], message_weight[1])
    w_u = (update_weight[0], update_weight[1])

    packed = pl.pallas_call(
        pack_body,
        grid=(4,),
        out_shape=jax.ShapeDtypeStruct((GRID_BLOCKS, PACKED, 2 * BLOCK), BF16),
        in_specs=[SM, pl.BlockSpec((CHAN, GRID_ROWS // 4), lambda i: (0, i))],
        out_specs=pl.BlockSpec((GRID_BLOCKS, PACKED, 2 * BLOCK), lambda i: (0, 0, 0)),
        scratch_shapes=[pltpu.SMEM((GRID_BLOCKS,), jnp.int32)],
        compiler_params=pltpu.CompilerParams(vmem_limit_bytes=56 * MIB),
        cost_estimate=pl.CostEstimate(flops=0, bytes_accessed=8 * MIB, transcendentals=0),
    )(grid_send, grid_feat.T)
    packed, cotangent, odd = lax.optimization_barrier((packed, cotangent, odd))
    received = exchange(packed, AXES)

    g_mix = g2m_coef.transpose(0, 2, 1, 3).reshape(MESH_BLOCKS, BLOCK, G_SLOTS * BLOCK)
    m_mix = mesh_coef.transpose(0, 2, 1, 3).reshape(MESH_BLOCKS, BLOCK, M_SLOTS * BLOCK)

    own_1, *halos = kernel_call(
        early_back_body, [rows_f32] + [halo] * 4, [SM] + [VM] * 3, [table_scratch, mesh_scratch],
        flops=2 * 10**9, moved=8 * MIB, limit=20,
    )(mesh_src, cotangent, w_u[1], m_mix)
    returned_1 = give_back(*halos)

    received, g_mix, m_mix, own_1 = lax.optimization_barrier((received, g_mix, m_mix, own_1))
    whole = lambda *shape: pl.BlockSpec(shape, lambda i: (0,) * len(shape))
    points, slope, embedded, mine_0 = pl.pallas_call(
        encode_body,
        grid=(4,),
        out_shape=[
            pltpu.HBM((CHAN, GRID_ROWS), BF16),
            pltpu.HBM((GRID_ROWS, WIDTH), BF16),
            jax.ShapeDtypeStruct((GRID_ROWS, WIDTH), BF16),
            jax.ShapeDtypeStruct((SHOWN, BLOCK, WIDTH), BF16),
        ],
        in_specs=[
            SM, SM,
            pl.BlockSpec((32, PACKED, 2 * BLOCK), lambda i: (i, 0, 0)),
            VM, VM, VM,
        ],
        out_specs=[
            pl.BlockSpec((CHAN, 2048), lambda i: (0, i)),
            pl.BlockSpec((2048, WIDTH), lambda i: (i, 0)),
            pl.BlockSpec((2048, WIDTH), lambda i: (i, 0)),
            whole(SHOWN, BLOCK, WIDTH),
        ],
        scratch_shapes=[
            pltpu.VMEM((GRID_ROWS, WIDTH), BF16), pltpu.VMEM((SHOWN * BLOCK, WIDTH), BF16)
        ],
        compiler_params=pltpu.CompilerParams(vmem_limit_bytes=28 * MIB),
        cost_estimate=pl.CostEstimate(flops=4 * 10**9, bytes_accessed=26 * MIB, transcendentals=0),
    )(g2m_src, halo_send, received, w_embed, g_mix, w_m[0])
    mine_0, *returned_1 = lax.optimization_barrier((mine_0, *returned_1))
    shown_0 = show(mine_0)
    mesh_0, sent_0, slope_0 = kernel_call(
        mesh_body, [rows_bf16] * 3, [SM] + [VM] * 3, flops=2 * 10**9, moved=12 * MIB, limit=24,
    )(g2m_src, embedded, g_mix, w_m[0])

    aggregate_0, mesh_1, sent_1, slope_1, mine_1 = kernel_call(
        forward_body, [rows_bf16] * 4 + [halo], [SM, SM] + [VM] * 9, [extended_scratch],
        flops=2 * 10**9, moved=10 * MIB, limit=20,
    )(mesh_src, halo_send, sent_0, *shown_0, m_mix, mesh_0, w_u[0], w_m[1])
    shown_1 = show(mine_1)

    grad_pre_1, grad_1, own_0, *halos = kernel_call(
        backward_body, [rows_bf16, rows_f32, rows_f32] + [halo] * 4, [SM, SM] + [VM] * 10,
        [table_scratch, mesh_scratch, mesh_scratch32], flops=2 * 10**9, moved=16 * MIB, limit=28,
    )(mesh_src, halo_send, own_1, *returned_1, slope_1, cotangent, w_m[1], w_u[0], m_mix)
    returned_0 = give_back(*halos)

    mesh_out, early, early_give = kernel_call(
        grads_body, [rows_bf16, ((3 * SLABS, 128), BF16), ((3 * SLABS, 128), BF16)],
        [SM, SM] + [VM] * 12, [extended_scratch, mesh_scratch], flops=4 * 10**9, moved=14 * MIB,
        limit=24,
    )(
        odd, mesh_src, sent_1, *shown_1, m_mix, mesh_1, w_u[1], cotangent, aggregate_0, grad_1,
        grad_pre_1,
    )
    early_other = swap_cores(early_give)

    late, late_give = pl.pallas_call(
        final_body,
        grid=(4,),
        out_shape=[jax.ShapeDtypeStruct((SLABS + 2 * TAIL, 128), BF16)] * 2,
        in_specs=[
            SM, SM, SM, *[VM] * 10,
            pl.BlockSpec((2048, WIDTH), lambda i: (i, 0)),
            pl.BlockSpec((CHAN, 2048), lambda i: (0, i)),
        ],
        out_specs=[VM, VM],
        scratch_shapes=[
            pltpu.VMEM((GRID_BLOCKS, BLOCK, WIDTH), F32),
            mesh_scratch, mesh_scratch, mesh_scratch32,
            pltpu.VMEM((TAIL, WIDTH), F32),
        ],
        compiler_params=pltpu.CompilerParams(vmem_limit_bytes=34 * MIB),
        cost_estimate=pl.CostEstimate(flops=4 * 10**9, bytes_accessed=24 * MIB, transcendentals=0),
    )(
        odd, g2m_src, halo_send, own_0, *returned_0, slope_0, grad_1, w_m[0], mesh_0, g_mix, slope,
        points,
    )
    late_other = swap_cores(late_give)

    by_chip = lambda part: part.reshape(CHIPS, -1, 128)
    pairs = kernel_call(
        pair_body, [((CHIPS, PART, 128), BF16)], [VM] * 4, moved=6 * MIB, limit=16
    )(by_chip(early), by_chip(early_other), by_chip(late), by_chip(late_other))[0]
    totals = kernel_call(
        sum_body, [((CHIPS, PART, 128), BF16)], [VM], moved=3 * MIB, limit=16
    )(exchange(pairs, CHIP_AXES))[0]
    own = exchange(totals, CHIP_AXES)
    d_embed, ms_grad, up_grad = kernel_call(
        unpack_body,
        [((CHAN, WIDTH), F32), ((2, WIDTH, WIDTH), F32), ((2, WIDTH, WIDTH), F32)],
        [SM, VM, VM], moved=7 * MIB, limit=24,
    )(odd, own, swap_cores(own))
    return mesh_out, d_embed, ms_grad, up_grad


def solution(mesh):
    by_core = Mesh(mesh.devices.reshape(16, 4, 2), AXES)
    split = P(AXES, None)
    return jax.shard_map(
        on_device,
        mesh=by_core,
        in_specs=(
            split, split, P(), split, P(AXES, None, None, None), split, P(AXES, None, None, None),
            split, P(), P(), split,
        ),
        out_specs=(split, P(), P(), P()),
        check_vma=False,
    )
```
